32 devices in a mesh: seq: 4 (over y, x), rows: 8 (over z, core).
Axes of the slice: x: 2, y: 2, z: 4, core: 2. Of those that a mesh axis runs over, the one named last changes fastest.
Arguments:
- enc_input: bfloat16 [32, 512, 512], P('rows', 'seq'), may hold values from -6 to 6
- dec_input: bfloat16 [32, 512, 512], P('rows', 'seq'), may hold values from -6 to 6
- src_lengths: int32 [32, 14], P('rows'), may hold values from 0 to 448, as said below
- tgt_lengths: int32 [32, 14], P('rows'), may hold values from 0 to 448, as said below
- masked: int32 [32, 512], P('rows', 'seq'), may hold values 0 or 1
- cotangent: bfloat16 [32, 512, 512], P('rows', 'seq'), may hold values from -6 to 6
- self_qkv: bfloat16 [2, 512, 1536], replicated, may hold values from -0.375 to 0.375
- attn_out: bfloat16 [3, 512, 512], replicated, may hold values from -0.75 to 0.75
- cross_q: bfloat16 [512, 512], replicated, may hold values from -0.375 to 0.375
- cross_kv: bfloat16 [512, 1024], replicated, may hold values from -0.375 to 0.375
- ffn_up: bfloat16 [2, 512, 2048], replicated, may hold values from -0.25 to 0.25
- ffn_down: bfloat16 [2, 2048, 512], replicated, may hold values from -0.125 to 0.125
- norm_gain: float32 [5, 512], replicated, may hold values from 0.25 to 1.75
- biases: float32 [16, 512], replicated, may hold values from -1.5 to 1.5
- up_bias: float32 [2, 2048], replicated, may hold values from -1.5 to 1.5
- mask_embed: float32 [512], replicated, may hold values from -3 to 3
Outputs:
- dec_output: bfloat16 [32, 512, 512], P('rows', 'seq')
- enc_input_grad: float32 [32, 512, 512], P('rows', 'seq')
- dec_input_grad: float32 [32, 512, 512], P('rows', 'seq')
- self_qkv_grad: float32 [2, 512, 1536], P(None, 'seq')
- attn_out_grad: float32 [3, 512, 512], P(None, 'seq')
- cross_q_grad: float32 [512, 512], P('seq')
- cross_kv_grad: float32 [512, 1024], P('seq')
- ffn_up_grad: float32 [2, 512, 2048], P(None, 'seq')
- ffn_down_grad: float32 [2, 2048, 512], P(None, 'seq')
- norm_gain_grad: float32 [5, 512], P(None, 'seq')
- biases_grad: float32 [16, 512], P(None, 'seq')
- up_bias_grad: float32 [2, 2048], P(None, 'seq')
- mask_embed_grad: float32 [512], P('seq')
The draws below stay inside these ranges and needn't reach their ends.
Inputs may be any that keep to these rules, and one draw needn't show every extreme that they name: `src_lengths`: documents are packed one after another from position 0 of each packed row. In each aligned block of 4 rows exactly one row, at a place drawn per block, begins with a document of 448 tokens and holds no other document; every other row begins with a document of 32 tokens followed by 6 pairs. The two documents of a pair fill 2 * 32 positions together, the first 16 to 48 tokens long but never 32. Entries after a row's documents are 0. `tgt_lengths`: packed as src_lengths, with the same rows holding the long document and the same count of pairs in each row; target document j of a row belongs to source document j of that row; how a pair's positions split between its two documents is drawn apart from the source's.
All inputs are finite; a program needn't handle non-finite values. No bound on the sum of `masked` on one device may be relied on, other than what follows from the above.
Results may differ from the reference program's by a relative error of at most 0.035.
Values may be sent and summed in bfloat16 or wider, within the bound.
No kernel may reach another device: no remote copies, remote signals or barrier semaphores. Data moves between devices by JAX's collectives and lax.ppermute only.
A program may use at most 384 MiB of HBM per device.

```python
import jax
import jax.numpy as jnp
from jax import lax

D = 512
HEADS = 8
HEAD_DIM = 64
FF = 2048
SEQ_DEV = 128
ROWS_DEV = 4
SHORT = 32
ROW = 512
NSEG = 14
ROWS_ALL = 32


def long_rows(key):
    choice_of_block = jax.random.randint(key, (ROWS_ALL // ROWS_DEV,), 0, ROWS_DEV)
    row_numbers = jnp.arange(ROWS_ALL, dtype=jnp.int32)
    return row_numbers % ROWS_DEV == choice_of_block[row_numbers // ROWS_DEV]


def packed_lengths(key, chosen):
    drawn = jax.random.randint(key, (ROWS_ALL, NSEG // 2), SHORT // 2, SHORT + SHORT // 2)
    firsts = (drawn + (drawn >= SHORT).astype(jnp.int32)).astype(jnp.int32)
    pairs = jnp.stack([firsts, 2 * SHORT - firsts], axis=2).reshape(ROWS_ALL, NSEG)
    shifted = jnp.concatenate([jnp.zeros((ROWS_ALL, 1), jnp.int32), pairs[:, :-1]], axis=1)
    slots = jnp.arange(NSEG, dtype=jnp.int32)[None, :]
    long_pairs = (SEQ_DEV - 4 * SHORT) // (2 * SHORT)
    long_layout = jnp.where(slots == 0, ROW - SEQ_DEV + 2 * SHORT, jnp.where(slots <= 2 * long_pairs, shifted, 0))
    drawn_layout = jnp.where(slots == 0, SHORT, jnp.where(slots <= NSEG - 2, shifted, 0))
    return jnp.where(chosen[:, None], long_layout, drawn_layout).astype(jnp.int32)


def draw_src_lengths(key, part):
    chosen = long_rows(key)
    key = jax.random.fold_in(key, 11)
    return packed_lengths(key, chosen)


def draw_tgt_lengths(key, part):
    chosen = long_rows(key)
    key = jax.random.fold_in(key, 23)
    return packed_lengths(key, chosen)


def touch_ends(array, stream_key, low, top_value):
    spot = [jax.random.randint(jax.random.fold_in(stream_key, axis), (), 0, length) for axis, length in enumerate(array.shape)]
    main_axis = array.shape.index(max(array.shape))
    beside = spot[:main_axis] + [(spot[main_axis] + 1) % array.shape[main_axis]] + spot[main_axis + 1:]
    return array.at[tuple(spot)].set(low).at[tuple(beside)].set(top_value)


def block_scale(key, shape, shards, low, largest):
    loudness, own = 1.0, jax.random.fold_in(key, 6)
    for position, blocks in shards:
        heights = jnp.exp(jax.random.uniform(jax.random.fold_in(own, position), (blocks,), jnp.float32, low / len(shards), largest / len(shards)))
        loudness = loudness * jnp.repeat(heights, shape[position] // blocks).reshape([-1 if axis == position else 1 for axis in range(len(shape))])
    return loudness


def gaussian(key, shape, scale, limit, cuts=(), held_as=jnp.bfloat16):
    gain = block_scale(key, shape, cuts, -0.22, 0.18) if cuts else 1.0
    values = jax.random.normal(key, shape, jnp.float32) * scale * gain
    return jnp.minimum(jnp.maximum(values, -limit), limit).astype(held_as)


def setup_inputs(seed: int = 0) -> dict:
    key_of = jax.random.split(jax.random.key(seed), 17)
    enc_input = gaussian(key_of[0], (ROWS_ALL, ROW, D), 1.0, 6.0, ((0, 8), (1, 4)))
    dec_input = gaussian(key_of[1], (ROWS_ALL, ROW, D), 1.0, 6.0, ((0, 8), (1, 4)))
    src_lengths = draw_src_lengths(jax.random.fold_in(key_of[16], 71), 0)
    tgt_lengths = draw_tgt_lengths(jax.random.fold_in(key_of[16], 71), 0)
    masked = touch_ends((jax.random.randint(key_of[4], (ROWS_ALL, ROW), 0, 2) < 1).astype(jnp.int32), jax.random.fold_in(key_of[4], 1), 0, 1)
    cotangent = gaussian(key_of[5], (ROWS_ALL, ROW, D), 1.0, 6.0, ((0, 8), (1, 4)))
    self_qkv = gaussian(key_of[6], (2, D, 3 * D), (D // 2) ** -0.5, 0.375)
    attn_out = gaussian(key_of[7], (3, D, D), (D // 8) ** -0.5, 0.75)
    cross_q = gaussian(key_of[8], (D, D), (D // 2) ** -0.5, 0.375)
    cross_kv = gaussian(key_of[9], (D, 2 * D), (D // 2) ** -0.5, 0.375)
    ffn_up = gaussian(key_of[10], (2, D, FF), D ** -0.5, 0.25)
    ffn_down = gaussian(key_of[11], (2, FF, D), FF ** -0.5, 0.125)
    norm_gain = jnp.clip(1.0 + 0.15 * jax.random.normal(key_of[12], (5, D), jnp.float32), 0.25, 1.75)
    biases = gaussian(key_of[13], (16, D), 0.3, 1.5, (), jnp.float32)
    up_bias = gaussian(key_of[14], (2, FF), 0.3, 1.5, (), jnp.float32)
    mask_embed = gaussian(key_of[15], (D,), 0.5, 3.0, (), jnp.float32)
    return {"enc_input": enc_input, "dec_input": dec_input, "src_lengths": src_lengths, "tgt_lengths": tgt_lengths, "masked": masked, "cotangent": cotangent, "self_qkv": self_qkv, "attn_out": attn_out, "cross_q": cross_q, "cross_kv": cross_kv, "ffn_up": ffn_up, "ffn_down": ffn_down, "norm_gain": norm_gain, "biases": biases, "up_bias": up_bias, "mask_embed": mask_embed}


@jax.custom_vjp
def low(v):
    return lax.optimization_barrier(v.astype(jnp.bfloat16)).astype(jnp.float32)

@jax.custom_vjp
def low_back(v):
    return v

def low_keep(v):
    return (low(v), None)

def low_pass(kept, grad):
    return (grad,)

def back_keep(v):
    return (v, None)

def back_low(kept, grad):
    return (low(grad),)
low.defvjp(low_keep, low_pass)
low_back.defvjp(back_keep, back_low)
HIGHEST = lax.Precision.HIGHEST
NEG_FILL = -1000000000.0
EPSILON = 1e-05

def matmul(left_side, right_side):
    return jnp.dot(left_side, right_side, precision=HIGHEST, preferred_element_type=jnp.float32)

def normalize(residual, scale_gain, offset):
    centred = residual - lax.optimization_barrier(jnp.mean(residual, axis=-1, keepdims=True))
    spread = lax.optimization_barrier(jnp.mean(centred * centred, axis=-1, keepdims=True))
    return centred * lax.rsqrt(spread + EPSILON) * scale_gain + offset

def segments(lengths, places):
    doc_ends = jnp.cumsum(lengths).astype(jnp.int32)
    return lax.optimization_barrier(jnp.sum((doc_ends[None, :] <= places[:, None]).astype(jnp.int32), axis=1)).astype(jnp.int32)

def attention(queries, keys, values, query_seg, key_seg):
    block_count = queries.shape[0] // SEQ_DEV
    key_heads = keys.reshape(-1, HEADS, HEAD_DIM)
    value_heads = values.reshape(-1, HEADS, HEAD_DIM)

    def one_block(block_pair):
        query_block, seg_block = block_pair
        query_heads = query_block.reshape(SEQ_DEV, HEADS, HEAD_DIM)
        scores = jnp.einsum('qhd,khd->hqk', query_heads, key_heads, precision=HIGHEST)
        scores = low_back(scores * HEAD_DIM ** (-0.5))
        allowed = (seg_block[:, None] == key_seg[None, :])[None]
        scores = jnp.where(allowed, scores, NEG_FILL)
        row_peak = lax.optimization_barrier(jnp.max(scores, axis=-1, keepdims=True))
        exp_scores = jnp.exp(scores - row_peak)
        row_total = lax.optimization_barrier(jnp.sum(exp_scores, axis=-1))
        context = jnp.einsum('hqk,khd->qhd', low(exp_scores), value_heads, precision=HIGHEST)
        context = context / jnp.transpose(row_total)[:, :, None]
        return context.reshape(SEQ_DEV, HEADS * HEAD_DIM)
    blocks = lax.map(jax.checkpoint(one_block), (queries.reshape(block_count, SEQ_DEV, -1), query_seg.reshape(block_count, SEQ_DEV)))
    return blocks.reshape(queries.shape[0], -1)

def self_attention(inputs, w_qkv, bias_q, bias_v, w_out, bias_out, segment):
    projected = low_back(matmul(inputs, w_qkv))
    queries = low(projected[:, :D] + bias_q)
    keys = low(projected[:, D:2 * D])
    values = low(projected[:, 2 * D:] + bias_v)
    context = low_back(low(attention(queries, keys, values, segment, segment)))
    return low_back(matmul(context, w_out)) + bias_out

def feed_forward(hidden, w_up, bias_up, w_down, bias_down):
    pre_act = low_back(matmul(low(hidden), w_up)) + bias_up
    activated = low(jax.nn.gelu(pre_act, approximate=False))
    return low_back(matmul(activated, w_down)) + bias_down

def forward_row(params, row_arrays):
    self_qkv, attn_out, cross_q, cross_kv, ffn_up, ffn_down, norm_gain, biases, up_bias, mask_embed = params
    enc_row, dec_row, mask_row, src_row, tgt_row = row_arrays
    places = jnp.arange(ROW, dtype=jnp.int32)
    src_seg = segments(src_row, places)
    tgt_seg = segments(tgt_row, places)
    enc_hidden = normalize(enc_row + self_attention(enc_row, self_qkv[0], biases[0], biases[1], attn_out[0], biases[2], src_seg), norm_gain[0], biases[11])
    memory = normalize(enc_hidden + feed_forward(enc_hidden, ffn_up[0], up_bias[0], ffn_down[0], biases[3]), norm_gain[1], biases[12])
    dec_inputs = dec_row + mask_row[:, None].astype(jnp.float32) * mask_embed
    dec_hidden = normalize(dec_inputs + self_attention(low(dec_inputs), self_qkv[1], biases[4], biases[5], attn_out[1], biases[6], tgt_seg), norm_gain[2], biases[13])
    cross_proj = low_back(matmul(low(dec_hidden), cross_q))
    cross_queries = low(cross_proj + biases[7])
    pair_proj = low_back(matmul(low(memory), cross_kv))
    cross_keys = low(pair_proj[:, :D])
    cross_values = low(pair_proj[:, D:] + biases[8])
    context = low_back(low(attention(cross_queries, cross_keys, cross_values, tgt_seg, src_seg)))
    cross_hidden = normalize(dec_hidden + low_back(matmul(context, attn_out[2])) + biases[9], norm_gain[3], biases[14])
    return normalize(cross_hidden + feed_forward(cross_hidden, ffn_up[1], up_bias[1], ffn_down[1], biases[10]), norm_gain[4], biases[15])

def reference(enc_input, dec_input, src_lengths, tgt_lengths, masked, cotangent, self_qkv, attn_out, cross_q, cross_kv, ffn_up, ffn_down, norm_gain, biases, up_bias, mask_embed):
    weights = (self_qkv.astype(jnp.float32), attn_out.astype(jnp.float32), cross_q.astype(jnp.float32), cross_kv.astype(jnp.float32), ffn_up.astype(jnp.float32), ffn_down.astype(jnp.float32), norm_gain.astype(jnp.float32), biases.astype(jnp.float32), up_bias.astype(jnp.float32), mask_embed.astype(jnp.float32))

    def forward(enc_all, dec_all, params):

        def one_row(row_arrays):
            return forward_row(params, row_arrays)
        return lax.map(one_row, (enc_all, dec_all, masked, src_lengths, tgt_lengths))
    final, pullback = jax.vjp(forward, enc_input.astype(jnp.float32), dec_input.astype(jnp.float32), weights)
    enc_grad, dec_grad, weight_grads = pullback(cotangent.astype(jnp.float32))
    return (final.astype(jnp.bfloat16), enc_grad, dec_grad, weight_grads[0], weight_grads[1], weight_grads[2], weight_grads[3], weight_grads[4], weight_grads[5], weight_grads[6], weight_grads[7], weight_grads[8], weight_grads[9])
```

```python
import functools
import types
import typing

import jax
import jax.numpy as jnp
from jax import lax
from jax.experimental import pallas as pl
from jax.experimental.pallas import tpu as pltpu
from jax.sharding import PartitionSpec as P

D = 512
HEADS = 8
HEAD_DIM = 64


EPSILON = 1e-05
NEG_FILL = -1000000000.0
START_FILL = -1e30


def normalize(residual, scale_gain, offset):
    centred = residual - jnp.mean(residual, axis=-1, keepdims=True)
    spread = jnp.mean(centred * centred, axis=-1, keepdims=True)
    return centred * lax.rsqrt(spread + EPSILON) * scale_gain + offset


def gelu_exact(values):
    return jax.nn.gelu(values, approximate=False)


def segments(lengths, places):
    doc_ends = jnp.cumsum(lengths, axis=1)
    return jnp.sum((doc_ends[:, None, :] <= places[None, :, None]).astype(jnp.int32), axis=2)


def project(inputs, weight):
    return jnp.einsum("rsd,df->rsf", inputs, weight, preferred_element_type=jnp.float32)


def project_back(gradient, weight):
    return jnp.einsum("rsf,df->rsd", gradient, weight, preferred_element_type=jnp.float32)


def weight_grad(inputs, gradient):
    return jnp.einsum("rsd,rsf->df", inputs, gradient, preferred_element_type=jnp.float32)


def token_sum(gradient):
    return jnp.sum(gradient, axis=(0, 1))


def split_heads(tensor):
    return tensor.reshape(tensor.shape[:2] + (HEADS, HEAD_DIM))


def split_blocks(tensor, block_size):
    new_shape = (tensor.shape[0], tensor.shape[1] // block_size, block_size) + tensor.shape[2:]
    return jnp.swapaxes(tensor.reshape(new_shape), 0, 1)


def block_scores(query_heads, key_heads, query_seg, key_seg):
    scores = jnp.einsum(
        "rqhd,rkhd->rhqk", query_heads, key_heads, preferred_element_type=jnp.float32
    ) * HEAD_DIM ** (-0.5)
    allowed = query_seg[:, None, :, None] == key_seg[:, None, None, :]
    return jnp.where(allowed, scores, NEG_FILL)


def block_grads(
    query_heads, grad_heads, log_total, delta_rows, query_seg, key_heads, value_heads, key_seg
):
    scores = block_scores(query_heads, key_heads, query_seg, key_seg)
    probs = jnp.exp(scores - log_total[..., None])
    dprobs = jnp.einsum(
        "rqhd,rkhd->rhqk", grad_heads, value_heads, preferred_element_type=jnp.float32
    )
    dscores = (probs * (dprobs - delta_rows[..., None])).astype(jnp.bfloat16)
    scaling = HEAD_DIM ** (-0.5)
    query_part = (
        jnp.einsum("rhqk,rkhd->rqhd", dscores, key_heads, preferred_element_type=jnp.float32)
        * scaling
    )
    key_part = (
        jnp.einsum("rhqk,rqhd->rkhd", dscores, query_heads, preferred_element_type=jnp.float32)
        * scaling
    )
    value_part = jnp.einsum(
        "rhqk,rqhd->rkhd",
        probs.astype(jnp.bfloat16),
        grad_heads,
        preferred_element_type=jnp.float32,
    )
    return (query_part, key_part, value_part)


def start_state(row_count, length):
    return (
        jnp.full((row_count, HEADS, length), START_FILL, jnp.float32),
        jnp.zeros((row_count, HEADS, length), jnp.float32),
        jnp.zeros((row_count, length, HEADS, HEAD_DIM), jnp.float32),
    )


def finish_state(state):
    running_max, running_sum, running_acc = state
    context = running_acc / jnp.swapaxes(running_sum, 1, 2)[..., None]
    return (
        context.reshape(context.shape[:2] + (HEADS * HEAD_DIM,)),
        running_max + jnp.log(running_sum),
    )


def absorber(query_heads, query_seg, key_lengths, length):

    def absorb(carried, piece_pair, first_pos):
        key_piece, value_piece = piece_pair
        piece_len = key_piece.shape[1]
        seg_piece = segments(key_lengths, jnp.arange(piece_len, dtype=jnp.int32))

        def advance(running, inputs):
            running_max, running_sum, running_acc = running
            key_block, value_block, seg_block = inputs
            scores = block_scores(query_heads, key_block, query_seg, seg_block)
            new_max = jnp.maximum(running_max, jnp.max(scores, axis=-1))
            factor = jnp.exp(running_max - new_max)
            exp_scores = jnp.exp(scores - new_max[..., None])
            running_sum = running_sum * factor + jnp.sum(exp_scores, axis=-1)
            running_acc = running_acc * jnp.swapaxes(factor, 1, 2)[..., None] + jnp.einsum(
                "rhqk,rkhd->rqhd",
                exp_scores.astype(jnp.bfloat16),
                value_block,
                preferred_element_type=jnp.float32,
            )
            return ((new_max, running_sum, running_acc), None)

        blocks = (
            split_blocks(split_heads(key_piece), length),
            split_blocks(split_heads(value_piece), length),
            split_blocks(seg_piece, length),
        )
        result, unused = lax.scan(advance, carried, blocks)
        return result

    return absorb


def attend_forward(queries, keys, values, query_seg, key_lengths):
    row_count, length = (queries.shape[0], queries.shape[1])
    query_heads = split_heads(queries)
    absorb = absorber(query_heads, query_seg, key_lengths, length)
    state = absorb(
        start_state(row_count, length),
        (
            lax.all_gather(keys, "seq", axis=1, tiled=True),
            lax.all_gather(values, "seq", axis=1, tiled=True),
        ),
        jnp.int32(0),
    )
    context, log_total = finish_state(state)
    return (context, log_total, None)


def attend_backward(
    queries,
    keys,
    values,
    query_seg,
    key_seg,
    query_lengths,
    key_lengths,
    context,
    log_total,
    context_grad,
):
    row_count, length = (queries.shape[0], queries.shape[1])
    grad_low = context_grad.astype(jnp.bfloat16)
    query_heads = split_heads(queries)
    grad_heads = split_heads(grad_low)
    delta_rows = jnp.swapaxes(
        jnp.sum(grad_heads.astype(jnp.float32) * split_heads(context), axis=-1), 1, 2
    )
    zero_heads = jnp.zeros((row_count, length, HEADS, HEAD_DIM), jnp.float32)
    key_piece = lax.all_gather(keys, "seq", axis=1, tiled=True)
    value_piece = lax.all_gather(values, "seq", axis=1, tiled=True)
    piece_len = key_piece.shape[1]
    block_size = length
    seg_piece = segments(key_lengths, jnp.arange(piece_len, dtype=jnp.int32))

    def advance(running, inputs):
        key_block, value_block, seg_block = inputs
        query_part, unused_keys, unused_values = block_grads(
            query_heads,
            grad_heads,
            log_total,
            delta_rows,
            query_seg,
            key_block,
            value_block,
            seg_block,
        )
        return (running + query_part, None)

    blocks = (
        split_blocks(split_heads(key_piece), block_size),
        split_blocks(split_heads(value_piece), block_size),
        split_blocks(seg_piece, block_size),
    )
    result, unused = lax.scan(advance, zero_heads, blocks)
    query_grad = result
    total_all, delta_all = (
        lax.all_gather(log_total, "seq", axis=2, tiled=True),
        lax.all_gather(delta_rows, "seq", axis=2, tiled=True),
    )
    key_heads = split_heads(keys)
    value_heads = split_heads(values)
    query_piece = lax.all_gather(queries, "seq", axis=1, tiled=True)
    grad_piece = lax.all_gather(grad_low, "seq", axis=1, tiled=True)
    piece_len = query_piece.shape[1]
    block_size = length
    seg_piece = segments(query_lengths, jnp.arange(piece_len, dtype=jnp.int32))
    offsets = jnp.arange(piece_len // block_size, dtype=jnp.int32) * block_size

    def advance(running, inputs):
        query_block, grad_block, seg_block, offset = inputs
        total_block = lax.dynamic_slice_in_dim(total_all, offset, block_size, 2)
        delta_block = lax.dynamic_slice_in_dim(delta_all, offset, block_size, 2)
        unused_query, key_part, value_part = block_grads(
            query_block,
            grad_block,
            total_block,
            delta_block,
            seg_block,
            key_heads,
            value_heads,
            key_seg,
        )
        return ((running[0] + key_part, running[1] + value_part), None)

    blocks = (
        split_blocks(split_heads(query_piece), block_size),
        split_blocks(split_heads(grad_piece), block_size),
        split_blocks(seg_piece, block_size),
        offsets,
    )
    result, unused = lax.scan(advance, (zero_heads, zero_heads), blocks)
    key_grad, value_grad = result
    return (
        query_grad.reshape(queries.shape),
        key_grad.reshape(queries.shape),
        value_grad.reshape(queries.shape),
    )


def self_forward(inputs_low, w_qkv, bias_q, bias_v, segment, lengths):
    projected = project(inputs_low, w_qkv)
    queries = (projected[..., :D] + bias_q).astype(jnp.bfloat16)
    keys = projected[..., D : 2 * D].astype(jnp.bfloat16)
    values = (projected[..., 2 * D :] + bias_v).astype(jnp.bfloat16)
    context, log_total, stored = attend_forward(queries, keys, values, segment, lengths)
    return (queries, keys, values, context, log_total, stored)


def ffn_forward(hidden, w_up, bias_up, w_down, bias_down):
    hidden_low = hidden.astype(jnp.bfloat16)
    pre_act = project(hidden_low, w_up) + bias_up
    activated, act_back = jax.vjp(gelu_exact, pre_act)
    act_low = activated.astype(jnp.bfloat16)
    return (project(act_low, w_down) + bias_down, (hidden_low, act_low, act_back))


def ffn_backward(out_grad, stored, w_up, w_down):
    hidden_low, act_low, act_back = stored
    out_low = out_grad.astype(jnp.bfloat16)
    down_grad = weight_grad(act_low, out_low)
    (pre_grad,) = act_back(project_back(out_low, w_down))
    pre_low = pre_grad.astype(jnp.bfloat16)
    up_grad = weight_grad(hidden_low, pre_low)
    return (
        project_back(pre_low, w_up),
        up_grad,
        token_sum(pre_grad),
        down_grad,
        token_sum(out_grad),
    )


def local(
    enc_input,
    dec_input,
    src_lengths,
    tgt_lengths,
    masked,
    cotangent,
    self_qkv,
    attn_out,
    cross_q,
    cross_kv,
    ffn_up,
    ffn_down,
    norm_gain,
    biases,
    up_bias,
    mask_embed,
):
    length = enc_input.shape[1]
    places = lax.axis_index("seq") * length + jnp.arange(length, dtype=jnp.int32)
    src_seg = segments(src_lengths, places)
    tgt_seg = segments(tgt_lengths, places)
    mask_float = masked.astype(jnp.float32)[..., None]
    enc_queries, enc_keys, enc_values, enc_context, enc_total, enc_stored = self_forward(
        enc_input, self_qkv[0], biases[0], biases[1], src_seg, src_lengths
    )
    enc_ctx_low = enc_context.astype(jnp.bfloat16)
    enc_resid = enc_input.astype(jnp.float32) + project(enc_ctx_low, attn_out[0]) + biases[2]
    enc_hidden, enc_norm_back = jax.vjp(normalize, enc_resid, norm_gain[0], biases[11])
    enc_ffn, enc_kept = ffn_forward(enc_hidden, ffn_up[0], up_bias[0], ffn_down[0], biases[3])
    memory, memory_back = jax.vjp(normalize, enc_hidden + enc_ffn, norm_gain[1], biases[12])
    memory_low = memory.astype(jnp.bfloat16)
    dec_inputs = dec_input.astype(jnp.float32) + mask_float * mask_embed
    dec_low = dec_inputs.astype(jnp.bfloat16)
    dec_queries, dec_keys, dec_values, dec_context, dec_total, dec_stored = self_forward(
        dec_low, self_qkv[1], biases[4], biases[5], tgt_seg, tgt_lengths
    )
    dec_ctx_low = dec_context.astype(jnp.bfloat16)
    dec_hidden, dec_norm_back = jax.vjp(
        normalize,
        dec_inputs + project(dec_ctx_low, attn_out[1]) + biases[6],
        norm_gain[2],
        biases[13],
    )
    dec_hidden_low = dec_hidden.astype(jnp.bfloat16)
    cross_queries = (project(dec_hidden_low, cross_q) + biases[7]).astype(jnp.bfloat16)
    cross_pair = project(memory_low, cross_kv)
    cross_keys = cross_pair[..., :D].astype(jnp.bfloat16)
    cross_values = (cross_pair[..., D:] + biases[8]).astype(jnp.bfloat16)
    cross_context, cross_total, cross_stored = attend_forward(
        cross_queries, cross_keys, cross_values, tgt_seg, src_lengths
    )
    cross_ctx_low = cross_context.astype(jnp.bfloat16)
    cross_hidden, cross_norm_back = jax.vjp(
        normalize,
        dec_hidden + project(cross_ctx_low, attn_out[2]) + biases[9],
        norm_gain[3],
        biases[14],
    )
    last_ffn, last_kept = ffn_forward(cross_hidden, ffn_up[1], up_bias[1], ffn_down[1], biases[10])
    final, final_back = jax.vjp(normalize, cross_hidden + last_ffn, norm_gain[4], biases[15])
    final_grad, gain_four, shift_four = final_back(cotangent.astype(jnp.float32))
    into_cross, up_grad_one, upb_grad_one, down_grad_one, bias_ten = ffn_backward(
        final_grad, last_kept, ffn_up[1], ffn_down[1]
    )
    cross_resid_grad, gain_three, shift_three = cross_norm_back(final_grad + into_cross)
    cross_out_low = cross_resid_grad.astype(jnp.bfloat16)
    out_grad_two = weight_grad(cross_ctx_low, cross_out_low)
    cross_q_part, cross_k_part, cross_v_part = attend_backward(
        cross_queries,
        cross_keys,
        cross_values,
        tgt_seg,
        src_seg,
        tgt_lengths,
        src_lengths,
        cross_context,
        cross_total,
        project_back(cross_out_low, attn_out[2]),
    )
    cross_q_low = cross_q_part.astype(jnp.bfloat16)
    cross_kv_low = jnp.concatenate([cross_k_part, cross_v_part], axis=-1).astype(jnp.bfloat16)
    cross_q_weight = weight_grad(dec_hidden_low, cross_q_low)
    cross_kv_weight = weight_grad(memory_low, cross_kv_low)
    memory_grad = project_back(cross_kv_low, cross_kv)
    dec_resid_grad, gain_two, shift_two = dec_norm_back(
        cross_resid_grad + project_back(cross_q_low, cross_q)
    )
    dec_out_low = dec_resid_grad.astype(jnp.bfloat16)
    out_grad_one = weight_grad(dec_ctx_low, dec_out_low)
    dec_q_part, dec_k_part, dec_v_part = attend_backward(
        dec_queries,
        dec_keys,
        dec_values,
        tgt_seg,
        tgt_seg,
        tgt_lengths,
        tgt_lengths,
        dec_context,
        dec_total,
        project_back(dec_out_low, attn_out[1]),
    )
    dec_qkv_low = jnp.concatenate([dec_q_part, dec_k_part, dec_v_part], axis=-1).astype(
        jnp.bfloat16
    )
    qkv_grad_one = weight_grad(dec_low, dec_qkv_low)
    dec_input_grad = dec_resid_grad + project_back(dec_qkv_low, self_qkv[1])
    mask_grad = jnp.sum(dec_input_grad * mask_float, axis=(0, 1))
    memory_resid_grad, gain_one, shift_one = memory_back(memory_grad)
    into_enc, up_grad_zero, upb_grad_zero, down_grad_zero, bias_three = ffn_backward(
        memory_resid_grad, enc_kept, ffn_up[0], ffn_down[0]
    )
    enc_resid_grad, gain_zero, shift_zero = enc_norm_back(memory_resid_grad + into_enc)
    enc_out_low = enc_resid_grad.astype(jnp.bfloat16)
    out_grad_zero = weight_grad(enc_ctx_low, enc_out_low)
    enc_q_part, enc_k_part, enc_v_part = attend_backward(
        enc_queries,
        enc_keys,
        enc_values,
        src_seg,
        src_seg,
        src_lengths,
        src_lengths,
        enc_context,
        enc_total,
        project_back(enc_out_low, attn_out[0]),
    )
    enc_qkv_low = jnp.concatenate([enc_q_part, enc_k_part, enc_v_part], axis=-1).astype(
        jnp.bfloat16
    )
    qkv_grad_zero = weight_grad(enc_input, enc_qkv_low)
    enc_input_grad = enc_resid_grad + project_back(enc_qkv_low, self_qkv[0])
    bias_rows = jnp.stack(
        [
            token_sum(enc_q_part),
            token_sum(enc_v_part),
            token_sum(enc_resid_grad),
            bias_three,
            token_sum(dec_q_part),
            token_sum(dec_v_part),
            token_sum(dec_resid_grad),
            token_sum(cross_q_part),
            token_sum(cross_v_part),
            token_sum(cross_resid_grad),
            bias_ten,
            shift_zero,
            shift_one,
            shift_two,
            shift_three,
            shift_four,
        ]
    )
    shares = (
        lax.psum_scatter(
            jnp.stack([qkv_grad_zero, qkv_grad_one]), "seq", scatter_dimension=1, tiled=True
        ),
        lax.psum_scatter(
            jnp.stack([out_grad_zero, out_grad_one, out_grad_two]),
            "seq",
            scatter_dimension=1,
            tiled=True,
        ),
        lax.psum_scatter(cross_q_weight, "seq", scatter_dimension=0, tiled=True),
        lax.psum_scatter(cross_kv_weight, "seq", scatter_dimension=0, tiled=True),
        lax.psum_scatter(
            jnp.stack([up_grad_zero, up_grad_one]), "seq", scatter_dimension=1, tiled=True
        ),
        lax.psum_scatter(
            jnp.stack([down_grad_zero, down_grad_one]), "seq", scatter_dimension=1, tiled=True
        ),
        lax.psum_scatter(
            jnp.stack([gain_zero, gain_one, gain_two, gain_three, gain_four]),
            "seq",
            scatter_dimension=1,
            tiled=True,
        ),
        lax.psum_scatter(bias_rows, "seq", scatter_dimension=1, tiled=True),
        lax.psum_scatter(
            jnp.stack([upb_grad_zero, upb_grad_one]), "seq", scatter_dimension=1, tiled=True
        ),
        lax.psum_scatter(mask_grad, "seq", scatter_dimension=0, tiled=True),
    )
    totals = lax.psum(
        (
            shares[0],
            shares[1],
            shares[2],
            shares[3],
            shares[4],
            shares[5],
            shares[6],
            shares[7],
            shares[8],
            shares[9],
        ),
        "rows",
    )
    return (
        final.astype(jnp.bfloat16),
        enc_input_grad,
        dec_input_grad,
        totals[0],
        totals[1],
        totals[2],
        totals[3],
        totals[4],
        totals[5],
        totals[6],
        totals[7],
        totals[8],
        totals[9],
    )


LANES = 128
CHANNELS = 96
COST = 50
MIX_COST = 4e9
BIG_VMEM = 64 * 2**20
LOW = jnp.bfloat16
WIDE = jnp.float32
HBM = pl.BlockSpec(memory_space=pltpu.HBM)
SMEM = pl.BlockSpec(memory_space=pltpu.SMEM)


def shape_of(dims, dtype):
    return jax.ShapeDtypeStruct(tuple(dims), dtype)


def distinct(arrays):
    found = []
    for array in arrays:
        if not any(array is other for other in found):
            found.append(array)
    return found


def where_in(arrays, array):
    return [other is array for other in arrays].index(True)


def parameters():
    return pltpu.CompilerParams(vmem_limit_bytes=BIG_VMEM)


def cost(flops, moved):
    return pl.CostEstimate(flops=int(flops), bytes_accessed=int(moved), transcendentals=0)


class Copies:
    def __init__(self, sems):
        self.sems, self.used, self.leaving = sems, 0, []

    def start(self, source, target):
        moved = pltpu.make_async_copy(source, target, self.sems.at[self.used])
        self.used += 1
        moved.start()
        return moved

    def leave(self, source, target):
        self.leaving.append(self.start(source, target))

    def finish(self):
        for moved in self.leaving:
            moved.wait()


class Arrivals:
    def __init__(self, copies, refs, groups):
        self._copies, self._refs, self._groups, self._coming = copies, refs, groups, {}
        self.more()

    def more(self):
        for name, origin, target in self._groups.pop(0) if self._groups else ():
            self._coming.setdefault(name, []).append(self._copies.start(origin, target))

    def finish(self):
        while self._groups:
            self.more()
        for name in self._refs:
            getattr(self, name)

    def __getattr__(self, name):
        while name not in self._coming and any(name == move[0] for group in self._groups for move in group):
            self.more()
        for moved in self._coming.get(name, ()):
            moved.wait()
        self._coming[name] = []
        return self._refs[name]


class Stage(typing.NamedTuple):
    scalars: typing.Any
    use: typing.Any
    out: typing.Any
    work: typing.Any
    copies: typing.Any
    targets: typing.Any

    def push(self, *buffers):
        for buffer in buffers:
            self.push_part(buffer, ())

    def push_part(self, buffer, index):
        target = [result for ref, result in self.targets if ref is buffer][0]
        if isinstance(target, list):
            self.copies.leave(buffer.at[index], target[index[0]].at[index[1:]] if index[1:] else target[index[0]])
        else:
            self.copies.leave(buffer.at[index] if index else buffer, target.at[index] if index else target)


def run_stage(name, body, scalars, parts, outs, work, flops, moved, after=()):
    all_parts = {key: part for group in parts for key, part in group.items()}
    arrays = distinct([move[0] for part in all_parts.values() for move in part[2]])
    after = [array for array in distinct(after) if not any(array is other for other in arrays)]
    flat_outs, spots = [], {}
    for key, shape in outs.items():
        several = shape if isinstance(shape, list) else [shape]
        spots[key] = (len(flat_outs), len(several))
        flat_outs += several
    buffers = [shape_of((len(s),) + s[0].shape, s[0].dtype) if isinstance(s, list) else s for s in outs.values()]

    def kernel(*refs):
        refs = list(refs)

        def take(count):
            taken = refs[:count]
            del refs[:count]
            return taken

        scalar_refs = types.SimpleNamespace(**dict(zip(scalars, take(len(scalars)))))
        inputs = take(len(arrays))
        take(len(after))
        results = take(len(flat_outs))
        part_refs = dict(zip(all_parts, take(len(all_parts))))
        out_refs = dict(zip(outs, take(len(outs))))
        work_refs = dict(zip(work, take(len(work))))
        copies = Copies(refs[0])
        groups = []
        for wanted in parts:
            groups.append([])
            for key, part in wanted.items():
                for array, source, target in part[2]:
                    origin, place = inputs[where_in(arrays, array)], part_refs[key]
                    origin = origin if source is None else origin.at[source(scalar_refs)]
                    groups[-1].append((key, origin, place if target is None else place.at[target]))
        targets = []
        for key, (start, count) in spots.items():
            several = isinstance(outs[key], list)
            targets.append((out_refs[key], list(results[start : start + count]) if several else results[start]))
        use = Arrivals(copies, part_refs, groups)
        stage = Stage(
            scalar_refs, use, types.SimpleNamespace(**out_refs), types.SimpleNamespace(**work_refs), copies, targets
        )
        body(stage)
        use.finish()
        copies.finish()

    given = pl.pallas_call(
        kernel,
        name=name,
        out_shape=flat_outs,
        in_specs=[SMEM] * len(scalars) + [HBM] * (len(arrays) + len(after)),
        out_specs=[HBM] * len(flat_outs),
        scratch_shapes=[pltpu.VMEM(part[0], part[1]) for part in all_parts.values()]
        + [pltpu.VMEM(each.shape, each.dtype) for each in buffers]
        + [pltpu.VMEM(each.shape, each.dtype) for each in work.values()]
        + [pltpu.SemaphoreType.DMA((CHANNELS,))],
        compiler_params=parameters(),
        cost_estimate=cost(flops * COST, moved),
    )(*scalars.values(), *arrays, *after)
    found = {}
    for key, (start, count) in spots.items():
        found[key] = list(given[start : start + count]) if isinstance(outs[key], list) else given[start]
    return types.SimpleNamespace(**found)


def whole(array):
    return (tuple(array.shape), array.dtype, [(array, None, None)])


def layer(array, index):
    return (tuple(array.shape[1:]), array.dtype, [(array, lambda s: index, None)])


def dot_nn(a, b):
    return lax.dot_general(a, b, (((1,), (0,)), ((), ())), preferred_element_type=WIDE)


def dot_nt(a, b):
    return lax.dot_general(a, b, (((1,), (1,)), ((), ())), preferred_element_type=WIDE)


def dot_tn(a, b):
    return lax.dot_general(a, b, (((0,), (0,)), ((), ())), preferred_element_type=WIDE)


def total(values):
    return jnp.sum(values, axis=0, keepdims=True)


def norm_parts(residual):
    centred = residual - jnp.mean(residual, axis=-1, keepdims=True)
    scale = lax.rsqrt(jnp.mean(centred * centred, axis=-1, keepdims=True) + EPSILON)
    return centred * scale, scale


def norm_keep(stage, residual, gain, shift, hat_ref, scale_ref):
    hat, scale = norm_parts(residual)
    hat_ref[...] = hat.astype(LOW)
    scale_ref[...] = jnp.broadcast_to(scale, scale_ref.shape)
    stage.push(hat_ref, scale_ref)
    return hat * gain + shift


def norm_back(grad, hat, scale, gain):
    scaled = grad * gain
    inner = jnp.mean(scaled, axis=-1, keepdims=True)
    along = jnp.mean(scaled * hat, axis=-1, keepdims=True)
    return scale * (scaled - inner - hat * along), total(grad * hat), total(grad)


def segment_ids(lengths_ref, row, places):
    end = jnp.int32(0)
    found = jnp.zeros(places.shape, jnp.int32)
    for slot in range(lengths_ref.shape[1]):
        end = end + lengths_ref[row, slot]
        found = found + (end <= places).astype(jnp.int32)
    return found


def positions(me, length, shape, axis):
    token = lax.broadcasted_iota(jnp.int32, shape, axis)
    bits = length.bit_length() - 1
    block = lax.shift_right_logical(token, jnp.int32(bits))
    return lax.shift_left(jnp.bitwise_xor(block, me), jnp.int32(bits)) + jnp.bitwise_and(token, length - 1)


def fill_bias(bias_ref, query_lengths, key_lengths, me, length):
    tokens = bias_ref.shape[0]
    query_seg = segment_ids(query_lengths, me, positions(me, length, (1, tokens), 1))
    key_seg = segment_ids(key_lengths, me, positions(me, length, (tokens, 1), 0))
    bias_ref[...] = jnp.where(key_seg == query_seg, 0.0, NEG_FILL)


def heads_of(values):
    return values.reshape(HEADS, HEAD_DIM, values.shape[-1])


def flat(ref):
    return ref[...].reshape(HEADS * HEAD_DIM, ref.shape[-1])


def attention_forward(q_ref, k_ref, v_ref, bias_ref, exp_ref, inverse_ref, context_ref):
    for head in range(HEADS):
        scores = dot_tn(k_ref[head], q_ref[head]) + bias_ref[...]
        peak = jnp.max(scores, axis=0, keepdims=True)
        exps = jnp.exp(scores - peak)
        inverse = 1.0 / jnp.sum(exps, axis=0, keepdims=True)
        low_exps = exps.astype(LOW)
        exp_ref[head] = low_exps
        inverse_ref[head] = jnp.broadcast_to(inverse, inverse_ref.shape[1:])
        context_ref[head] = (dot_nn(v_ref[head], low_exps) * inverse).astype(LOW)


def attention_backward(q_ref, k_ref, v_ref, exp_ref, inverse_ref, context_ref, work):
    for head in range(HEADS):
        exps = exp_ref[head]
        grad = (work.context_grad[head].astype(LOW).astype(WIDE) * inverse_ref[head][0:1]).astype(LOW)
        delta = total(grad.astype(WIDE) * context_ref[head].astype(WIDE))
        score_grad = (exps.astype(WIDE) * (dot_tn(v_ref[head], grad) - delta)).astype(LOW)
        dv = dot_nt(grad, exps)
        dq = dot_nn(k_ref[head], score_grad) * HEAD_DIM ** (-0.5)
        work.dv[head] = dv.astype(LOW)
        work.dk[head] = dot_nt(q_ref[head], score_grad).astype(LOW)
        work.dq[head] = dq.astype(LOW)
        wide = (HEAD_DIM, LANES)
        work.sums[0, head] = jnp.broadcast_to(jnp.sum(dq, axis=1, keepdims=True), wide)
        work.sums[1, head] = jnp.broadcast_to(jnp.sum(dv, axis=1, keepdims=True), wide)


def sum_row(sums_ref, which):
    return jnp.transpose(sums_ref[which].reshape(HEADS * HEAD_DIM, LANES))[0:1]


def qkv_forward(stage, weight, low_t, bias_t, q_col, v_col, q_ref, k_ref, v_ref):
    d = low_t.shape[0]
    queries = (dot_tn(weight[:, 0:d], low_t) + bias_t[:, q_col : q_col + 1]).astype(LOW)
    q_ref[...] = heads_of(queries * HEAD_DIM ** (-0.5))
    k_ref[...] = heads_of(dot_tn(weight[:, d : 2 * d], low_t).astype(LOW))
    v_ref[...] = heads_of((dot_tn(weight[:, 2 * d :], low_t) + bias_t[:, v_col : v_col + 1]).astype(LOW))
    stage.push(q_ref, k_ref, v_ref)


def gelu_parts(pre):
    half = 0.5 * (1.0 + lax.erf(pre * 0.5**0.5))
    density = jnp.exp(pre * pre * -0.5) * (0.5 / 3.141592653589793) ** 0.5
    return pre * half, half + pre * density


def feed_forward(low, up, up_bias, down, act_ref, slope_ref):
    width = low.shape[1]
    for j in range(act_ref.shape[1] // width):
        cols = slice(j * width, (j + 1) * width)
        act, slope = gelu_parts(dot_nn(low, up[:, cols]) + up_bias[:, cols])
        act_ref[:, cols] = act.astype(LOW)
        slope_ref[:, cols] = slope.astype(LOW)
    return dot_nn(act_ref[...], down[...])


class Halves(typing.NamedTuple):
    ref: typing.Any
    first: int
    rest: int
    me: typing.Any
    core: typing.Any
    stage: typing.Any

    def leave_regions(self, start, rows):
        for side in (0, 1):
            for begin in (start, start + 2 * (self.first + self.rest)):
                self.stage.push_part(self.ref, (side, slice(begin, begin + rows)))

    def leave_first(self, rows):
        self.leave_regions(0, 2 * self.first)

    def leave_rest(self, rows):
        self.leave_regions(2 * self.first, 2 * self.rest)

    def put(self, half, chunk, start, rows):
        away = jnp.bitwise_xor(self.me, chunk)
        low, high = jnp.bitwise_and(away, 1), lax.shift_right_logical(away, 1)
        both = 2 * (self.first + self.rest)
        if start < self.first:
            place = high * self.first + jnp.where(low == 1, 0, both) + start
        else:
            place = low * self.rest + jnp.where(high == 1, 0, both) + 2 * self.first + start - self.first
        side = jnp.bitwise_xor(self.core, half)
        self.ref[side, pl.ds(pl.multiple_of(place, 16), rows.shape[0])] = rows.astype(LOW)


def put_units(grads, block, half, unit):
    rows = LANES
    for chunk in range(block.shape[0] // rows):
        grads.put(half, chunk, unit * rows, block[chunk * rows : (chunk + 1) * rows])


def feed_back(out_grad, low, act, slope, up, down, vec_ref, vec_row, grads, pre_ref, more=None):
    width = out_grad.shape[1]
    half = width // 2
    out_low = out_grad.astype(LOW)
    columns = [slice(j * width, (j + 1) * width) for j in range(pre_ref.shape[1] // width)]
    for j, cols in enumerate(columns):
        pre = dot_nt(out_low, down[cols, :]) * slope[:, cols].astype(WIDE)
        vec_ref[vec_row + j : vec_row + j + 1, :] = total(pre)
        pre_ref[:, cols] = pre.astype(LOW)
        down_grad = dot_tn(act[:, cols], out_low)
        for r in range(2):
            grads.put(r, j, half, down_grad[r * half : (r + 1) * half])
    grads.leave_rest(half)
    low, up = low(), up()
    for j, cols in enumerate(columns):
        put_units(grads, dot_tn(low[...], pre_ref[:, cols]), j // 2, j % 2)
    grads.leave_first(half)
    return dot_nt(pre_ref[...], up[...])


def own_row(s):
    return s.ids[0]


def token_pieces(local, others, length, start=0):
    pieces = [(local, own_row, (slice(0, length),))]
    for d, array in enumerate(others, 1):
        pieces.append((array, lambda s: (slice(start, start + length),), (slice(d * length, (d + 1) * length),)))
    return pieces


def put_blocks(ref, values):
    for i in range(ref.shape[0]):
        ref[i] = values[i * ref.shape[1] : (i + 1) * ref.shape[1]]


def encoder_forward(length, stage):
    me, use, out = stage.scalars.ids[0], stage.use, stage.out
    fill_bias(stage.work.bias, stage.scalars.src, stage.scalars.src, me, length)
    x = use.x[...]
    x_t = jnp.transpose(x)
    out.x_t[...] = x_t
    stage.push(out.x_t)
    biases = use.biases[...]
    qkv = use.qkv
    use.more()
    qkv_forward(stage, qkv, x_t, jnp.transpose(biases), 0, 1, out.q, out.k, out.v)
    attention_forward(out.q, out.k, out.v, stage.work.bias, out.exps, out.inverse, out.context)
    stage.push(out.exps, out.inverse, out.context)
    gains = use.gains
    residual = x.astype(WIDE) + dot_tn(flat(out.context), use.proj[...]) + biases[2:3]
    hidden = norm_keep(stage, residual, gains[0:1], biases[11:12], out.hat0, out.scale0)
    hidden_low = hidden.astype(LOW)
    out.low1[...] = hidden_low
    stage.push(out.low1)
    ffn = feed_forward(hidden_low, use.up, use.up_bias[0:1], use.down, out.act1, out.slope1)
    stage.push(out.act1, out.slope1)
    memory = norm_keep(stage, hidden + ffn + biases[3:4], gains[1:2], biases[12:13], out.hat1, out.scale1)
    out.memory_t[...] = jnp.transpose(memory.astype(LOW))
    stage.push(out.memory_t)


def mask_columns(mask, d):
    row = jnp.concatenate([mask[i][0:1, 0:LANES].astype(WIDE) for i in range(mask.shape[0])], axis=1)
    columns = jnp.transpose(jnp.broadcast_to(row, (LANES, row.shape[1])))
    return jnp.concatenate([columns] * (d // LANES), axis=1)


def decoder(length, stage):
    me, use, out, work = stage.scalars.ids[0], stage.use, stage.out, stage.work
    biases = use.biases[...]
    bias_t = jnp.transpose(biases)
    gains = use.gains
    src, tgt = stage.scalars.src, stage.scalars.tgt
    fill_bias(work.bias, tgt, tgt, me, length)
    x = use.x[...].astype(WIDE)
    d = x.shape[1]
    y = x + mask_columns(use.mask, d) * use.embed[...]
    y_t = jnp.transpose(y.astype(LOW))
    out.x_t[...] = y_t
    stage.push(out.x_t)
    qkv = use.qkv
    use.more()
    qkv_forward(stage, qkv, y_t, bias_t, 4, 5, out.q2, out.k2, out.v2)
    use.more()
    attention_forward(out.q2, out.k2, out.v2, work.bias, out.exps2, out.inverse2, out.context2)
    stage.push(out.exps2, out.inverse2, out.context2)
    residual = y + dot_tn(flat(out.context2), use.proj1[...]) + biases[6:7]
    hidden = norm_keep(stage, residual, gains[2:3], biases[13:14], out.hat2, out.scale2)
    hidden_t = jnp.transpose(hidden.astype(LOW))
    work.hidden_t[...] = hidden_t
    queries = (dot_tn(use.cross_q[...], hidden_t) + bias_t[:, 7:8]).astype(LOW)
    work.q[...] = heads_of(queries * HEAD_DIM ** (-0.5))
    memory_t = use.memory_t
    kv = use.cross_kv
    work.k[...] = heads_of(dot_tn(kv[:, 0:d], memory_t[...]).astype(LOW))
    work.v[...] = heads_of((dot_tn(kv[:, d:], memory_t[...]) + bias_t[:, 8:9]).astype(LOW))
    fill_bias(work.bias, tgt, src, me, length)
    attention_forward(work.q, work.k, work.v, work.bias, work.exps, work.inverse, work.context)
    proj = use.proj2
    residual = hidden + dot_tn(flat(work.context), proj[...]) + biases[9:10]
    hat, scale = norm_parts(residual)
    work.hat[...] = hat
    work.scale[...] = jnp.broadcast_to(scale, work.scale.shape)
    hidden = hat * gains[3:4] + biases[14:15]
    work.low[...] = hidden.astype(LOW)
    up, down = use.up, use.down
    ffn = feed_forward(work.low[...], up, use.up_bias[1:2], down, work.act, work.slope)
    hat, scale = norm_parts(hidden + ffn + biases[10:11])
    put_blocks(out.final, (hat * gains[4:5] + biases[15:16]).astype(LOW))
    for i in range(out.final.shape[0]):
        stage.push_part(out.final, (i,))
    vec, vec_cross = out.vec, out.vec_cross
    vec[...] = jnp.zeros_like(vec)
    vec_cross[...] = jnp.zeros_like(vec_cross)
    cotangent = use.cotangent[...].astype(WIDE)
    grad, vec[0:1, :], vec[1:2, :] = norm_back(cotangent, hat, scale, gains[4:5])
    vec[2:3, :] = total(grad)
    into = feed_back(
        grad,
        lambda: work.low,
        work.act,
        work.slope,
        lambda: up,
        down,
        vec,
        3,
        Halves(out.grads, 2 * LANES, 2 * LANES, me, stage.scalars.ids[1], stage),
        work.pre,
    )
    stage.push(vec)
    grads = Halves(out.grads_cross, LANES, LANES, me, stage.scalars.ids[1], stage)
    grad = out_backward(
        grad + into, work.hat[...], work.scale[:, 0:1], gains[3:4], proj, work.context, work, vec_cross, grads
    )
    attention_backward(work.q, work.k, work.v, work.exps, work.inverse, work.context, work)
    dq, dk, dv = attention_sums(work, vec_cross)
    stage.push(vec_cross)
    put_units(grads, dot_nt(work.hidden_t[...], dq), 0, 1)
    put_units(grads, dot_nt(memory_t[...], dk), 1, 0)
    put_units(grads, dot_nt(memory_t[...], dv), 1, 1)
    grads.leave_first(0)
    grads.leave_rest(0)
    out.memory_grad[...] = jnp.transpose(dot_nn(kv[:, 0:d], dk) + dot_nn(kv[:, d:], dv))
    stage.push(out.memory_grad)
    out.hidden_grad[...] = grad + jnp.transpose(dot_nn(use.cross_q[...], dq))
    stage.push(out.hidden_grad)


def out_backward(grad, hat, scale, gain, proj, context, work, vec, grads):
    grad, vec[0:1, :], vec[1:2, :] = norm_back(grad, hat, scale, gain)
    vec[2:3, :] = total(grad)
    low = grad.astype(LOW)
    work.context_grad[...] = heads_of(dot_nt(proj[...], low))
    put_units(grads, dot_nn(flat(context), low), 0, 0)
    return grad


def attention_sums(work, vec):
    vec[3:4, :] = sum_row(work.sums, 0)
    vec[4:5, :] = sum_row(work.sums, 1)
    return flat(work.dq), flat(work.dk), flat(work.dv)


def encoder_ffn_backward(stage):
    me, core = stage.scalars.ids[0], stage.scalars.ids[1]
    use, out = stage.use, stage.out
    vec = out.vec
    vec[...] = jnp.zeros_like(vec)
    hat, scale, grad = use.hat, use.scale, use.grad
    use.more()
    hat, scale = hat[...].astype(WIDE), scale[...][:, 0:1]
    grad, vec[0:1, :], vec[1:2, :] = norm_back(grad[...], hat, scale, use.gains[1:2])
    vec[2:3, :] = total(grad)
    grads = Halves(out.grads, 2 * LANES, 2 * LANES, me, core, stage)
    down, slope, act = use.down, use.slope, use.act
    use.more()
    into = feed_back(
        grad, lambda: use.low, act, slope, lambda: use.up, down, vec, 3, grads, stage.work.pre
    )
    stage.push(vec)
    out.grad1[...] = grad + into
    stage.push(out.grad1)


def put_vectors(grads, start, own, others):
    d = own.shape[1]
    for chunk in range(d // LANES):
        cols = slice(chunk * LANES, (chunk + 1) * LANES)
        first = jnp.concatenate([own[:, cols]] + [each[:, cols] for each in others[:3]], axis=1)
        first = jnp.concatenate([first, jnp.zeros_like(first)], axis=0)
        second = jnp.concatenate([others[3][:, cols], jnp.zeros((8, d - LANES), WIDE)], axis=1)
        ups = [each[3 + chunk : 4 + chunk] for each in (others[0], others[3])]
        second = jnp.concatenate([second] + ups + [jnp.zeros((6, d), WIDE)], axis=0)
        grads.put(0, chunk, start, first)
        grads.put(1, chunk, start, second)


def self_backward(norm_row, last, stage):
    me, core = stage.scalars.ids[0], stage.scalars.ids[1]
    use, out, work = stage.use, stage.out, stage.work
    vec = work.vec
    grads = Halves(out.grads, LANES, LANES + (16 if last else 0), me, core, stage)
    vec[...] = jnp.zeros_like(vec)
    hat, scale, grad, proj, context = use.hat, use.scale, use.grad, use.proj, use.context
    use.more()
    hat, scale = hat[...].astype(WIDE), scale[...][:, 0:1]
    gain = use.gains[norm_row : norm_row + 1]
    grad = out_backward(grad[...], hat, scale, gain, proj, context, work, vec, grads)
    q, k, v, exps, inverse = use.q, use.k, use.v, use.exps, use.inverse
    use.more()
    attention_backward(q, k, v, exps, inverse, context, work)
    dq, dk, dv = attention_sums(work, vec)
    x_t = use.x_t[...]
    put_units(grads, dot_nt(x_t, dk), 1, 0)
    grads.leave_first(0)
    put_units(grads, dot_nt(x_t, dq), 0, 1)
    put_units(grads, dot_nt(x_t, dv), 1, 1)
    if last:
        others = [each[...] for each in (use.vec_enc, use.vec_self, use.vec_cross, use.vec_dec)]
        put_vectors(grads, 2 * LANES, vec[...], others)
    grads.leave_rest(0)
    qkv = use.qkv
    d = x_t.shape[0]
    through = dot_nn(qkv[:, 0:d], dq) + dot_nn(qkv[:, d : 2 * d], dk) + dot_nn(qkv[:, 2 * d :], dv)
    input_grad = grad + jnp.transpose(through)
    if not last:
        vec[5:6, :] = total(input_grad * mask_columns(use.mask, d))
        out.vec[...] = vec[...]
        stage.push(out.vec)
    out.input_grad[...] = input_grad.astype(LOW)
    stage.push(out.input_grad)


def swap(array, axis_name, bit):
    size = lax.axis_size(axis_name)
    return lax.ppermute(array, axis_name, [(i, i ^ bit) for i in range(size)])


def spread_rows(local, me):
    return [
        swap(lax.dynamic_index_in_dim(local, me ^ d, 0, keepdims=False), "seq", d) for d in range(1, local.shape[0])
    ]


def pack_rows(ids, dec_input, cotangent, masked):
    count, length, d = dec_input.shape
    rows = 2 * length + 16

    def kernel(ids_ref, mask_ref, dec_ref, cot_ref, *refs):
        results, scratch, copies = refs[:count], refs[count], Copies(refs[count + 1])
        me = ids_ref[0]
        coming = []
        for away in range(1, count):
            row = jnp.bitwise_xor(me, away)
            coming.append(copies.start(dec_ref.at[row], scratch.at[away, 0:length]))
            coming.append(copies.start(cot_ref.at[row], scratch.at[away, length : 2 * length]))
        for away in range(count):
            row = mask_ref[jnp.bitwise_xor(me, away)].astype(WIDE).astype(LOW)
            row = jnp.concatenate([jnp.broadcast_to(row, (16, length))] * (d // length), axis=1)
            scratch[away, 2 * length : rows] = row
        copies.leave(scratch.at[0, 2 * length : rows], results[0])
        for away in range(1, count):
            coming[2 * away - 2].wait()
            coming[2 * away - 1].wait()
            copies.leave(scratch.at[away], results[away])
        copies.finish()

    return pl.pallas_call(
        kernel,
        name="pack_rows",
        out_shape=[shape_of((16, d), LOW)] + [shape_of((rows, d), LOW)] * (count - 1),
        in_specs=[SMEM, pl.BlockSpec(memory_space=pltpu.VMEM), HBM, HBM],
        out_specs=[HBM] * count,
        scratch_shapes=[pltpu.VMEM((count, rows, d), LOW), pltpu.SemaphoreType.DMA((3 * count,))],
        compiler_params=parameters(),
        cost_estimate=cost(0, 2e6),
    )(ids, masked.reshape(count, 1, length), dec_input, cotangent)


class Piece(typing.NamedTuple):
    array: typing.Any
    start: int
    rows: int
    half: int = -1

    def halved(self, half):
        return self._replace(half=half)

    @property
    def lanes(self):
        width = self.array.shape[-1]
        return width if self.half < 0 else width // 2

    def origin(self, ref, place):
        if self.half < 0:
            return ref.at[pl.ds(self.start, self.rows)]
        start = pl.multiple_of(jnp.bitwise_xor(place, self.half) * self.lanes, self.lanes)
        return ref.at[pl.ds(self.start, self.rows), pl.ds(start, self.lanes)]


class Step(typing.NamedTuple):
    channel: typing.Any
    sources: tuple


X, Y, DIAGONAL, PAIR, PAIRS = 0, 1, 2, 3, 4
CHANNEL = (("seq", 1), ("seq", 2), ("seq", 3), ("rows", 2), ("rows", 4))


def boundary(name, ids, steps, after=(), weight=1):
    arrays = distinct([piece.array for step in steps for piece in step.sources])
    after = [array for array in distinct(after) if not any(array is other for other in arrays)]
    outs, places = {}, []
    for step in steps:
        rows = step.sources[0].rows
        key = (step.channel, step.sources[0].lanes)
        start = outs.get(key, 0)
        outs[key] = start + rows
        places.append((key, start, rows))
    keys = list(outs)
    tally = sum(len(step.sources) for step in steps) + len(steps)

    def kernel(ids_ref, *refs):
        inputs, refs = refs[: len(arrays)], refs[len(arrays) + len(after) :]
        results, refs = dict(zip(keys, refs)), refs[len(keys) :]
        buffers, refs = dict(zip(keys, refs)), refs[len(keys) :]
        scratch, copies = list(refs[:-1]), Copies(refs[-1])
        coming = []
        for step in steps:
            for piece in step.sources:
                origin = piece.origin(inputs[where_in(arrays, piece.array)], ids_ref[2])
                coming.append((copies.start(origin, scratch[len(coming)]), scratch[len(coming)]))
        for step, (key, start, rows) in zip(steps, places):
            terms = []
            for _ in step.sources:
                moved, ref = coming.pop(0)
                moved.wait()
                terms.append(ref)
            rest = slice(start, start + rows)
            summed = functools.reduce(jnp.add, [term[...].astype(WIDE) for term in terms])
            buffers[key][rest, :] = summed.astype(LOW)
            copies.leave(buffers[key].at[rest], results[key].at[rest])
        copies.finish()

    shapes = [shape_of((outs[key], key[1]), LOW) for key in keys]
    given = pl.pallas_call(
        kernel,
        name=name,
        out_shape=shapes,
        in_specs=[SMEM] + [HBM] * (len(arrays) + len(after)),
        out_specs=[HBM] * len(keys),
        scratch_shapes=[pltpu.VMEM(each.shape, LOW) for each in shapes]
        + [pltpu.VMEM((piece.rows, piece.lanes), LOW) for step in steps for piece in step.sources]
        + [pltpu.SemaphoreType.DMA((tally,))],
        compiler_params=parameters(),
        cost_estimate=cost(MIX_COST * weight, 0),
    )(ids, *arrays, *after)
    formed = dict(zip(keys, given))
    arrived = {key: swap(formed[key], *CHANNEL[key[0]]) for key in keys if key[0] is not None}
    pieces = []
    for key, start, rows in places:
        mine = Piece(formed[key], start, rows)
        pieces.append((mine, mine._replace(array=arrived[key]) if key in arrived else None))
    return pieces, list(given)


class Flow:
    def __init__(self, grads, first, rest):
        keep, send = grads
        self.arrays = (keep, swap(send, "rows", 1))
        self.first, self.rest, self.at = first, rest, 0
        self.sent = self.arrived = None

    def both(self, start, rows):
        return tuple(Piece(array, start, rows) for array in self.arrays)

    def next_steps(self):
        a, b = self.first, self.rest
        own = 2 * (a + b)
        if self.at == 0:
            return [Step(X, self.both(0, 2 * a)), Step(Y, self.both(2 * a, 2 * b))]
        x, y = self.arrived
        if self.at == 1:
            self.x, self.y = x, y
            return [
                Step(Y, self.both(own + a, a) + (x._replace(start=x.start + a, rows=a),)),
                Step(X, self.both(own + 2 * a + b, b) + (y._replace(start=y.start + b, rows=b),)),
            ]
        if self.at == 2:
            sums = [
                self.both(own, a) + (self.x._replace(rows=a), x),
                self.both(own + 2 * a, b) + (self.y._replace(rows=b), y),
            ]
            return [
                Step(channel, tuple(piece.halved(half) for piece in each))
                for channel, half in ((PAIR, 1), (None, 0))
                for each in sums
            ]
        if self.at == 3:
            return [Step(PAIRS, (self.sent[2], x)), Step(PAIRS, (self.sent[3], y))]
        return [Step(PAIR, (self.sent[0], x)), Step(PAIR, (self.sent[1], y))]

    def take(self, pieces):
        self.sent = [piece[0] for piece in pieces]
        self.arrived = [piece[1] for piece in pieces[:2]]
        self.at += 1

    def parts(self, own, other):
        done = []
        for z_other, pieces in enumerate((self.sent, self.arrived)):
            start = 0
            for piece in pieces:
                for c_other, arrays in enumerate((own, other)):
                    done.append((piece._replace(array=arrays[z_other]), c_other, z_other, start))
                start += piece.rows
        return done

    @property
    def rows(self):
        return self.first + self.rest


def advance(name, ids, flows, extra=(), after=(), weight=1):
    steps, counts = [], []
    for flow in flows:
        own = flow.next_steps()
        counts.append(len(own))
        steps += own
    steps += list(extra)
    pieces, arrays = boundary(name, ids, steps, after, weight)
    for flow, n in zip(flows, counts):
        flow.take(pieces[:n])
        pieces = pieces[n:]
    return pieces, arrays


def cross_cores(flows):
    own = (flows[0].sent[0].array, flows[0].arrived[0].array)
    return own, tuple(swap(array, "rows", 1) for array in own)


def finish_units(name, ids, groups, outs, old, returns=(), vectors=None, after=()):
    parts = [part for _, group, _ in groups for part in group]
    back = [block for _, blocks in returns for block in blocks]
    arrays = distinct([part[0].array for part in parts] + [block.array for block in back])
    kept, names = list(old), list(outs)
    vector_outs = [outs[each] for each in vectors or ()]
    d = HEADS * HEAD_DIM

    def kernel(ids_ref, *refs):
        refs = list(refs)

        def take(count):
            taken = refs[:count]
            del refs[:count]
            return taken

        inputs = take(len(arrays))
        take(len(kept) + len(after))
        results = dict(zip(names, take(len(names))))
        scratch, back_in = take(len(parts)), take(len(back))
        units, back_out, vec_out = take(len(groups)), take(len(returns)), take(len(vector_outs))
        copies = Copies(refs[0])
        me, core, place = ids_ref[0], ids_ref[1], ids_ref[2]

        def bring(piece, target):
            return copies.start(piece.origin(inputs[where_in(arrays, piece.array)], place), target)

        coming = [bring(part[0], target) for part, target in zip(parts, scratch)]
        blocks_coming = [bring(block, target) for block, target in zip(back, back_in)]
        slot = 0
        for (_, group, goals), unit in zip(groups, units):
            for piece, c_other, z_other, start in group:
                coming[slot].wait()
                side, rows = jnp.bitwise_xor(core, c_other), slice(start, start + piece.rows)
                if piece.lanes == d:
                    unit[side, rows, :] = scratch[slot][...].astype(WIDE)
                else:
                    offset = pl.multiple_of(jnp.bitwise_xor(place, z_other) * piece.lanes, piece.lanes)
                    unit[side, rows, pl.ds(offset, piece.lanes)] = scratch[slot][...].astype(WIDE)
                slot += 1
            for half, start, rows, output, index in goals:
                copies.leave(unit.at[half, start : start + rows], results[output].at[index])
        if vectors:
            last = groups[-1][0]
            top, low = units[-1][0, last - 16 : last, :], units[-1][1, last - 16 : last, :]
            stages = [top[0:8, i * LANES : (i + 1) * LANES] for i in range(4)] + [low[0:8, 0:LANES]]
            enc_s, enc_f, dec_s, crs, dec_f = stages
            gains, biases, ups, embed = vec_out
            for row, part in enumerate(stages):
                gains[row : row + 1, :] = part[0:1]
                biases[11 + row : 12 + row, :] = part[1:2]
            order = ((enc_s, 3), (enc_s, 4), (enc_s, 2), (enc_f, 2), (dec_s, 3), (dec_s, 4), (dec_s, 2))
            order += ((crs, 3), (crs, 4), (crs, 2), (dec_f, 2))
            for row, (part, at) in enumerate(order):
                biases[row : row + 1, :] = part[at : at + 1]
            ups[...] = low[8:10, :]
            embed[...] = dec_s[5:6]
            for output, buffer in zip(vectors, vec_out):
                copies.leave(buffer, results[output])
        slot = 0
        for (output, blocks), buffer in zip(returns, back_out):
            for block in range(len(blocks)):
                blocks_coming[slot].wait()
                buffer[jnp.bitwise_xor(me, block)] = back_in[slot][...].astype(buffer.dtype)
                slot += 1
            copies.leave(buffer, results[output])
        copies.finish()

    sems = len(parts) + len(back) + sum(len(goals) for _, _, goals in groups) + len(returns) + len(vector_outs)
    given = pl.pallas_call(
        kernel,
        name=name,
        out_shape=[outs[each] for each in names],
        in_specs=[SMEM] + [HBM] * (len(arrays) + len(kept) + len(after)),
        out_specs=[HBM] * len(names),
        scratch_shapes=[pltpu.VMEM((part[0].rows, part[0].lanes), LOW) for part in parts]
        + [pltpu.VMEM((block.rows, block.lanes), LOW) for block in back]
        + [pltpu.VMEM((2, rows, d), WIDE) for rows, _, _ in groups]
        + [pltpu.VMEM(outs[output].shape, outs[output].dtype) for output, _ in returns]
        + [pltpu.VMEM(each.shape, each.dtype) for each in vector_outs]
        + [pltpu.SemaphoreType.DMA((sems,))],
        input_output_aliases={1 + len(arrays) + i: names.index(each) for i, each in enumerate(kept)},
        compiler_params=parameters(),
        cost_estimate=cost(MIX_COST, 0),
    )(ids, *arrays, *[old[each] for each in kept], *after)
    return types.SimpleNamespace(**dict(zip(names, given)))


def by_rows(
    enc_input,
    dec_input,
    src_lengths,
    tgt_lengths,
    masked,
    cotangent,
    self_qkv,
    attn_out,
    cross_q,
    cross_kv,
    ffn_up,
    ffn_down,
    norm_gain,
    biases,
    up_bias,
    mask_embed,
):
    count, length, d = enc_input.shape
    tokens, ff = count * length, ffn_up.shape[2]
    me = lax.axis_index("seq")
    row = lax.axis_index("rows")
    ids = jnp.stack([me, row % 2, row // 2 % 2]).astype(jnp.int32)
    enc_others = spread_rows(enc_input, me)
    packed = pack_rows(ids, dec_input, cotangent, masked)
    packs = [swap(packed[away], "seq", away) for away in range(1, count)]
    embed = mask_embed.reshape(1, d)
    head_shape = (HEADS, HEAD_DIM, tokens)
    low_tokens, wide_tokens = shape_of((tokens, d), LOW), shape_of((tokens, d), WIDE)
    low_t, low_heads, low_ff = shape_of((d, tokens), LOW), shape_of(head_shape, LOW), shape_of((tokens, ff), LOW)
    exps, inverse = shape_of((HEADS, tokens, tokens), LOW), shape_of((HEADS, 8, tokens), WIDE)
    scale, vec = shape_of((tokens, LANES), WIDE), shape_of((8, d), WIDE)
    bias = shape_of((tokens, tokens), WIDE)
    scalars = dict(ids=ids, src=src_lengths, tgt=tgt_lengths)
    step = dict(ids=ids)
    small = dict(biases=whole(biases), gains=whole(norm_gain))
    dense, score = 2 * tokens * d * d, 2 * tokens * tokens * d
    mask_pieces = [(packed[0], None, (0,))]
    for i, array in enumerate(packs, 1):
        mask_pieces.append((array, lambda s: (slice(2 * length, 2 * length + 16),), (i,)))
    mask_part = ((count, 16, d), LOW, mask_pieces)

    def tokens_of(local, others, start=0):
        return ((tokens, d), LOW, token_pieces(local, others, length, start))

    def halves(rows):
        return [shape_of((count * rows, d), LOW)] * 2

    enc = run_stage(
        "encoder_forward",
        functools.partial(encoder_forward, length),
        scalars,
        [dict(
            x=tokens_of(enc_input, enc_others),
            **small,
            qkv=layer(self_qkv, 0),
            proj=layer(attn_out, 0),
            up_bias=whole(up_bias),
            up=layer(ffn_up, 0),
            down=layer(ffn_down, 0),
        )],
        dict(
            x_t=low_t,
            q=low_heads,
            k=low_heads,
            v=low_heads,
            exps=exps,
            inverse=inverse,
            context=low_heads,
            hat0=low_tokens,
            scale0=scale,
            low1=low_tokens,
            act1=low_ff,
            slope1=low_ff,
            hat1=low_tokens,
            scale1=scale,
            memory_t=low_t,
        ),
        dict(bias=bias),
        12 * dense + 2 * score,
        24e6,
        after=packed[1:],
    )
    attention_work = dict(
        context_grad=shape_of(head_shape, WIDE),
        dq=low_heads,
        dk=low_heads,
        dv=low_heads,
        sums=shape_of((2, HEADS, HEAD_DIM, LANES), WIDE),
    )
    dec = run_stage(
        "decoder",
        functools.partial(decoder, length),
        scalars,
        [dict(
            **small,
            mask=mask_part,
            x=tokens_of(dec_input, packs),
            embed=whole(embed),
            qkv=layer(self_qkv, 1),
            proj1=layer(attn_out, 1),
            cross_q=whole(cross_q),
            memory_t=whole(enc.memory_t),
            cross_kv=whole(cross_kv),
            proj2=layer(attn_out, 2),
            up_bias=whole(up_bias),
            up=layer(ffn_up, 1),
            down=layer(ffn_down, 1),
            cotangent=tokens_of(cotangent, packs, length),
        )],
        dict(
            x_t=low_t,
            q2=low_heads,
            k2=low_heads,
            v2=low_heads,
            exps2=exps,
            inverse2=inverse,
            context2=low_heads,
            hat2=low_tokens,
            scale2=scale,
            final=[shape_of((length, d), LOW)] * count,
            vec=vec,
            vec_cross=vec,
            grads=halves(4 * LANES),
            grads_cross=halves(2 * LANES),
            memory_grad=wide_tokens,
            hidden_grad=wide_tokens,
        ),
        dict(
            bias=bias,
            low=low_tokens,
            act=low_ff,
            slope=low_ff,
            pre=low_ff,
            hidden_t=low_t,
            hat=wide_tokens,
            scale=scale,
            q=low_heads,
            k=low_heads,
            v=low_heads,
            exps=exps,
            inverse=inverse,
            context=low_heads,
            **attention_work,
        ),
        40 * dense + 8 * score,
        50e6,
    )

    def attention_parts(context, inverse, q, k, v, exps):
        return dict(
            context=whole(context),
            inverse=whole(inverse),
            q=whole(q),
            k=whole(k),
            v=whole(v),
            exps=whole(exps),
        )

    final_back = [swap(dec.final[i], "seq", i) for i in range(1, count)]
    flow_ffn, flow_cross = Flow(dec.grads, 2 * LANES, 2 * LANES), Flow(dec.grads_cross, LANES, LANES)
    first_flows = [flow_ffn, flow_cross]

    def self_stage(name, norm_row, last, grad, hat, scale, attention, x_t, index, more, after):
        rows = 2 * LANES + (16 if last else 0)
        return run_stage(
            name,
            functools.partial(self_backward, norm_row, last),
            step,
            [dict(
                gains=whole(norm_gain),
                grad=whole(grad),
                hat=whole(hat),
                scale=whole(scale),
                proj=layer(attn_out, index),
                **attention_parts(*attention),
                x_t=whole(x_t),
                qkv=layer(self_qkv, index),
                **more,
            )],
            dict(input_grad=low_tokens, grads=halves(rows), **({} if last else dict(vec=vec))),
            dict(vec=vec, **attention_work),
            8 * dense + 4 * score,
            20e6,
            after,
        )

    enc_ffn = run_stage(
        "encoder_ffn_backward",
        encoder_ffn_backward,
        step,
        [dict(
            gains=whole(norm_gain),
            grad=whole(dec.memory_grad),
            hat=whole(enc.hat1),
            scale=whole(enc.scale1),
            down=layer(ffn_down, 0),
            slope=whole(enc.slope1),
            act=whole(enc.act1),
            low=whole(enc.low1),
            up=layer(ffn_up, 0),
        )],
        dict(vec=vec, grad1=wide_tokens, grads=halves(4 * LANES)),
        dict(pre=low_ff),
        16 * dense,
        18e6,
    )
    flow_enc = Flow(enc_ffn.grads, 2 * LANES, 2 * LANES)
    _, formed = advance("first_xy", ids, first_flows, after=[enc_ffn.vec] + final_back, weight=50)
    _, formed = advance("encoder_ffn_xy", ids, [flow_enc], after=formed)
    dec_self = self_stage(
        "decoder_self_backward",
        2,
        False,
        dec.hidden_grad,
        dec.hat2,
        dec.scale2,
        (dec.context2, dec.inverse2, dec.q2, dec.k2, dec.v2, dec.exps2),
        dec.x_t,
        1,
        dict(mask=mask_part),
        formed,
    )
    flow_dec = Flow(dec_self.grads, LANES, LANES)
    _, formed = advance("first_yx", ids, first_flows, after=[dec_self.vec], weight=50)
    _, formed = advance("decoder_self_xy", ids, [flow_dec], after=formed)
    enc_self = self_stage(
        "encoder_self_backward",
        0,
        True,
        enc_ffn.grad1,
        enc.hat0,
        enc.scale0,
        (enc.context, enc.inverse, enc.q, enc.k, enc.v, enc.exps),
        enc.x_t,
        0,
        dict(
            vec_enc=whole(enc_ffn.vec),
            vec_self=whole(dec_self.vec),
            vec_cross=whole(dec.vec_cross),
            vec_dec=whole(dec.vec),
        ),
        formed,
    )
    flow_last = Flow(enc_self.grads, LANES, LANES + 16)
    ffns, last_two = first_flows + [flow_enc], [flow_dec, flow_last]
    dec_blocks = [Piece(dec_self.input_grad, i * length, length) for i in range(count)]
    enc_blocks = [Piece(enc_self.input_grad, i * length, length) for i in range(count)]

    def sent_back(blocks):
        return [Step(channel, (blocks[i],)) for i, channel in enumerate((X, Y, DIAGONAL), 1)]

    def came_back(blocks, pieces):
        return [blocks[0]] + [piece[1] for piece in pieces]

    _, formed = advance("ffn_one", ids, ffns, after=[enc_self.input_grad], weight=50)
    _, formed = advance("last_xy", ids, [flow_last], after=formed)
    _, formed = advance("decoder_self_yx", ids, [flow_dec], after=formed)
    _, formed = advance("ffn_two", ids, ffns, after=formed)
    dec_back, formed = advance("last_yx", ids, [flow_last], sent_back(dec_blocks), after=formed)
    enc_back, formed = advance("two_pair", ids, last_two, sent_back(enc_blocks), after=formed)
    _, formed = advance("ffn_three", ids, ffns, after=formed)
    first_done = cross_cores(first_flows)
    _, formed = advance("two_pairs", ids, last_two, after=formed)
    _, formed = advance("ffn_four", ids, [flow_enc], after=formed)
    enc_done = cross_cores([flow_enc])
    half = 2 * LANES

    def ffn_targets(index):
        goals = []
        for side in (0, 1):
            for unit in (0, 1):
                j = side * 2 + unit
                goals.append((side, unit * LANES, LANES, "up", (index, slice(None), slice(j * d, (j + 1) * d))))
            goals.append((side, half, half, "down", (index, slice(side * half, (side + 1) * half))))
        return goals

    def self_targets(index):
        goals = [(0, 0, LANES, "proj", (index,))]
        for j, (side, unit) in enumerate(((0, 1), (1, 0), (1, 1))):
            goals.append((side, unit * LANES, LANES, "qkv", (index, slice(None), slice(j * d, (j + 1) * d))))
        return goals

    cross_targets = [
        (0, 0, LANES, "proj", (2,)),
        (0, LANES, LANES, "cross_q", (slice(None),)),
        (1, 0, LANES, "cross_kv", (slice(None), slice(0, d))),
        (1, LANES, LANES, "cross_kv", (slice(None), slice(d, 2 * d))),
    ]
    local_rows = (count, length, d)
    up_down = dict(up=shape_of((2, LANES, ff), WIDE), down=shape_of((2, d, d), WIDE))
    proj = shape_of((3, LANES, d), WIDE)
    first = finish_units(
        "finish_first",
        ids,
        [
            (flow_ffn.rows, flow_ffn.parts(*first_done), ffn_targets(1)),
            (flow_cross.rows, flow_cross.parts(*first_done), cross_targets),
        ],
        dict(
            final=shape_of(local_rows, LOW),
            cross_q=shape_of((LANES, d), WIDE),
            cross_kv=shape_of((LANES, 2 * d), WIDE),
            proj=proj,
            **up_down,
        ),
        {},
        [("final", [Piece(array, 0, length) for array in [dec.final[0]] + final_back])],
        after=formed,
    )
    _, formed = advance("two_back", ids, last_two, after=[first.final])
    two_done = cross_cores(last_two)
    second = finish_units(
        "finish_encoder_ffn",
        ids,
        [(flow_enc.rows, flow_enc.parts(*enc_done), ffn_targets(0))],
        dict(dec_grad=shape_of(local_rows, WIDE), **up_down),
        dict(up=first.up, down=first.down),
        [("dec_grad", came_back(dec_blocks, dec_back))],
        after=formed,
    )
    third = finish_units(
        "finish_last",
        ids,
        [
            (flow_dec.rows, flow_dec.parts(*two_done), self_targets(1)),
            (flow_last.rows, flow_last.parts(*two_done), self_targets(0)),
        ],
        dict(
            enc_grad=shape_of(local_rows, WIDE),
            gains=shape_of((5, LANES), WIDE),
            biases=shape_of((16, LANES), WIDE),
            ups=shape_of((2, d), WIDE),
            embed=shape_of((1, LANES), WIDE),
            proj=proj,
            qkv=shape_of((2, LANES, 3 * d), WIDE),
        ),
        dict(proj=first.proj),
        [("enc_grad", came_back(enc_blocks, enc_back))],
        ("gains", "biases", "ups", "embed"),
        after=[second.dec_grad],
    )
    return (
        first.final,
        third.enc_grad,
        second.dec_grad,
        third.qkv,
        third.proj,
        first.cross_q,
        first.cross_kv,
        second.up,
        second.down,
        third.gains,
        third.biases,
        third.ups,
        third.embed.reshape(LANES),
    )


def fits_by_rows(mesh, enc_input, ffn_up):
    count, length = enc_input.shape[0], enc_input.shape[1]
    return (
        mesh.shape["seq"] == 4
        and count == 4
        and mesh.shape["rows"] == 8
        and length == LANES
        and ffn_up.shape[2] == count * ffn_up.shape[1]
        and enc_input.shape[2] == HEADS * HEAD_DIM == count * LANES
    )


def device_program(mesh, *arrays):
    if fits_by_rows(mesh, arrays[0], arrays[10]):
        return by_rows(*arrays)
    return local(*arrays)


def solution(mesh):
    return jax.shard_map(
        functools.partial(device_program, mesh),
        mesh=mesh,
        in_specs=(
            P("rows", "seq", None),
            P("rows", "seq", None),
            P("rows", None),
            P("rows", None),
            P("rows", "seq"),
            P("rows", "seq", None),
            P(),
            P(),
            P(),
            P(),
            P(),
            P(),
            P(),
            P(),
            P(),
            P(),
        ),
        out_specs=(
            P("rows", "seq", None),
            P("rows", "seq", None),
            P("rows", "seq", None),
            P(None, "seq", None),
            P(None, "seq", None),
            P("seq", None),
            P("seq", None),
            P(None, "seq", None),
            P(None, "seq", None),
            P(None, "seq"),
            P(None, "seq"),
            P(None, "seq"),
            P("seq"),
        ),
        check_vma=False,
    )
```

```python
import functools
import types
import typing

import jax
import jax.numpy as jnp
from jax import lax
from jax.experimental import pallas as pl
from jax.experimental.pallas import tpu as pltpu
from jax.sharding import PartitionSpec as P

D = 512
HEADS = 8
HEAD_DIM = 64


EPSILON = 1e-05
NEG_FILL = -1000000000.0
START_FILL = -1e30


def normalize(residual, scale_gain, offset):
    centred = residual - jnp.mean(residual, axis=-1, keepdims=True)
    spread = jnp.mean(centred * centred, axis=-1, keepdims=True)
    return centred * lax.rsqrt(spread + EPSILON) * scale_gain + offset


def gelu_exact(values):
    return jax.nn.gelu(values, approximate=False)


def segments(lengths, places):
    doc_ends = jnp.cumsum(lengths, axis=1)
    return jnp.sum((doc_ends[:, None, :] <= places[None, :, None]).astype(jnp.int32), axis=2)


def project(inputs, weight):
    return jnp.einsum("rsd,df->rsf", inputs, weight, preferred_element_type=jnp.float32)


def project_back(gradient, weight):
    return jnp.einsum("rsf,df->rsd", gradient, weight, preferred_element_type=jnp.float32)


def weight_grad(inputs, gradient):
    return jnp.einsum("rsd,rsf->df", inputs, gradient, preferred_element_type=jnp.float32)


def token_sum(gradient):
    return jnp.sum(gradient, axis=(0, 1))


def split_heads(tensor):
    return tensor.reshape(tensor.shape[:2] + (HEADS, HEAD_DIM))


def split_blocks(tensor, block_size):
    new_shape = (tensor.shape[0], tensor.shape[1] // block_size, block_size) + tensor.shape[2:]
    return jnp.swapaxes(tensor.reshape(new_shape), 0, 1)


def block_scores(query_heads, key_heads, query_seg, key_seg):
    scores = jnp.einsum(
        "rqhd,rkhd->rhqk", query_heads, key_heads, preferred_element_type=jnp.float32
    ) * HEAD_DIM ** (-0.5)
    allowed = query_seg[:, None, :, None] == key_seg[:, None, None, :]
    return jnp.where(allowed, scores, NEG_FILL)


def block_grads(
    query_heads, grad_heads, log_total, delta_rows, query_seg, key_heads, value_heads, key_seg
):
    scores = block_scores(query_heads, key_heads, query_seg, key_seg)
    probs = jnp.exp(scores - log_total[..., None])
    dprobs = jnp.einsum(
        "rqhd,rkhd->rhqk", grad_heads, value_heads, preferred_element_type=jnp.float32
    )
    dscores = (probs * (dprobs - delta_rows[..., None])).astype(jnp.bfloat16)
    scaling = HEAD_DIM ** (-0.5)
    query_part = (
        jnp.einsum("rhqk,rkhd->rqhd", dscores, key_heads, preferred_element_type=jnp.float32)
        * scaling
    )
    key_part = (
        jnp.einsum("rhqk,rqhd->rkhd", dscores, query_heads, preferred_element_type=jnp.float32)
        * scaling
    )
    value_part = jnp.einsum(
        "rhqk,rqhd->rkhd",
        probs.astype(jnp.bfloat16),
        grad_heads,
        preferred_element_type=jnp.float32,
    )
    return (query_part, key_part, value_part)


def start_state(row_count, length):
    return (
        jnp.full((row_count, HEADS, length), START_FILL, jnp.float32),
        jnp.zeros((row_count, HEADS, length), jnp.float32),
        jnp.zeros((row_count, length, HEADS, HEAD_DIM), jnp.float32),
    )


def finish_state(state):
    running_max, running_sum, running_acc = state
    context = running_acc / jnp.swapaxes(running_sum, 1, 2)[..., None]
    return (
        context.reshape(context.shape[:2] + (HEADS * HEAD_DIM,)),
        running_max + jnp.log(running_sum),
    )


def absorber(query_heads, query_seg, key_lengths, length):

    def absorb(carried, piece_pair, first_pos):
        key_piece, value_piece = piece_pair
        piece_len = key_piece.shape[1]
        seg_piece = segments(key_lengths, jnp.arange(piece_len, dtype=jnp.int32))

        def advance(running, inputs):
            running_max, running_sum, running_acc = running
            key_block, value_block, seg_block = inputs
            scores = block_scores(query_heads, key_block, query_seg, seg_block)
            new_max = jnp.maximum(running_max, jnp.max(scores, axis=-1))
            factor = jnp.exp(running_max - new_max)
            exp_scores = jnp.exp(scores - new_max[..., None])
            running_sum = running_sum * factor + jnp.sum(exp_scores, axis=-1)
            running_acc = running_acc * jnp.swapaxes(factor, 1, 2)[..., None] + jnp.einsum(
                "rhqk,rkhd->rqhd",
                exp_scores.astype(jnp.bfloat16),
                value_block,
                preferred_element_type=jnp.float32,
            )
            return ((new_max, running_sum, running_acc), None)

        blocks = (
            split_blocks(split_heads(key_piece), length),
            split_blocks(split_heads(value_piece), length),
            split_blocks(seg_piece, length),
        )
        result, unused = lax.scan(advance, carried, blocks)
        return result

    return absorb


def attend_forward(queries, keys, values, query_seg, key_lengths):
    row_count, length = (queries.shape[0], queries.shape[1])
    query_heads = split_heads(queries)
    absorb = absorber(query_heads, query_seg, key_lengths, length)
    state = absorb(
        start_state(row_count, length),
        (
            lax.all_gather(keys, "seq", axis=1, tiled=True),
            lax.all_gather(values, "seq", axis=1, tiled=True),
        ),
        jnp.int32(0),
    )
    context, log_total = finish_state(state)
    return (context, log_total, None)


def attend_backward(
    queries,
    keys,
    values,
    query_seg,
    key_seg,
    query_lengths,
    key_lengths,
    context,
    log_total,
    context_grad,
):
    row_count, length = (queries.shape[0], queries.shape[1])
    grad_low = context_grad.astype(jnp.bfloat16)
    query_heads = split_heads(queries)
    grad_heads = split_heads(grad_low)
    delta_rows = jnp.swapaxes(
        jnp.sum(grad_heads.astype(jnp.float32) * split_heads(context), axis=-1), 1, 2
    )
    zero_heads = jnp.zeros((row_count, length, HEADS, HEAD_DIM), jnp.float32)
    key_piece = lax.all_gather(keys, "seq", axis=1, tiled=True)
    value_piece = lax.all_gather(values, "seq", axis=1, tiled=True)
    piece_len = key_piece.shape[1]
    block_size = length
    seg_piece = segments(key_lengths, jnp.arange(piece_len, dtype=jnp.int32))

    def advance(running, inputs):
        key_block, value_block, seg_block = inputs
        query_part, unused_keys, unused_values = block_grads(
            query_heads,
            grad_heads,
            log_total,
            delta_rows,
            query_seg,
            key_block,
            value_block,
            seg_block,
        )
        return (running + query_part, None)

    blocks = (
        split_blocks(split_heads(key_piece), block_size),
        split_blocks(split_heads(value_piece), block_size),
        split_blocks(seg_piece, block_size),
    )
    result, unused = lax.scan(advance, zero_heads, blocks)
    query_grad = result
    total_all, delta_all = (
        lax.all_gather(log_total, "seq", axis=2, tiled=True),
        lax.all_gather(delta_rows, "seq", axis=2, tiled=True),
    )
    key_heads = split_heads(keys)
    value_heads = split_heads(values)
    query_piece = lax.all_gather(queries, "seq", axis=1, tiled=True)
    grad_piece = lax.all_gather(grad_low, "seq", axis=1, tiled=True)
    piece_len = query_piece.shape[1]
    block_size = length
    seg_piece = segments(query_lengths, jnp.arange(piece_len, dtype=jnp.int32))
    offsets = jnp.arange(piece_len // block_size, dtype=jnp.int32) * block_size

    def advance(running, inputs):
        query_block, grad_block, seg_block, offset = inputs
        total_block = lax.dynamic_slice_in_dim(total_all, offset, block_size, 2)
        delta_block = lax.dynamic_slice_in_dim(delta_all, offset, block_size, 2)
        unused_query, key_part, value_part = block_grads(
            query_block,
            grad_block,
            total_block,
            delta_block,
            seg_block,
            key_heads,
            value_heads,
            key_seg,
        )
        return ((running[0] + key_part, running[1] + value_part), None)

    blocks = (
        split_blocks(split_heads(query_piece), block_size),
        split_blocks(split_heads(grad_piece), block_size),
        split_blocks(seg_piece, block_size),
        offsets,
    )
    result, unused = lax.scan(advance, (zero_heads, zero_heads), blocks)
    key_grad, value_grad = result
    return (
        query_grad.reshape(queries.shape),
        key_grad.reshape(queries.shape),
        value_grad.reshape(queries.shape),
    )


def self_forward(inputs_low, w_qkv, bias_q, bias_v, segment, lengths):
    projected = project(inputs_low, w_qkv)
    queries = (projected[..., :D] + bias_q).astype(jnp.bfloat16)
    keys = projected[..., D : 2 * D].astype(jnp.bfloat16)
    values = (projected[..., 2 * D :] + bias_v).astype(jnp.bfloat16)
    context, log_total, stored = attend_forward(queries, keys, values, segment, lengths)
    return (queries, keys, values, context, log_total, stored)


def ffn_forward(hidden, w_up, bias_up, w_down, bias_down):
    hidden_low = hidden.astype(jnp.bfloat16)
    pre_act = project(hidden_low, w_up) + bias_up
    activated, act_back = jax.vjp(gelu_exact, pre_act)
    act_low = activated.astype(jnp.bfloat16)
    return (project(act_low, w_down) + bias_down, (hidden_low, act_low, act_back))


def ffn_backward(out_grad, stored, w_up, w_down):
    hidden_low, act_low, act_back = stored
    out_low = out_grad.astype(jnp.bfloat16)
    down_grad = weight_grad(act_low, out_low)
    (pre_grad,) = act_back(project_back(out_low, w_down))
    pre_low = pre_grad.astype(jnp.bfloat16)
    up_grad = weight_grad(hidden_low, pre_low)
    return (
        project_back(pre_low, w_up),
        up_grad,
        token_sum(pre_grad),
        down_grad,
        token_sum(out_grad),
    )


def local(
    enc_input,
    dec_input,
    src_lengths,
    tgt_lengths,
    masked,
    cotangent,
    self_qkv,
    attn_out,
    cross_q,
    cross_kv,
    ffn_up,
    ffn_down,
    norm_gain,
    biases,
    up_bias,
    mask_embed,
):
    length = enc_input.shape[1]
    places = lax.axis_index("seq") * length + jnp.arange(length, dtype=jnp.int32)
    src_seg = segments(src_lengths, places)
    tgt_seg = segments(tgt_lengths, places)
    mask_float = masked.astype(jnp.float32)[..., None]
    enc_queries, enc_keys, enc_values, enc_context, enc_total, enc_stored = self_forward(
        enc_input, self_qkv[0], biases[0], biases[1], src_seg, src_lengths
    )
    enc_ctx_low = enc_context.astype(jnp.bfloat16)
    enc_resid = enc_input.astype(jnp.float32) + project(enc_ctx_low, attn_out[0]) + biases[2]
    enc_hidden, enc_norm_back = jax.vjp(normalize, enc_resid, norm_gain[0], biases[11])
    enc_ffn, enc_kept = ffn_forward(enc_hidden, ffn_up[0], up_bias[0], ffn_down[0], biases[3])
    memory, memory_back = jax.vjp(normalize, enc_hidden + enc_ffn, norm_gain[1], biases[12])
    memory_low = memory.astype(jnp.bfloat16)
    dec_inputs = dec_input.astype(jnp.float32) + mask_float * mask_embed
    dec_low = dec_inputs.astype(jnp.bfloat16)
    dec_queries, dec_keys, dec_values, dec_context, dec_total, dec_stored = self_forward(
        dec_low, self_qkv[1], biases[4], biases[5], tgt_seg, tgt_lengths
    )
    dec_ctx_low = dec_context.astype(jnp.bfloat16)
    dec_hidden, dec_norm_back = jax.vjp(
        normalize,
        dec_inputs + project(dec_ctx_low, attn_out[1]) + biases[6],
        norm_gain[2],
        biases[13],
    )
    dec_hidden_low = dec_hidden.astype(jnp.bfloat16)
    cross_queries = (project(dec_hidden_low, cross_q) + biases[7]).astype(jnp.bfloat16)
    cross_pair = project(memory_low, cross_kv)
    cross_keys = cross_pair[..., :D].astype(jnp.bfloat16)
    cross_values = (cross_pair[..., D:] + biases[8]).astype(jnp.bfloat16)
    cross_context, cross_total, cross_stored = attend_forward(
        cross_queries, cross_keys, cross_values, tgt_seg, src_lengths
    )
    cross_ctx_low = cross_context.astype(jnp.bfloat16)
    cross_hidden, cross_norm_back = jax.vjp(
        normalize,
        dec_hidden + project(cross_ctx_low, attn_out[2]) + biases[9],
        norm_gain[3],
        biases[14],
    )
    last_ffn, last_kept = ffn_forward(cross_hidden, ffn_up[1], up_bias[1], ffn_down[1], biases[10])
    final, final_back = jax.vjp(normalize, cross_hidden + last_ffn, norm_gain[4], biases[15])
    final_grad, gain_four, shift_four = final_back(cotangent.astype(jnp.float32))
    into_cross, up_grad_one, upb_grad_one, down_grad_one, bias_ten = ffn_backward(
        final_grad, last_kept, ffn_up[1], ffn_down[1]
    )
    cross_resid_grad, gain_three, shift_three = cross_norm_back(final_grad + into_cross)
    cross_out_low = cross_resid_grad.astype(jnp.bfloat16)
    out_grad_two = weight_grad(cross_ctx_low, cross_out_low)
    cross_q_part, cross_k_part, cross_v_part = attend_backward(
        cross_queries,
        cross_keys,
        cross_values,
        tgt_seg,
        src_seg,
        tgt_lengths,
        src_lengths,
        cross_context,
        cross_total,
        project_back(cross_out_low, attn_out[2]),
    )
    cross_q_low = cross_q_part.astype(jnp.bfloat16)
    cross_kv_low = jnp.concatenate([cross_k_part, cross_v_part], axis=-1).astype(jnp.bfloat16)
    cross_q_weight = weight_grad(dec_hidden_low, cross_q_low)
    cross_kv_weight = weight_grad(memory_low, cross_kv_low)
    memory_grad = project_back(cross_kv_low, cross_kv)
    dec_resid_grad, gain_two, shift_two = dec_norm_back(
        cross_resid_grad + project_back(cross_q_low, cross_q)
    )
    dec_out_low = dec_resid_grad.astype(jnp.bfloat16)
    out_grad_one = weight_grad(dec_ctx_low, dec_out_low)
    dec_q_part, dec_k_part, dec_v_part = attend_backward(
        dec_queries,
        dec_keys,
        dec_values,
        tgt_seg,
        tgt_seg,
        tgt_lengths,
        tgt_lengths,
        dec_context,
        dec_total,
        project_back(dec_out_low, attn_out[1]),
    )
    dec_qkv_low = jnp.concatenate([dec_q_part, dec_k_part, dec_v_part], axis=-1).astype(
        jnp.bfloat16
    )
    qkv_grad_one = weight_grad(dec_low, dec_qkv_low)
    dec_input_grad = dec_resid_grad + project_back(dec_qkv_low, self_qkv[1])
    mask_grad = jnp.sum(dec_input_grad * mask_float, axis=(0, 1))
    memory_resid_grad, gain_one, shift_one = memory_back(memory_grad)
    into_enc, up_grad_zero, upb_grad_zero, down_grad_zero, bias_three = ffn_backward(
        memory_resid_grad, enc_kept, ffn_up[0], ffn_down[0]
    )
    enc_resid_grad, gain_zero, shift_zero = enc_norm_back(memory_resid_grad + into_enc)
    enc_out_low = enc_resid_grad.astype(jnp.bfloat16)
    out_grad_zero = weight_grad(enc_ctx_low, enc_out_low)
    enc_q_part, enc_k_part, enc_v_part = attend_backward(
        enc_queries,
        enc_keys,
        enc_values,
        src_seg,
        src_seg,
        src_lengths,
        src_lengths,
        enc_context,
        enc_total,
        project_back(enc_out_low, attn_out[0]),
    )
    enc_qkv_low = jnp.concatenate([enc_q_part, enc_k_part, enc_v_part], axis=-1).astype(
        jnp.bfloat16
    )
    qkv_grad_zero = weight_grad(enc_input, enc_qkv_low)
    enc_input_grad = enc_resid_grad + project_back(enc_qkv_low, self_qkv[0])
    bias_rows = jnp.stack(
        [
            token_sum(enc_q_part),
            token_sum(enc_v_part),
            token_sum(enc_resid_grad),
            bias_three,
            token_sum(dec_q_part),
            token_sum(dec_v_part),
            token_sum(dec_resid_grad),
            token_sum(cross_q_part),
            token_sum(cross_v_part),
            token_sum(cross_resid_grad),
            bias_ten,
            shift_zero,
            shift_one,
            shift_two,
            shift_three,
            shift_four,
        ]
    )
    shares = (
        lax.psum_scatter(
            jnp.stack([qkv_grad_zero, qkv_grad_one]), "seq", scatter_dimension=1, tiled=True
        ),
        lax.psum_scatter(
            jnp.stack([out_grad_zero, out_grad_one, out_grad_two]),
            "seq",
            scatter_dimension=1,
            tiled=True,
        ),
        lax.psum_scatter(cross_q_weight, "seq", scatter_dimension=0, tiled=True),
        lax.psum_scatter(cross_kv_weight, "seq", scatter_dimension=0, tiled=True),
        lax.psum_scatter(
            jnp.stack([up_grad_zero, up_grad_one]), "seq", scatter_dimension=1, tiled=True
        ),
        lax.psum_scatter(
            jnp.stack([down_grad_zero, down_grad_one]), "seq", scatter_dimension=1, tiled=True
        ),
        lax.psum_scatter(
            jnp.stack([gain_zero, gain_one, gain_two, gain_three, gain_four]),
            "seq",
            scatter_dimension=1,
            tiled=True,
        ),
        lax.psum_scatter(bias_rows, "seq", scatter_dimension=1, tiled=True),
        lax.psum_scatter(
            jnp.stack([upb_grad_zero, upb_grad_one]), "seq", scatter_dimension=1, tiled=True
        ),
        lax.psum_scatter(mask_grad, "seq", scatter_dimension=0, tiled=True),
    )
    totals = lax.psum(
        (
            shares[0],
            shares[1],
            shares[2],
            shares[3],
            shares[4],
            shares[5],
            shares[6],
            shares[7],
            shares[8],
            shares[9],
        ),
        "rows",
    )
    return (
        final.astype(jnp.bfloat16),
        enc_input_grad,
        dec_input_grad,
        totals[0],
        totals[1],
        totals[2],
        totals[3],
        totals[4],
        totals[5],
        totals[6],
        totals[7],
        totals[8],
        totals[9],
    )


LANES = 128
CHANNELS = 96
COST = 50
MIX_COST = 4e9
BIG_WEIGHT = 2e11 / MIX_COST
BIG_VMEM = 64 * 2**20
LOW = jnp.bfloat16
WIDE = jnp.float32
HBM = pl.BlockSpec(memory_space=pltpu.HBM)
SMEM = pl.BlockSpec(memory_space=pltpu.SMEM)


def shape_of(dims, dtype):
    return jax.ShapeDtypeStruct(tuple(dims), dtype)


def distinct(arrays):
    found = []
    for array in arrays:
        if not any(array is other for other in found):
            found.append(array)
    return found


def where_in(arrays, array):
    return [other is array for other in arrays].index(True)


def parameters():
    return pltpu.CompilerParams(vmem_limit_bytes=BIG_VMEM)


def cost(flops, moved):
    return pl.CostEstimate(flops=int(flops), bytes_accessed=int(moved), transcendentals=0)


class Copies:
    def __init__(self, sems):
        self.sems, self.used, self.leaving = sems, 0, []

    def start(self, source, target):
        moved = pltpu.make_async_copy(source, target, self.sems.at[self.used])
        self.used += 1
        moved.start()
        return moved

    def leave(self, source, target):
        self.leaving.append(self.start(source, target))

    def finish(self):
        for moved in self.leaving:
            moved.wait()


class Arrivals:
    def __init__(self, copies, refs, groups):
        self._copies, self._refs, self._groups, self._coming = copies, refs, groups, {}
        self.more()

    def more(self):
        for name, origin, target in self._groups.pop(0) if self._groups else ():
            self._coming.setdefault(name, []).append(self._copies.start(origin, target))

    def finish(self):
        while self._groups:
            self.more()
        for name in self._refs:
            getattr(self, name)

    def __getattr__(self, name):
        while name not in self._coming and any(name == move[0] for group in self._groups for move in group):
            self.more()
        for moved in self._coming.get(name, ()):
            moved.wait()
        self._coming[name] = []
        return self._refs[name]


class Stage(typing.NamedTuple):
    scalars: typing.Any
    use: typing.Any
    out: typing.Any
    work: typing.Any
    copies: typing.Any
    targets: typing.Any

    def push(self, *buffers):
        for buffer in buffers:
            self.push_part(buffer, ())

    def push_part(self, buffer, index):
        target = [result for ref, result in self.targets if ref is buffer][0]
        if isinstance(target, list):
            self.copies.leave(buffer.at[index], target[index[0]].at[index[1:]] if index[1:] else target[index[0]])
        else:
            self.copies.leave(buffer.at[index] if index else buffer, target.at[index] if index else target)


def run_stage(name, body, scalars, parts, outs, work, flops, moved, after=()):
    all_parts = {key: part for group in parts for key, part in group.items()}
    arrays = distinct([move[0] for part in all_parts.values() for move in part[2]])
    after = [array for array in distinct(after) if not any(array is other for other in arrays)]
    flat_outs, spots = [], {}
    for key, shape in outs.items():
        several = shape if isinstance(shape, list) else [shape]
        spots[key] = (len(flat_outs), len(several))
        flat_outs += several
    buffers = [shape_of((len(s),) + s[0].shape, s[0].dtype) if isinstance(s, list) else s for s in outs.values()]

    def kernel(*refs):
        refs = list(refs)

        def take(count):
            taken = refs[:count]
            del refs[:count]
            return taken

        scalar_refs = types.SimpleNamespace(**dict(zip(scalars, take(len(scalars)))))
        inputs = take(len(arrays))
        take(len(after))
        results = take(len(flat_outs))
        part_refs = dict(zip(all_parts, take(len(all_parts))))
        out_refs = dict(zip(outs, take(len(outs))))
        work_refs = dict(zip(work, take(len(work))))
        copies = Copies(refs[0])
        groups = []
        for wanted in parts:
            groups.append([])
            for key, part in wanted.items():
                for array, source, target in part[2]:
                    origin, place = inputs[where_in(arrays, array)], part_refs[key]
                    origin = origin if source is None else origin.at[source(scalar_refs)]
                    groups[-1].append((key, origin, place if target is None else place.at[target]))
        targets = []
        for key, (start, count) in spots.items():
            several = isinstance(outs[key], list)
            targets.append((out_refs[key], list(results[start : start + count]) if several else results[start]))
        use = Arrivals(copies, part_refs, groups)
        stage = Stage(
            scalar_refs, use, types.SimpleNamespace(**out_refs), types.SimpleNamespace(**work_refs), copies, targets
        )
        body(stage)
        use.finish()
        copies.finish()

    given = pl.pallas_call(
        kernel,
        name=name,
        out_shape=flat_outs,
        in_specs=[SMEM] * len(scalars) + [HBM] * (len(arrays) + len(after)),
        out_specs=[HBM] * len(flat_outs),
        scratch_shapes=[pltpu.VMEM(part[0], part[1]) for part in all_parts.values()]
        + [pltpu.VMEM(each.shape, each.dtype) for each in buffers]
        + [pltpu.VMEM(each.shape, each.dtype) for each in work.values()]
        + [pltpu.SemaphoreType.DMA((CHANNELS,))],
        compiler_params=parameters(),
        cost_estimate=cost(flops * COST, moved),
    )(*scalars.values(), *arrays, *after)
    found = {}
    for key, (start, count) in spots.items():
        found[key] = list(given[start : start + count]) if isinstance(outs[key], list) else given[start]
    return types.SimpleNamespace(**found)


def whole(array):
    return (tuple(array.shape), array.dtype, [(array, None, None)])


def layer(array, index):
    return (tuple(array.shape[1:]), array.dtype, [(array, lambda s: index, None)])


def dot_nn(a, b):
    return lax.dot_general(a, b, (((1,), (0,)), ((), ())), preferred_element_type=WIDE)


def dot_nt(a, b):
    return lax.dot_general(a, b, (((1,), (1,)), ((), ())), preferred_element_type=WIDE)


def dot_tn(a, b):
    return lax.dot_general(a, b, (((0,), (0,)), ((), ())), preferred_element_type=WIDE)


def total(values):
    return jnp.sum(values, axis=0, keepdims=True)


def norm_parts(residual):
    centred = residual - jnp.mean(residual, axis=-1, keepdims=True)
    scale = lax.rsqrt(jnp.mean(centred * centred, axis=-1, keepdims=True) + EPSILON)
    return centred * scale, scale


def norm_keep(stage, residual, gain, shift, hat_ref, scale_ref):
    hat, scale = norm_parts(residual)
    hat_ref[...] = hat.astype(LOW)
    scale_ref[...] = jnp.broadcast_to(scale, scale_ref.shape)
    stage.push(hat_ref, scale_ref)
    return hat * gain + shift


def norm_back(grad, hat, scale, gain):
    scaled = grad * gain
    inner = jnp.mean(scaled, axis=-1, keepdims=True)
    along = jnp.mean(scaled * hat, axis=-1, keepdims=True)
    return scale * (scaled - inner - hat * along), total(grad * hat), total(grad)


def segment_ids(lengths_ref, row, places):
    end = jnp.int32(0)
    found = jnp.zeros(places.shape, jnp.int32)
    for slot in range(lengths_ref.shape[1]):
        end = end + lengths_ref[row, slot]
        found = found + (end <= places).astype(jnp.int32)
    return found


def positions(me, length, shape, axis):
    token = lax.broadcasted_iota(jnp.int32, shape, axis)
    bits = length.bit_length() - 1
    block = lax.shift_right_logical(token, jnp.int32(bits))
    return lax.shift_left(jnp.bitwise_xor(block, me), jnp.int32(bits)) + jnp.bitwise_and(token, length - 1)


def fill_bias(bias_ref, query_lengths, key_lengths, me, length):
    tokens = bias_ref.shape[0]
    query_seg = segment_ids(query_lengths, me, positions(me, length, (1, tokens), 1))
    key_seg = segment_ids(key_lengths, me, positions(me, length, (tokens, 1), 0))
    bias_ref[...] = jnp.where(key_seg == query_seg, 0.0, NEG_FILL)


def heads_of(values):
    return values.reshape(HEADS, HEAD_DIM, values.shape[-1])


def flat(ref):
    return ref[...].reshape(HEADS * HEAD_DIM, ref.shape[-1])


def attention_forward(q_ref, k_ref, v_ref, bias_ref, exp_ref, inverse_ref, context_ref):
    for head in range(HEADS):
        scores = dot_tn(k_ref[head], q_ref[head]) + bias_ref[...]
        peak = jnp.max(scores, axis=0, keepdims=True)
        exps = jnp.exp(scores - peak)
        inverse = 1.0 / jnp.sum(exps, axis=0, keepdims=True)
        low_exps = exps.astype(LOW)
        exp_ref[head] = low_exps
        inverse_ref[head] = jnp.broadcast_to(inverse, inverse_ref.shape[1:])
        context_ref[head] = (dot_nn(v_ref[head], low_exps) * inverse).astype(LOW)


def attention_backward(q_ref, k_ref, v_ref, exp_ref, inverse_ref, context_ref, work):
    for head in range(HEADS):
        exps = exp_ref[head]
        grad = (work.context_grad[head].astype(LOW).astype(WIDE) * inverse_ref[head][0:1]).astype(LOW)
        delta = total(grad.astype(WIDE) * context_ref[head].astype(WIDE))
        score_grad = (exps.astype(WIDE) * (dot_tn(v_ref[head], grad) - delta)).astype(LOW)
        dv = dot_nt(grad, exps)
        dq = dot_nn(k_ref[head], score_grad) * HEAD_DIM ** (-0.5)
        work.dv[head] = dv.astype(LOW)
        work.dk[head] = dot_nt(q_ref[head], score_grad).astype(LOW)
        work.dq[head] = dq.astype(LOW)
        wide = (HEAD_DIM, LANES)
        work.sums[0, head] = jnp.broadcast_to(jnp.sum(dq, axis=1, keepdims=True), wide)
        work.sums[1, head] = jnp.broadcast_to(jnp.sum(dv, axis=1, keepdims=True), wide)


def sum_row(sums_ref, which):
    return jnp.transpose(sums_ref[which].reshape(HEADS * HEAD_DIM, LANES))[0:1]


def qkv_forward(stage, weight, low_t, bias_t, q_col, v_col, q_ref, k_ref, v_ref):
    d = low_t.shape[0]
    queries = (dot_tn(weight[:, 0:d], low_t) + bias_t[:, q_col : q_col + 1]).astype(LOW)
    q_ref[...] = heads_of(queries * HEAD_DIM ** (-0.5))
    k_ref[...] = heads_of(dot_tn(weight[:, d : 2 * d], low_t).astype(LOW))
    v_ref[...] = heads_of((dot_tn(weight[:, 2 * d :], low_t) + bias_t[:, v_col : v_col + 1]).astype(LOW))
    stage.push(q_ref, k_ref, v_ref)


def gelu_parts(pre):
    half = 0.5 * (1.0 + lax.erf(pre * 0.5**0.5))
    density = jnp.exp(pre * pre * -0.5) * (0.5 / 3.141592653589793) ** 0.5
    return pre * half, half + pre * density


def feed_forward(low, up, up_bias, down, act_ref, slope_ref):
    width = low.shape[1]
    for j in range(act_ref.shape[1] // width):
        cols = slice(j * width, (j + 1) * width)
        act, slope = gelu_parts(dot_nn(low, up[:, cols]) + up_bias[:, cols])
        act_ref[:, cols] = act.astype(LOW)
        slope_ref[:, cols] = slope.astype(LOW)
    return dot_nn(act_ref[...], down[...])


class Halves(typing.NamedTuple):
    ref: typing.Any
    first: int
    rest: int
    me: typing.Any
    core: typing.Any
    stage: typing.Any

    def leave_regions(self, start, rows):
        for side in (0, 1):
            for begin in (start, start + 2 * (self.first + self.rest)):
                self.stage.push_part(self.ref, (side, slice(begin, begin + rows)))

    def leave_first(self, rows):
        self.leave_regions(0, 2 * self.first)

    def leave_rest(self, rows):
        self.leave_regions(2 * self.first, 2 * self.rest)

    def put(self, half, chunk, start, rows):
        away = jnp.bitwise_xor(self.me, chunk)
        low, high = jnp.bitwise_and(away, 1), lax.shift_right_logical(away, 1)
        both = 2 * (self.first + self.rest)
        if start < self.first:
            place = high * self.first + jnp.where(low == 1, 0, both) + start
        else:
            place = low * self.rest + jnp.where(high == 1, 0, both) + 2 * self.first + start - self.first
        side = jnp.bitwise_xor(self.core, half)
        self.ref[side, pl.ds(pl.multiple_of(place, 16), rows.shape[0])] = rows.astype(LOW)


def put_units(grads, block, half, unit):
    rows = LANES
    for chunk in range(block.shape[0] // rows):
        grads.put(half, chunk, unit * rows, block[chunk * rows : (chunk + 1) * rows])


def feed_back(out_grad, low, act, slope, up, down, vec_ref, vec_row, grads, pre_ref, more=None):
    width = out_grad.shape[1]
    half = width // 2
    out_low = out_grad.astype(LOW)
    columns = [slice(j * width, (j + 1) * width) for j in range(pre_ref.shape[1] // width)]
    for j, cols in enumerate(columns):
        pre = dot_nt(out_low, down[cols, :]) * slope[:, cols].astype(WIDE)
        vec_ref[vec_row + j : vec_row + j + 1, :] = total(pre)
        pre_ref[:, cols] = pre.astype(LOW)
        down_grad = dot_tn(act[:, cols], out_low)
        for r in range(2):
            grads.put(r, j, half, down_grad[r * half : (r + 1) * half])
    grads.leave_rest(half)
    low, up = low(), up()
    for j, cols in enumerate(columns):
        put_units(grads, dot_tn(low[...], pre_ref[:, cols]), j // 2, j % 2)
    grads.leave_first(half)
    return dot_nt(pre_ref[...], up[...])


def own_row(s):
    return s.ids[0]


def token_pieces(local, others, length, start=0):
    pieces = [(local, own_row, (slice(0, length),))]
    for d, array in enumerate(others, 1):
        pieces.append((array, lambda s: (slice(start, start + length),), (slice(d * length, (d + 1) * length),)))
    return pieces


def put_blocks(ref, values):
    for i in range(ref.shape[0]):
        ref[i] = values[i * ref.shape[1] : (i + 1) * ref.shape[1]]


def encoder_forward(length, stage):
    me, use, out = stage.scalars.ids[0], stage.use, stage.out
    fill_bias(stage.work.bias, stage.scalars.src, stage.scalars.src, me, length)
    x = use.x[...]
    x_t = jnp.transpose(x)
    out.x_t[...] = x_t
    stage.push(out.x_t)
    biases = use.biases[...]
    qkv = use.qkv
    use.more()
    qkv_forward(stage, qkv, x_t, jnp.transpose(biases), 0, 1, out.q, out.k, out.v)
    attention_forward(out.q, out.k, out.v, stage.work.bias, out.exps, out.inverse, out.context)
    stage.push(out.exps, out.inverse, out.context)
    gains = use.gains
    residual = x.astype(WIDE) + dot_tn(flat(out.context), use.proj[...]) + biases[2:3]
    hidden = norm_keep(stage, residual, gains[0:1], biases[11:12], out.hat0, out.scale0)
    hidden_low = hidden.astype(LOW)
    out.low1[...] = hidden_low
    stage.push(out.low1)
    ffn = feed_forward(hidden_low, use.up, use.up_bias[0:1], use.down, out.act1, out.slope1)
    stage.push(out.act1, out.slope1)
    memory = norm_keep(stage, hidden + ffn + biases[3:4], gains[1:2], biases[12:13], out.hat1, out.scale1)
    out.memory_t[...] = jnp.transpose(memory.astype(LOW))
    stage.push(out.memory_t)


def mask_columns(mask, d):
    row = jnp.concatenate([mask[i][0:1, 0:LANES].astype(WIDE) for i in range(mask.shape[0])], axis=1)
    columns = jnp.transpose(jnp.broadcast_to(row, (LANES, row.shape[1])))
    return jnp.concatenate([columns] * (d // LANES), axis=1)


def decoder(length, stage):
    me, use, out, work = stage.scalars.ids[0], stage.use, stage.out, stage.work
    biases = use.biases[...]
    bias_t = jnp.transpose(biases)
    gains = use.gains
    src, tgt = stage.scalars.src, stage.scalars.tgt
    fill_bias(work.bias, tgt, tgt, me, length)
    x = use.x[...].astype(WIDE)
    d = x.shape[1]
    y = x + mask_columns(use.mask, d) * use.embed[...]
    y_t = jnp.transpose(y.astype(LOW))
    out.x_t[...] = y_t
    stage.push(out.x_t)
    qkv = use.qkv
    use.more()
    qkv_forward(stage, qkv, y_t, bias_t, 4, 5, out.q2, out.k2, out.v2)
    use.more()
    attention_forward(out.q2, out.k2, out.v2, work.bias, out.exps2, out.inverse2, out.context2)
    stage.push(out.exps2, out.inverse2, out.context2)
    residual = y + dot_tn(flat(out.context2), use.proj1[...]) + biases[6:7]
    hidden = norm_keep(stage, residual, gains[2:3], biases[13:14], out.hat2, out.scale2)
    hidden_t = jnp.transpose(hidden.astype(LOW))
    work.hidden_t[...] = hidden_t
    queries = (dot_tn(use.cross_q[...], hidden_t) + bias_t[:, 7:8]).astype(LOW)
    work.q[...] = heads_of(queries * HEAD_DIM ** (-0.5))
    memory_t = use.memory_t
    kv = use.cross_kv
    work.k[...] = heads_of(dot_tn(kv[:, 0:d], memory_t[...]).astype(LOW))
    work.v[...] = heads_of((dot_tn(kv[:, d:], memory_t[...]) + bias_t[:, 8:9]).astype(LOW))
    fill_bias(work.bias, tgt, src, me, length)
    attention_forward(work.q, work.k, work.v, work.bias, work.exps, work.inverse, work.context)
    proj = use.proj2
    residual = hidden + dot_tn(flat(work.context), proj[...]) + biases[9:10]
    hat, scale = norm_parts(residual)
    work.hat[...] = hat
    work.scale[...] = jnp.broadcast_to(scale, work.scale.shape)
    hidden = hat * gains[3:4] + biases[14:15]
    work.low[...] = hidden.astype(LOW)
    up, down = use.up, use.down
    ffn = feed_forward(work.low[...], up, use.up_bias[1:2], down, work.act, work.slope)
    hat, scale = norm_parts(hidden + ffn + biases[10:11])
    put_blocks(out.final, (hat * gains[4:5] + biases[15:16]).astype(LOW))
    for i in range(out.final.shape[0]):
        stage.push_part(out.final, (i,))
    vec, vec_cross = out.vec, out.vec_cross
    vec[...] = jnp.zeros_like(vec)
    vec_cross[...] = jnp.zeros_like(vec_cross)
    cotangent = use.cotangent[...].astype(WIDE)
    grad, vec[0:1, :], vec[1:2, :] = norm_back(cotangent, hat, scale, gains[4:5])
    vec[2:3, :] = total(grad)
    into = feed_back(
        grad,
        lambda: work.low,
        work.act,
        work.slope,
        lambda: up,
        down,
        vec,
        3,
        Halves(out.grads, 2 * LANES, 2 * LANES, me, stage.scalars.ids[1], stage),
        work.pre,
    )
    stage.push(vec)
    grads = Halves(out.grads_cross, LANES, LANES, me, stage.scalars.ids[1], stage)
    grad = out_backward(
        grad + into, work.hat[...], work.scale[:, 0:1], gains[3:4], proj, work.context, work, vec_cross, grads
    )
    attention_backward(work.q, work.k, work.v, work.exps, work.inverse, work.context, work)
    dq, dk, dv = attention_sums(work, vec_cross)
    stage.push(vec_cross)
    put_units(grads, dot_nt(work.hidden_t[...], dq), 0, 1)
    put_units(grads, dot_nt(memory_t[...], dk), 1, 0)
    put_units(grads, dot_nt(memory_t[...], dv), 1, 1)
    grads.leave_first(0)
    grads.leave_rest(0)
    out.memory_grad[...] = jnp.transpose(dot_nn(kv[:, 0:d], dk) + dot_nn(kv[:, d:], dv))
    stage.push(out.memory_grad)
    out.hidden_grad[...] = grad + jnp.transpose(dot_nn(use.cross_q[...], dq))
    stage.push(out.hidden_grad)


def out_backward(grad, hat, scale, gain, proj, context, work, vec, grads):
    grad, vec[0:1, :], vec[1:2, :] = norm_back(grad, hat, scale, gain)
    vec[2:3, :] = total(grad)
    low = grad.astype(LOW)
    work.context_grad[...] = heads_of(dot_nt(proj[...], low))
    put_units(grads, dot_nn(flat(context), low), 0, 0)
    return grad


def attention_sums(work, vec):
    vec[3:4, :] = sum_row(work.sums, 0)
    vec[4:5, :] = sum_row(work.sums, 1)
    return flat(work.dq), flat(work.dk), flat(work.dv)


def encoder_ffn_backward(stage):
    me, core = stage.scalars.ids[0], stage.scalars.ids[1]
    use, out = stage.use, stage.out
    vec = out.vec
    vec[...] = jnp.zeros_like(vec)
    hat, scale, grad = use.hat, use.scale, use.grad
    use.more()
    hat, scale = hat[...].astype(WIDE), scale[...][:, 0:1]
    grad, vec[0:1, :], vec[1:2, :] = norm_back(grad[...], hat, scale, use.gains[1:2])
    vec[2:3, :] = total(grad)
    grads = Halves(out.grads, 2 * LANES, 2 * LANES, me, core, stage)
    down, slope, act = use.down, use.slope, use.act
    use.more()
    into = feed_back(
        grad, lambda: use.low, act, slope, lambda: use.up, down, vec, 3, grads, stage.work.pre
    )
    stage.push(vec)
    out.grad1[...] = grad + into
    stage.push(out.grad1)


def put_vectors(grads, start, own, others):
    d = own.shape[1]
    for chunk in range(d // LANES):
        cols = slice(chunk * LANES, (chunk + 1) * LANES)
        first = jnp.concatenate([own[:, cols]] + [each[:, cols] for each in others[:3]], axis=1)
        first = jnp.concatenate([first, jnp.zeros_like(first)], axis=0)
        second = jnp.concatenate([others[3][:, cols], jnp.zeros((8, d - LANES), WIDE)], axis=1)
        ups = [each[3 + chunk : 4 + chunk] for each in (others[0], others[3])]
        second = jnp.concatenate([second] + ups + [jnp.zeros((6, d), WIDE)], axis=0)
        grads.put(0, chunk, start, first)
        grads.put(1, chunk, start, second)


def self_backward(norm_row, last, stage):
    me, core = stage.scalars.ids[0], stage.scalars.ids[1]
    use, out, work = stage.use, stage.out, stage.work
    vec = work.vec
    grads = Halves(out.grads, LANES, LANES + (16 if last else 0), me, core, stage)
    vec[...] = jnp.zeros_like(vec)
    hat, scale, grad, proj, context = use.hat, use.scale, use.grad, use.proj, use.context
    use.more()
    hat, scale = hat[...].astype(WIDE), scale[...][:, 0:1]
    gain = use.gains[norm_row : norm_row + 1]
    grad = out_backward(grad[...], hat, scale, gain, proj, context, work, vec, grads)
    q, k, v, exps, inverse = use.q, use.k, use.v, use.exps, use.inverse
    use.more()
    attention_backward(q, k, v, exps, inverse, context, work)
    dq, dk, dv = attention_sums(work, vec)
    x_t = use.x_t[...]
    put_units(grads, dot_nt(x_t, dk), 1, 0)
    grads.leave_first(0)
    put_units(grads, dot_nt(x_t, dq), 0, 1)
    put_units(grads, dot_nt(x_t, dv), 1, 1)
    if last:
        others = [each[...] for each in (use.vec_enc, use.vec_self, use.vec_cross, use.vec_dec)]
        put_vectors(grads, 2 * LANES, vec[...], others)
    grads.leave_rest(0)
    qkv = use.qkv
    d = x_t.shape[0]
    through = dot_nn(qkv[:, 0:d], dq) + dot_nn(qkv[:, d : 2 * d], dk) + dot_nn(qkv[:, 2 * d :], dv)
    input_grad = grad + jnp.transpose(through)
    if not last:
        vec[5:6, :] = total(input_grad * mask_columns(use.mask, d))
        out.vec[...] = vec[...]
        stage.push(out.vec)
    out.input_grad[...] = input_grad.astype(LOW)
    stage.push(out.input_grad)


def swap(array, axis_name, bit):
    size = lax.axis_size(axis_name)
    return lax.ppermute(array, axis_name, [(i, i ^ bit) for i in range(size)])


def spread_rows(local, me):
    return [
        swap(lax.dynamic_index_in_dim(local, me ^ d, 0, keepdims=False), "seq", d) for d in range(1, local.shape[0])
    ]


def pack_rows(ids, dec_input, cotangent, masked):
    count, length, d = dec_input.shape
    rows = 2 * length + 16

    def kernel(ids_ref, mask_ref, dec_ref, cot_ref, *refs):
        results, scratch, copies = refs[:count], refs[count], Copies(refs[count + 1])
        me = ids_ref[0]
        coming = []
        for away in range(1, count):
            row = jnp.bitwise_xor(me, away)
            coming.append(copies.start(dec_ref.at[row], scratch.at[away, 0:length]))
            coming.append(copies.start(cot_ref.at[row], scratch.at[away, length : 2 * length]))
        for away in range(count):
            row = mask_ref[jnp.bitwise_xor(me, away)].astype(WIDE).astype(LOW)
            row = jnp.concatenate([jnp.broadcast_to(row, (16, length))] * (d // length), axis=1)
            scratch[away, 2 * length : rows] = row
        copies.leave(scratch.at[0, 2 * length : rows], results[0])
        for away in range(1, count):
            coming[2 * away - 2].wait()
            coming[2 * away - 1].wait()
            copies.leave(scratch.at[away], results[away])
        copies.finish()

    return pl.pallas_call(
        kernel,
        name="pack_rows",
        out_shape=[shape_of((16, d), LOW)] + [shape_of((rows, d), LOW)] * (count - 1),
        in_specs=[SMEM, pl.BlockSpec(memory_space=pltpu.VMEM), HBM, HBM],
        out_specs=[HBM] * count,
        scratch_shapes=[pltpu.VMEM((count, rows, d), LOW), pltpu.SemaphoreType.DMA((3 * count,))],
        compiler_params=parameters(),
        cost_estimate=cost(0, 2e6),
    )(ids, masked.reshape(count, 1, length), dec_input, cotangent)


class Piece(typing.NamedTuple):
    array: typing.Any
    start: int
    rows: int
    half: int = -1

    def halved(self, half):
        return self._replace(half=half)

    @property
    def lanes(self):
        width = self.array.shape[-1]
        return width if self.half < 0 else width // 2

    def origin(self, ref, place):
        if self.half < 0:
            return ref.at[pl.ds(self.start, self.rows)]
        start = pl.multiple_of(jnp.bitwise_xor(place, self.half) * self.lanes, self.lanes)
        return ref.at[pl.ds(self.start, self.rows), pl.ds(start, self.lanes)]


class Step(typing.NamedTuple):
    channel: typing.Any
    sources: tuple


X, Y, DIAGONAL, PAIR, PAIRS = 0, 1, 2, 3, 4
CHANNEL = (("seq", 1), ("seq", 2), ("seq", 3), ("rows", 2), ("rows", 4))


def boundary(name, ids, steps, after=(), weight=1):
    arrays = distinct([piece.array for step in steps for piece in step.sources])
    after = [array for array in distinct(after) if not any(array is other for other in arrays)]
    outs, places = {}, []
    for step in steps:
        rows = step.sources[0].rows
        key = (step.channel, step.sources[0].lanes)
        start = outs.get(key, 0)
        outs[key] = start + rows
        places.append((key, start, rows))
    keys = list(outs)
    tally = sum(len(step.sources) for step in steps) + len(steps)

    def kernel(ids_ref, *refs):
        inputs, refs = refs[: len(arrays)], refs[len(arrays) + len(after) :]
        results, refs = dict(zip(keys, refs)), refs[len(keys) :]
        buffers, refs = dict(zip(keys, refs)), refs[len(keys) :]
        scratch, copies = list(refs[:-1]), Copies(refs[-1])
        coming = []
        for step in steps:
            for piece in step.sources:
                origin = piece.origin(inputs[where_in(arrays, piece.array)], ids_ref[2])
                coming.append((copies.start(origin, scratch[len(coming)]), scratch[len(coming)]))
        for step, (key, start, rows) in zip(steps, places):
            terms = []
            for _ in step.sources:
                moved, ref = coming.pop(0)
                moved.wait()
                terms.append(ref)
            rest = slice(start, start + rows)
            summed = functools.reduce(jnp.add, [term[...].astype(WIDE) for term in terms])
            buffers[key][rest, :] = summed.astype(LOW)
            copies.leave(buffers[key].at[rest], results[key].at[rest])
        copies.finish()

    shapes = [shape_of((outs[key], key[1]), LOW) for key in keys]
    given = pl.pallas_call(
        kernel,
        name=name,
        out_shape=shapes,
        in_specs=[SMEM] + [HBM] * (len(arrays) + len(after)),
        out_specs=[HBM] * len(keys),
        scratch_shapes=[pltpu.VMEM(each.shape, LOW) for each in shapes]
        + [pltpu.VMEM((piece.rows, piece.lanes), LOW) for step in steps for piece in step.sources]
        + [pltpu.SemaphoreType.DMA((tally,))],
        compiler_params=parameters(),
        cost_estimate=cost(MIX_COST * weight, 0),
    )(ids, *arrays, *after)
    formed = dict(zip(keys, given))
    arrived = {key: swap(formed[key], *CHANNEL[key[0]]) for key in keys if key[0] is not None}
    pieces = []
    for key, start, rows in places:
        mine = Piece(formed[key], start, rows)
        pieces.append((mine, mine._replace(array=arrived[key]) if key in arrived else None))
    return pieces, list(given)


class Flow:
    def __init__(self, grads, first, rest):
        keep, send = grads
        self.arrays = (keep, swap(send, "rows", 1))
        self.first, self.rest, self.at = first, rest, 0
        self.sent = self.arrived = None

    def both(self, start, rows):
        return tuple(Piece(array, start, rows) for array in self.arrays)

    def next_steps(self):
        a, b = self.first, self.rest
        own = 2 * (a + b)
        if self.at == 0:
            return [Step(X, self.both(0, 2 * a)), Step(Y, self.both(2 * a, 2 * b))]
        x, y = self.arrived
        if self.at == 1:
            self.x, self.y = x, y
            return [
                Step(Y, self.both(own + a, a) + (x._replace(start=x.start + a, rows=a),)),
                Step(X, self.both(own + 2 * a + b, b) + (y._replace(start=y.start + b, rows=b),)),
            ]
        if self.at == 2:
            sums = [
                self.both(own, a) + (self.x._replace(rows=a), x),
                self.both(own + 2 * a, b) + (self.y._replace(rows=b), y),
            ]
            return [
                Step(channel, tuple(piece.halved(half) for piece in each))
                for channel, half in ((PAIR, 1), (None, 0))
                for each in sums
            ]
        if self.at == 3:
            return [Step(PAIRS, (self.sent[2], x)), Step(PAIRS, (self.sent[3], y))]
        return [Step(PAIR, (self.sent[0], x)), Step(PAIR, (self.sent[1], y))]

    def take(self, pieces):
        self.sent = [piece[0] for piece in pieces]
        self.arrived = [piece[1] for piece in pieces[:2]]
        self.at += 1

    def parts(self, own, other):
        done = []
        for z_other, pieces in enumerate((self.sent, self.arrived)):
            start = 0
            for piece in pieces:
                for c_other, arrays in enumerate((own, other)):
                    done.append((piece._replace(array=arrays[z_other]), c_other, z_other, start))
                start += piece.rows
        return done

    @property
    def rows(self):
        return self.first + self.rest


def advance(name, ids, flows, extra=(), after=(), weight=1):
    steps, counts = [], []
    for flow in flows:
        own = flow.next_steps()
        counts.append(len(own))
        steps += own
    steps += list(extra)
    pieces, arrays = boundary(name, ids, steps, after, weight)
    for flow, n in zip(flows, counts):
        flow.take(pieces[:n])
        pieces = pieces[n:]
    return pieces, arrays


def cross_cores(flows):
    own = (flows[0].sent[0].array, flows[0].arrived[0].array)
    return own, tuple(swap(array, "rows", 1) for array in own)


def cross_both(flows):
    formed = flows[0].sent[0].array
    return (formed, flows[0].arrived[0].array), (swap(formed, "rows", 1), swap(formed, "rows", 3))


def finish_units(name, ids, groups, outs, old, returns=(), vectors=None, after=()):
    parts = [part for _, group, _ in groups for part in group]
    back = [block for _, blocks in returns for block in blocks]
    arrays = distinct([part[0].array for part in parts] + [block.array for block in back])
    kept, names = list(old), list(outs)
    vector_outs = [outs[each] for each in vectors or ()]
    d = HEADS * HEAD_DIM

    def kernel(ids_ref, *refs):
        refs = list(refs)

        def take(count):
            taken = refs[:count]
            del refs[:count]
            return taken

        inputs = take(len(arrays))
        take(len(kept) + len(after))
        results = dict(zip(names, take(len(names))))
        scratch, back_in = take(len(parts)), take(len(back))
        units, back_out, vec_out = take(len(groups)), take(len(returns)), take(len(vector_outs))
        copies = Copies(refs[0])
        me, core, place = ids_ref[0], ids_ref[1], ids_ref[2]

        def bring(piece, target):
            return copies.start(piece.origin(inputs[where_in(arrays, piece.array)], place), target)

        coming = [bring(part[0], target) for part, target in zip(parts, scratch)]
        blocks_coming = [bring(block, target) for block, target in zip(back, back_in)]
        slot = 0
        for (_, group, goals), unit in zip(groups, units):
            for piece, c_other, z_other, start in group:
                coming[slot].wait()
                side, rows = jnp.bitwise_xor(core, c_other), slice(start, start + piece.rows)
                if piece.lanes == d:
                    unit[side, rows, :] = scratch[slot][...].astype(WIDE)
                else:
                    offset = pl.multiple_of(jnp.bitwise_xor(place, z_other) * piece.lanes, piece.lanes)
                    unit[side, rows, pl.ds(offset, piece.lanes)] = scratch[slot][...].astype(WIDE)
                slot += 1
            for half, start, rows, output, index in goals:
                copies.leave(unit.at[half, start : start + rows], results[output].at[index])
        if vectors:
            last = groups[-1][0]
            top, low = units[-1][0, last - 16 : last, :], units[-1][1, last - 16 : last, :]
            stages = [top[0:8, i * LANES : (i + 1) * LANES] for i in range(4)] + [low[0:8, 0:LANES]]
            enc_s, enc_f, dec_s, crs, dec_f = stages
            gains, biases, ups, embed = vec_out
            for row, part in enumerate(stages):
                gains[row : row + 1, :] = part[0:1]
                biases[11 + row : 12 + row, :] = part[1:2]
            order = ((enc_s, 3), (enc_s, 4), (enc_s, 2), (enc_f, 2), (dec_s, 3), (dec_s, 4), (dec_s, 2))
            order += ((crs, 3), (crs, 4), (crs, 2), (dec_f, 2))
            for row, (part, at) in enumerate(order):
                biases[row : row + 1, :] = part[at : at + 1]
            ups[...] = low[8:10, :]
            embed[...] = dec_s[5:6]
            for output, buffer in zip(vectors, vec_out):
                copies.leave(buffer, results[output])
        slot = 0
        for (output, blocks), buffer in zip(returns, back_out):
            for block in range(len(blocks)):
                blocks_coming[slot].wait()
                buffer[jnp.bitwise_xor(me, block)] = back_in[slot][...].astype(buffer.dtype)
                slot += 1
            copies.leave(buffer, results[output])
        copies.finish()

    sems = len(parts) + len(back) + sum(len(goals) for _, _, goals in groups) + len(returns) + len(vector_outs)
    given = pl.pallas_call(
        kernel,
        name=name,
        out_shape=[outs[each] for each in names],
        in_specs=[SMEM] + [HBM] * (len(arrays) + len(kept) + len(after)),
        out_specs=[HBM] * len(names),
        scratch_shapes=[pltpu.VMEM((part[0].rows, part[0].lanes), LOW) for part in parts]
        + [pltpu.VMEM((block.rows, block.lanes), LOW) for block in back]
        + [pltpu.VMEM((2, rows, d), WIDE) for rows, _, _ in groups]
        + [pltpu.VMEM(outs[output].shape, outs[output].dtype) for output, _ in returns]
        + [pltpu.VMEM(each.shape, each.dtype) for each in vector_outs]
        + [pltpu.SemaphoreType.DMA((sems,))],
        input_output_aliases={1 + len(arrays) + i: names.index(each) for i, each in enumerate(kept)},
        compiler_params=parameters(),
        cost_estimate=cost(MIX_COST, 0),
    )(ids, *arrays, *[old[each] for each in kept], *after)
    return types.SimpleNamespace(**dict(zip(names, given)))


def by_rows(
    enc_input,
    dec_input,
    src_lengths,
    tgt_lengths,
    masked,
    cotangent,
    self_qkv,
    attn_out,
    cross_q,
    cross_kv,
    ffn_up,
    ffn_down,
    norm_gain,
    biases,
    up_bias,
    mask_embed,
):
    count, length, d = enc_input.shape
    tokens, ff = count * length, ffn_up.shape[2]
    me = lax.axis_index("seq")
    row = lax.axis_index("rows")
    ids = jnp.stack([me, row % 2, row // 2 % 2]).astype(jnp.int32)
    enc_others = spread_rows(enc_input, me)
    packed = pack_rows(ids, dec_input, cotangent, masked)
    packs = [swap(packed[away], "seq", away) for away in range(1, count)]
    embed = mask_embed.reshape(1, d)
    head_shape = (HEADS, HEAD_DIM, tokens)
    low_tokens, wide_tokens = shape_of((tokens, d), LOW), shape_of((tokens, d), WIDE)
    low_t, low_heads, low_ff = shape_of((d, tokens), LOW), shape_of(head_shape, LOW), shape_of((tokens, ff), LOW)
    exps, inverse = shape_of((HEADS, tokens, tokens), LOW), shape_of((HEADS, 8, tokens), WIDE)
    scale, vec = shape_of((tokens, LANES), WIDE), shape_of((8, d), WIDE)
    bias = shape_of((tokens, tokens), WIDE)
    scalars = dict(ids=ids, src=src_lengths, tgt=tgt_lengths)
    step = dict(ids=ids)
    small = dict(biases=whole(biases), gains=whole(norm_gain))
    dense, score = 2 * tokens * d * d, 2 * tokens * tokens * d
    mask_pieces = [(packed[0], None, (0,))]
    for i, array in enumerate(packs, 1):
        mask_pieces.append((array, lambda s: (slice(2 * length, 2 * length + 16),), (i,)))
    mask_part = ((count, 16, d), LOW, mask_pieces)

    def tokens_of(local, others, start=0):
        return ((tokens, d), LOW, token_pieces(local, others, length, start))

    def halves(rows):
        return [shape_of((count * rows, d), LOW)] * 2

    enc = run_stage(
        "encoder_forward",
        functools.partial(encoder_forward, length),
        scalars,
        [dict(
            x=tokens_of(enc_input, enc_others),
            **small,
            qkv=layer(self_qkv, 0),
            proj=layer(attn_out, 0),
            up_bias=whole(up_bias),
            up=layer(ffn_up, 0),
            down=layer(ffn_down, 0),
        )],
        dict(
            x_t=low_t,
            q=low_heads,
            k=low_heads,
            v=low_heads,
            exps=exps,
            inverse=inverse,
            context=low_heads,
            hat0=low_tokens,
            scale0=scale,
            low1=low_tokens,
            act1=low_ff,
            slope1=low_ff,
            hat1=low_tokens,
            scale1=scale,
            memory_t=low_t,
        ),
        dict(bias=bias),
        12 * dense + 2 * score,
        24e6,
        after=packed[1:],
    )
    attention_work = dict(
        context_grad=shape_of(head_shape, WIDE),
        dq=low_heads,
        dk=low_heads,
        dv=low_heads,
        sums=shape_of((2, HEADS, HEAD_DIM, LANES), WIDE),
    )
    dec = run_stage(
        "decoder",
        functools.partial(decoder, length),
        scalars,
        [dict(
            **small,
            mask=mask_part,
            x=tokens_of(dec_input, packs),
            embed=whole(embed),
            qkv=layer(self_qkv, 1),
            proj1=layer(attn_out, 1),
            cross_q=whole(cross_q),
            memory_t=whole(enc.memory_t),
            cross_kv=whole(cross_kv),
            proj2=layer(attn_out, 2),
            up_bias=whole(up_bias),
            up=layer(ffn_up, 1),
            down=layer(ffn_down, 1),
            cotangent=tokens_of(cotangent, packs, length),
        )],
        dict(
            x_t=low_t,
            q2=low_heads,
            k2=low_heads,
            v2=low_heads,
            exps2=exps,
            inverse2=inverse,
            context2=low_heads,
            hat2=low_tokens,
            scale2=scale,
            final=[shape_of((length, d), LOW)] * count,
            vec=vec,
            vec_cross=vec,
            grads=halves(4 * LANES),
            grads_cross=halves(2 * LANES),
            memory_grad=wide_tokens,
            hidden_grad=wide_tokens,
        ),
        dict(
            bias=bias,
            low=low_tokens,
            act=low_ff,
            slope=low_ff,
            pre=low_ff,
            hidden_t=low_t,
            hat=wide_tokens,
            scale=scale,
            q=low_heads,
            k=low_heads,
            v=low_heads,
            exps=exps,
            inverse=inverse,
            context=low_heads,
            **attention_work,
        ),
        40 * dense + 8 * score,
        50e6,
    )

    def attention_parts(context, inverse, q, k, v, exps):
        return dict(
            context=whole(context),
            inverse=whole(inverse),
            q=whole(q),
            k=whole(k),
            v=whole(v),
            exps=whole(exps),
        )

    final_back = [swap(dec.final[i], "seq", i) for i in range(1, count)]
    flow_ffn, flow_cross = Flow(dec.grads, 2 * LANES, 2 * LANES), Flow(dec.grads_cross, LANES, LANES)
    first_flows = [flow_ffn, flow_cross]

    def self_stage(name, norm_row, last, grad, hat, scale, attention, x_t, index, more, after):
        rows = 2 * LANES + (16 if last else 0)
        return run_stage(
            name,
            functools.partial(self_backward, norm_row, last),
            step,
            [dict(
                gains=whole(norm_gain),
                grad=whole(grad),
                hat=whole(hat),
                scale=whole(scale),
                proj=layer(attn_out, index),
                **attention_parts(*attention),
                x_t=whole(x_t),
                qkv=layer(self_qkv, index),
                **more,
            )],
            dict(input_grad=low_tokens, grads=halves(rows), **({} if last else dict(vec=vec))),
            dict(vec=vec, **attention_work),
            8 * dense + 4 * score,
            20e6,
            after,
        )

    enc_ffn = run_stage(
        "encoder_ffn_backward",
        encoder_ffn_backward,
        step,
        [dict(
            gains=whole(norm_gain),
            grad=whole(dec.memory_grad),
            hat=whole(enc.hat1),
            scale=whole(enc.scale1),
            down=layer(ffn_down, 0),
            slope=whole(enc.slope1),
            act=whole(enc.act1),
            low=whole(enc.low1),
            up=layer(ffn_up, 0),
        )],
        dict(vec=vec, grad1=wide_tokens, grads=halves(4 * LANES)),
        dict(pre=low_ff),
        16 * dense,
        18e6,
    )
    flow_enc = Flow(enc_ffn.grads, 2 * LANES, 2 * LANES)
    _, formed = advance("first_xy", ids, first_flows, after=[enc_ffn.vec] + final_back, weight=BIG_WEIGHT)
    _, formed = advance("encoder_ffn_xy", ids, [flow_enc], after=formed)
    dec_self = self_stage(
        "decoder_self_backward",
        2,
        False,
        dec.hidden_grad,
        dec.hat2,
        dec.scale2,
        (dec.context2, dec.inverse2, dec.q2, dec.k2, dec.v2, dec.exps2),
        dec.x_t,
        1,
        dict(mask=mask_part),
        formed,
    )
    flow_dec = Flow(dec_self.grads, LANES, LANES)
    _, formed = advance("first_yx", ids, first_flows, after=[dec_self.vec], weight=BIG_WEIGHT)
    dec_blocks = [Piece(dec_self.input_grad, i * length, length) for i in range(count)]

    def sent_back(blocks):
        return [Step(channel, (blocks[i],)) for i, channel in ((1, X), (2, Y), (3, X))]

    def forwarded(pieces):
        return [Step(Y, (pieces[2][1],))]

    def came_back(blocks, pieces):
        return [blocks[0]] + [pieces[i][1] for i in (0, 1, 3)]

    _, formed = advance("decoder_self_xy", ids, [flow_dec], after=formed)
    enc_self = self_stage(
        "encoder_self_backward",
        0,
        True,
        enc_ffn.grad1,
        enc.hat0,
        enc.scale0,
        (enc.context, enc.inverse, enc.q, enc.k, enc.v, enc.exps),
        enc.x_t,
        0,
        dict(
            vec_enc=whole(enc_ffn.vec),
            vec_self=whole(dec_self.vec),
            vec_cross=whole(dec.vec_cross),
            vec_dec=whole(dec.vec),
        ),
        formed,
    )
    flow_last = Flow(enc_self.grads, LANES, LANES + 16)
    next_flows = [flow_enc, flow_dec]
    four = first_flows + next_flows
    enc_blocks = [Piece(enc_self.input_grad, i * length, length) for i in range(count)]


    def arrivals(pieces):
        return [piece[1].array for piece in pieces]

    _, formed = advance("four_one", ids, four, after=[enc_self.input_grad], weight=BIG_WEIGHT)
    _, formed = advance("last_xy", ids, [flow_last], after=formed)
    _, formed = advance("four_two", ids, four, after=formed)
    back, formed = advance("last_yx", ids, [flow_last], sent_back(dec_blocks) + sent_back(enc_blocks), after=formed)
    dec_back, enc_back = back[:3], back[3:]
    _, formed = advance("four_three", ids, four, after=formed)
    first_done = cross_cores(first_flows)
    back, formed = advance("last_pair", ids, [flow_last], forwarded(dec_back) + forwarded(enc_back), after=formed)
    dec_back, enc_back = dec_back + back[:1], enc_back + back[1:]
    _, formed = advance("last_pairs", ids, [flow_last], after=formed + arrivals(back))
    _, formed = advance("next_four", ids, next_flows, after=formed)
    next_done = cross_cores(next_flows)
    _, formed = advance("last_back", ids, [flow_last], after=formed)
    last_done = cross_both([flow_last])
    half = 2 * LANES

    def ffn_targets(index):
        goals = []
        for side in (0, 1):
            for unit in (0, 1):
                j = side * 2 + unit
                goals.append((side, unit * LANES, LANES, "up", (index, slice(None), slice(j * d, (j + 1) * d))))
            goals.append((side, half, half, "down", (index, slice(side * half, (side + 1) * half))))
        return goals

    def self_targets(index):
        goals = [(0, 0, LANES, "proj", (index,))]
        for j, (side, unit) in enumerate(((0, 1), (1, 0), (1, 1))):
            goals.append((side, unit * LANES, LANES, "qkv", (index, slice(None), slice(j * d, (j + 1) * d))))
        return goals

    cross_targets = [
        (0, 0, LANES, "proj", (2,)),
        (0, LANES, LANES, "cross_q", (slice(None),)),
        (1, 0, LANES, "cross_kv", (slice(None), slice(0, d))),
        (1, LANES, LANES, "cross_kv", (slice(None), slice(d, 2 * d))),
    ]
    local_rows = (count, length, d)
    up_down = dict(up=shape_of((2, LANES, ff), WIDE), down=shape_of((2, d, d), WIDE))
    proj = shape_of((3, LANES, d), WIDE)
    proj_qkv = dict(proj=proj, qkv=shape_of((2, LANES, 3 * d), WIDE))
    first = finish_units(
        "finish_first",
        ids,
        [
            (flow_ffn.rows, flow_ffn.parts(*first_done), ffn_targets(1)),
            (flow_cross.rows, flow_cross.parts(*first_done), cross_targets),
        ],
        dict(
            final=shape_of(local_rows, LOW),
            cross_q=shape_of((LANES, d), WIDE),
            cross_kv=shape_of((LANES, 2 * d), WIDE),
            proj=proj,
            **up_down,
        ),
        {},
        [("final", [Piece(array, 0, length) for array in [dec.final[0]] + final_back])],
        after=formed,
    )
    second = finish_units(
        "finish_next",
        ids,
        [
            (flow_enc.rows, flow_enc.parts(*next_done), ffn_targets(0)),
            (flow_dec.rows, flow_dec.parts(*next_done), self_targets(1)),
        ],
        dict(dec_grad=shape_of(local_rows, WIDE), **up_down, **proj_qkv),
        dict(up=first.up, down=first.down, proj=first.proj),
        [("dec_grad", came_back(dec_blocks, dec_back))],
        after=[first.final],
    )
    third = finish_units(
        "finish_last",
        ids,
        [(flow_last.rows, flow_last.parts(*last_done), self_targets(0))],
        dict(
            enc_grad=shape_of(local_rows, WIDE),
            gains=shape_of((5, LANES), WIDE),
            biases=shape_of((16, LANES), WIDE),
            ups=shape_of((2, d), WIDE),
            embed=shape_of((1, LANES), WIDE),
            **proj_qkv,
        ),
        dict(proj=second.proj, qkv=second.qkv),
        [("enc_grad", came_back(enc_blocks, enc_back))],
        ("gains", "biases", "ups", "embed"),
    )
    return (
        first.final,
        third.enc_grad,
        second.dec_grad,
        third.qkv,
        third.proj,
        first.cross_q,
        first.cross_kv,
        second.up,
        second.down,
        third.gains,
        third.biases,
        third.ups,
        third.embed.reshape(LANES),
    )


def fits_by_rows(mesh, enc_input, ffn_up):
    count, length = enc_input.shape[0], enc_input.shape[1]
    return (
        mesh.shape["seq"] == 4
        and count == 4
        and mesh.shape["rows"] == 8
        and length == LANES
        and ffn_up.shape[2] == count * ffn_up.shape[1]
        and enc_input.shape[2] == HEADS * HEAD_DIM == count * LANES
    )


def device_program(mesh, *arrays):
    if fits_by_rows(mesh, arrays[0], arrays[10]):
        return by_rows(*arrays)
    return local(*arrays)


def solution(mesh):
    return jax.shard_map(
        functools.partial(device_program, mesh),
        mesh=mesh,
        in_specs=(
            P("rows", "seq", None),
            P("rows", "seq", None),
            P("rows", None),
            P("rows", None),
            P("rows", "seq"),
            P("rows", "seq", None),
            P(),
            P(),
            P(),
            P(),
            P(),
            P(),
            P(),
            P(),
            P(),
            P(),
        ),
        out_specs=(
            P("rows", "seq", None),
            P("rows", "seq", None),
            P("rows", "seq", None),
            P(None, "seq", None),
            P(None, "seq", None),
            P("seq", None),
            P("seq", None),
            P(None, "seq", None),
            P(None, "seq", None),
            P(None, "seq"),
            P(None, "seq"),
            P(None, "seq"),
            P("seq"),
        ),
        check_vma=False,
    )
```

```python
import functools
import types
import typing

import jax
import jax.numpy as jnp
from jax import lax
from jax.experimental import pallas as pl
from jax.experimental.pallas import tpu as pltpu
from jax.sharding import PartitionSpec as P

D = 512
HEADS = 8
HEAD_DIM = 64


EPSILON = 1e-05
NEG_FILL = -1000000000.0
START_FILL = -1e30


def normalize(residual, scale_gain, offset):
    centred = residual - jnp.mean(residual, axis=-1, keepdims=True)
    spread = jnp.mean(centred * centred, axis=-1, keepdims=True)
    return centred * lax.rsqrt(spread + EPSILON) * scale_gain + offset


def gelu_exact(values):
    return jax.nn.gelu(values, approximate=False)


def segments(lengths, places):
    doc_ends = jnp.cumsum(lengths, axis=1)
    return jnp.sum((doc_ends[:, None, :] <= places[None, :, None]).astype(jnp.int32), axis=2)


def project(inputs, weight):
    return jnp.einsum("rsd,df->rsf", inputs, weight, preferred_element_type=jnp.float32)


def project_back(gradient, weight):
    return jnp.einsum("rsf,df->rsd", gradient, weight, preferred_element_type=jnp.float32)


def weight_grad(inputs, gradient):
    return jnp.einsum("rsd,rsf->df", inputs, gradient, preferred_element_type=jnp.float32)


def token_sum(gradient):
    return jnp.sum(gradient, axis=(0, 1))


def split_heads(tensor):
    return tensor.reshape(tensor.shape[:2] + (HEADS, HEAD_DIM))


def split_blocks(tensor, block_size):
    new_shape = (tensor.shape[0], tensor.shape[1] // block_size, block_size) + tensor.shape[2:]
    return jnp.swapaxes(tensor.reshape(new_shape), 0, 1)


def block_scores(query_heads, key_heads, query_seg, key_seg):
    scores = jnp.einsum(
        "rqhd,rkhd->rhqk", query_heads, key_heads, preferred_element_type=jnp.float32
    ) * HEAD_DIM ** (-0.5)
    allowed = query_seg[:, None, :, None] == key_seg[:, None, None, :]
    return jnp.where(allowed, scores, NEG_FILL)


def block_grads(
    query_heads, grad_heads, log_total, delta_rows, query_seg, key_heads, value_heads, key_seg
):
    scores = block_scores(query_heads, key_heads, query_seg, key_seg)
    probs = jnp.exp(scores - log_total[..., None])
    dprobs = jnp.einsum(
        "rqhd,rkhd->rhqk", grad_heads, value_heads, preferred_element_type=jnp.float32
    )
    dscores = (probs * (dprobs - delta_rows[..., None])).astype(jnp.bfloat16)
    scaling = HEAD_DIM ** (-0.5)
    query_part = (
        jnp.einsum("rhqk,rkhd->rqhd", dscores, key_heads, preferred_element_type=jnp.float32)
        * scaling
    )
    key_part = (
        jnp.einsum("rhqk,rqhd->rkhd", dscores, query_heads, preferred_element_type=jnp.float32)
        * scaling
    )
    value_part = jnp.einsum(
        "rhqk,rqhd->rkhd",
        probs.astype(jnp.bfloat16),
        grad_heads,
        preferred_element_type=jnp.float32,
    )
    return (query_part, key_part, value_part)


def start_state(row_count, length):
    return (
        jnp.full((row_count, HEADS, length), START_FILL, jnp.float32),
        jnp.zeros((row_count, HEADS, length), jnp.float32),
        jnp.zeros((row_count, length, HEADS, HEAD_DIM), jnp.float32),
    )


def finish_state(state):
    running_max, running_sum, running_acc = state
    context = running_acc / jnp.swapaxes(running_sum, 1, 2)[..., None]
    return (
        context.reshape(context.shape[:2] + (HEADS * HEAD_DIM,)),
        running_max + jnp.log(running_sum),
    )


def absorber(query_heads, query_seg, key_lengths, length):

    def absorb(carried, piece_pair, first_pos):
        key_piece, value_piece = piece_pair
        piece_len = key_piece.shape[1]
        seg_piece = segments(key_lengths, jnp.arange(piece_len, dtype=jnp.int32))

        def advance(running, inputs):
            running_max, running_sum, running_acc = running
            key_block, value_block, seg_block = inputs
            scores = block_scores(query_heads, key_block, query_seg, seg_block)
            new_max = jnp.maximum(running_max, jnp.max(scores, axis=-1))
            factor = jnp.exp(running_max - new_max)
            exp_scores = jnp.exp(scores - new_max[..., None])
            running_sum = running_sum * factor + jnp.sum(exp_scores, axis=-1)
            running_acc = running_acc * jnp.swapaxes(factor, 1, 2)[..., None] + jnp.einsum(
                "rhqk,rkhd->rqhd",
                exp_scores.astype(jnp.bfloat16),
                value_block,
                preferred_element_type=jnp.float32,
            )
            return ((new_max, running_sum, running_acc), None)

        blocks = (
            split_blocks(split_heads(key_piece), length),
            split_blocks(split_heads(value_piece), length),
            split_blocks(seg_piece, length),
        )
        result, unused = lax.scan(advance, carried, blocks)
        return result

    return absorb


def attend_forward(queries, keys, values, query_seg, key_lengths):
    row_count, length = (queries.shape[0], queries.shape[1])
    query_heads = split_heads(queries)
    absorb = absorber(query_heads, query_seg, key_lengths, length)
    state = absorb(
        start_state(row_count, length),
        (
            lax.all_gather(keys, "seq", axis=1, tiled=True),
            lax.all_gather(values, "seq", axis=1, tiled=True),
        ),
        jnp.int32(0),
    )
    context, log_total = finish_state(state)
    return (context, log_total, None)


def attend_backward(
    queries,
    keys,
    values,
    query_seg,
    key_seg,
    query_lengths,
    key_lengths,
    context,
    log_total,
    context_grad,
):
    row_count, length = (queries.shape[0], queries.shape[1])
    grad_low = context_grad.astype(jnp.bfloat16)
    query_heads = split_heads(queries)
    grad_heads = split_heads(grad_low)
    delta_rows = jnp.swapaxes(
        jnp.sum(grad_heads.astype(jnp.float32) * split_heads(context), axis=-1), 1, 2
    )
    zero_heads = jnp.zeros((row_count, length, HEADS, HEAD_DIM), jnp.float32)
    key_piece = lax.all_gather(keys, "seq", axis=1, tiled=True)
    value_piece = lax.all_gather(values, "seq", axis=1, tiled=True)
    piece_len = key_piece.shape[1]
    block_size = length
    seg_piece = segments(key_lengths, jnp.arange(piece_len, dtype=jnp.int32))

    def advance(running, inputs):
        key_block, value_block, seg_block = inputs
        query_part, unused_keys, unused_values = block_grads(
            query_heads,
            grad_heads,
            log_total,
            delta_rows,
            query_seg,
            key_block,
            value_block,
            seg_block,
        )
        return (running + query_part, None)

    blocks = (
        split_blocks(split_heads(key_piece), block_size),
        split_blocks(split_heads(value_piece), block_size),
        split_blocks(seg_piece, block_size),
    )
    result, unused = lax.scan(advance, zero_heads, blocks)
    query_grad = result
    total_all, delta_all = (
        lax.all_gather(log_total, "seq", axis=2, tiled=True),
        lax.all_gather(delta_rows, "seq", axis=2, tiled=True),
    )
    key_heads = split_heads(keys)
    value_heads = split_heads(values)
    query_piece = lax.all_gather(queries, "seq", axis=1, tiled=True)
    grad_piece = lax.all_gather(grad_low, "seq", axis=1, tiled=True)
    piece_len = query_piece.shape[1]
    block_size = length
    seg_piece = segments(query_lengths, jnp.arange(piece_len, dtype=jnp.int32))
    offsets = jnp.arange(piece_len // block_size, dtype=jnp.int32) * block_size

    def advance(running, inputs):
        query_block, grad_block, seg_block, offset = inputs
        total_block = lax.dynamic_slice_in_dim(total_all, offset, block_size, 2)
        delta_block = lax.dynamic_slice_in_dim(delta_all, offset, block_size, 2)
        unused_query, key_part, value_part = block_grads(
            query_block,
            grad_block,
            total_block,
            delta_block,
            seg_block,
            key_heads,
            value_heads,
            key_seg,
        )
        return ((running[0] + key_part, running[1] + value_part), None)

    blocks = (
        split_blocks(split_heads(query_piece), block_size),
        split_blocks(split_heads(grad_piece), block_size),
        split_blocks(seg_piece, block_size),
        offsets,
    )
    result, unused = lax.scan(advance, (zero_heads, zero_heads), blocks)
    key_grad, value_grad = result
    return (
        query_grad.reshape(queries.shape),
        key_grad.reshape(queries.shape),
        value_grad.reshape(queries.shape),
    )


def self_forward(inputs_low, w_qkv, bias_q, bias_v, segment, lengths):
    projected = project(inputs_low, w_qkv)
    queries = (projected[..., :D] + bias_q).astype(jnp.bfloat16)
    keys = projected[..., D : 2 * D].astype(jnp.bfloat16)
    values = (projected[..., 2 * D :] + bias_v).astype(jnp.bfloat16)
    context, log_total, stored = attend_forward(queries, keys, values, segment, lengths)
    return (queries, keys, values, context, log_total, stored)


def ffn_forward(hidden, w_up, bias_up, w_down, bias_down):
    hidden_low = hidden.astype(jnp.bfloat16)
    pre_act = project(hidden_low, w_up) + bias_up
    activated, act_back = jax.vjp(gelu_exact, pre_act)
    act_low = activated.astype(jnp.bfloat16)
    return (project(act_low, w_down) + bias_down, (hidden_low, act_low, act_back))


def ffn_backward(out_grad, stored, w_up, w_down):
    hidden_low, act_low, act_back = stored
    out_low = out_grad.astype(jnp.bfloat16)
    down_grad = weight_grad(act_low, out_low)
    (pre_grad,) = act_back(project_back(out_low, w_down))
    pre_low = pre_grad.astype(jnp.bfloat16)
    up_grad = weight_grad(hidden_low, pre_low)
    return (
        project_back(pre_low, w_up),
        up_grad,
        token_sum(pre_grad),
        down_grad,
        token_sum(out_grad),
    )


def local(
    enc_input,
    dec_input,
    src_lengths,
    tgt_lengths,
    masked,
    cotangent,
    self_qkv,
    attn_out,
    cross_q,
    cross_kv,
    ffn_up,
    ffn_down,
    norm_gain,
    biases,
    up_bias,
    mask_embed,
):
    length = enc_input.shape[1]
    places = lax.axis_index("seq") * length + jnp.arange(length, dtype=jnp.int32)
    src_seg = segments(src_lengths, places)
    tgt_seg = segments(tgt_lengths, places)
    mask_float = masked.astype(jnp.float32)[..., None]
    enc_queries, enc_keys, enc_values, enc_context, enc_total, enc_stored = self_forward(
        enc_input, self_qkv[0], biases[0], biases[1], src_seg, src_lengths
    )
    enc_ctx_low = enc_context.astype(jnp.bfloat16)
    enc_resid = enc_input.astype(jnp.float32) + project(enc_ctx_low, attn_out[0]) + biases[2]
    enc_hidden, enc_norm_back = jax.vjp(normalize, enc_resid, norm_gain[0], biases[11])
    enc_ffn, enc_kept = ffn_forward(enc_hidden, ffn_up[0], up_bias[0], ffn_down[0], biases[3])
    memory, memory_back = jax.vjp(normalize, enc_hidden + enc_ffn, norm_gain[1], biases[12])
    memory_low = memory.astype(jnp.bfloat16)
    dec_inputs = dec_input.astype(jnp.float32) + mask_float * mask_embed
    dec_low = dec_inputs.astype(jnp.bfloat16)
    dec_queries, dec_keys, dec_values, dec_context, dec_total, dec_stored = self_forward(
        dec_low, self_qkv[1], biases[4], biases[5], tgt_seg, tgt_lengths
    )
    dec_ctx_low = dec_context.astype(jnp.bfloat16)
    dec_hidden, dec_norm_back = jax.vjp(
        normalize,
        dec_inputs + project(dec_ctx_low, attn_out[1]) + biases[6],
        norm_gain[2],
        biases[13],
    )
    dec_hidden_low = dec_hidden.astype(jnp.bfloat16)
    cross_queries = (project(dec_hidden_low, cross_q) + biases[7]).astype(jnp.bfloat16)
    cross_pair = project(memory_low, cross_kv)
    cross_keys = cross_pair[..., :D].astype(jnp.bfloat16)
    cross_values = (cross_pair[..., D:] + biases[8]).astype(jnp.bfloat16)
    cross_context, cross_total, cross_stored = attend_forward(
        cross_queries, cross_keys, cross_values, tgt_seg, src_lengths
    )
    cross_ctx_low = cross_context.astype(jnp.bfloat16)
    cross_hidden, cross_norm_back = jax.vjp(
        normalize,
        dec_hidden + project(cross_ctx_low, attn_out[2]) + biases[9],
        norm_gain[3],
        biases[14],
    )
    last_ffn, last_kept = ffn_forward(cross_hidden, ffn_up[1], up_bias[1], ffn_down[1], biases[10])
    final, final_back = jax.vjp(normalize, cross_hidden + last_ffn, norm_gain[4], biases[15])
    final_grad, gain_four, shift_four = final_back(cotangent.astype(jnp.float32))
    into_cross, up_grad_one, upb_grad_one, down_grad_one, bias_ten = ffn_backward(
        final_grad, last_kept, ffn_up[1], ffn_down[1]
    )
    cross_resid_grad, gain_three, shift_three = cross_norm_back(final_grad + into_cross)
    cross_out_low = cross_resid_grad.astype(jnp.bfloat16)
    out_grad_two = weight_grad(cross_ctx_low, cross_out_low)
    cross_q_part, cross_k_part, cross_v_part = attend_backward(
        cross_queries,
        cross_keys,
        cross_values,
        tgt_seg,
        src_seg,
        tgt_lengths,
        src_lengths,
        cross_context,
        cross_total,
        project_back(cross_out_low, attn_out[2]),
    )
    cross_q_low = cross_q_part.astype(jnp.bfloat16)
    cross_kv_low = jnp.concatenate([cross_k_part, cross_v_part], axis=-1).astype(jnp.bfloat16)
    cross_q_weight = weight_grad(dec_hidden_low, cross_q_low)
    cross_kv_weight = weight_grad(memory_low, cross_kv_low)
    memory_grad = project_back(cross_kv_low, cross_kv)
    dec_resid_grad, gain_two, shift_two = dec_norm_back(
        cross_resid_grad + project_back(cross_q_low, cross_q)
    )
    dec_out_low = dec_resid_grad.astype(jnp.bfloat16)
    out_grad_one = weight_grad(dec_ctx_low, dec_out_low)
    dec_q_part, dec_k_part, dec_v_part = attend_backward(
        dec_queries,
        dec_keys,
        dec_values,
        tgt_seg,
        tgt_seg,
        tgt_lengths,
        tgt_lengths,
        dec_context,
        dec_total,
        project_back(dec_out_low, attn_out[1]),
    )
    dec_qkv_low = jnp.concatenate([dec_q_part, dec_k_part, dec_v_part], axis=-1).astype(
        jnp.bfloat16
    )
    qkv_grad_one = weight_grad(dec_low, dec_qkv_low)
    dec_input_grad = dec_resid_grad + project_back(dec_qkv_low, self_qkv[1])
    mask_grad = jnp.sum(dec_input_grad * mask_float, axis=(0, 1))
    memory_resid_grad, gain_one, shift_one = memory_back(memory_grad)
    into_enc, up_grad_zero, upb_grad_zero, down_grad_zero, bias_three = ffn_backward(
        memory_resid_grad, enc_kept, ffn_up[0], ffn_down[0]
    )
    enc_resid_grad, gain_zero, shift_zero = enc_norm_back(memory_resid_grad + into_enc)
    enc_out_low = enc_resid_grad.astype(jnp.bfloat16)
    out_grad_zero = weight_grad(enc_ctx_low, enc_out_low)
    enc_q_part, enc_k_part, enc_v_part = attend_backward(
        enc_queries,
        enc_keys,
        enc_values,
        src_seg,
        src_seg,
        src_lengths,
        src_lengths,
        enc_context,
        enc_total,
        project_back(enc_out_low, attn_out[0]),
    )
    enc_qkv_low = jnp.concatenate([enc_q_part, enc_k_part, enc_v_part], axis=-1).astype(
        jnp.bfloat16
    )
    qkv_grad_zero = weight_grad(enc_input, enc_qkv_low)
    enc_input_grad = enc_resid_grad + project_back(enc_qkv_low, self_qkv[0])
    bias_rows = jnp.stack(
        [
            token_sum(enc_q_part),
            token_sum(enc_v_part),
            token_sum(enc_resid_grad),
            bias_three,
            token_sum(dec_q_part),
            token_sum(dec_v_part),
            token_sum(dec_resid_grad),
            token_sum(cross_q_part),
            token_sum(cross_v_part),
            token_sum(cross_resid_grad),
            bias_ten,
            shift_zero,
            shift_one,
            shift_two,
            shift_three,
            shift_four,
        ]
    )
    shares = (
        lax.psum_scatter(
            jnp.stack([qkv_grad_zero, qkv_grad_one]), "seq", scatter_dimension=1, tiled=True
        ),
        lax.psum_scatter(
            jnp.stack([out_grad_zero, out_grad_one, out_grad_two]),
            "seq",
            scatter_dimension=1,
            tiled=True,
        ),
        lax.psum_scatter(cross_q_weight, "seq", scatter_dimension=0, tiled=True),
        lax.psum_scatter(cross_kv_weight, "seq", scatter_dimension=0, tiled=True),
        lax.psum_scatter(
            jnp.stack([up_grad_zero, up_grad_one]), "seq", scatter_dimension=1, tiled=True
        ),
        lax.psum_scatter(
            jnp.stack([down_grad_zero, down_grad_one]), "seq", scatter_dimension=1, tiled=True
        ),
        lax.psum_scatter(
            jnp.stack([gain_zero, gain_one, gain_two, gain_three, gain_four]),
            "seq",
            scatter_dimension=1,
            tiled=True,
        ),
        lax.psum_scatter(bias_rows, "seq", scatter_dimension=1, tiled=True),
        lax.psum_scatter(
            jnp.stack([upb_grad_zero, upb_grad_one]), "seq", scatter_dimension=1, tiled=True
        ),
        lax.psum_scatter(mask_grad, "seq", scatter_dimension=0, tiled=True),
    )
    totals = lax.psum(
        (
            shares[0],
            shares[1],
            shares[2],
            shares[3],
            shares[4],
            shares[5],
            shares[6],
            shares[7],
            shares[8],
            shares[9],
        ),
        "rows",
    )
    return (
        final.astype(jnp.bfloat16),
        enc_input_grad,
        dec_input_grad,
        totals[0],
        totals[1],
        totals[2],
        totals[3],
        totals[4],
        totals[5],
        totals[6],
        totals[7],
        totals[8],
        totals[9],
    )


LANES = 128
CHANNELS = 96
COST = 50
MIX_COST = 4e9
BIG_WEIGHT = 2e11 / MIX_COST
BIG_VMEM = 64 * 2**20
LOW = jnp.bfloat16
WIDE = jnp.float32
HBM = pl.BlockSpec(memory_space=pltpu.HBM)
SMEM = pl.BlockSpec(memory_space=pltpu.SMEM)


def shape_of(dims, dtype):
    return jax.ShapeDtypeStruct(tuple(dims), dtype)


def distinct(arrays):
    found = []
    for array in arrays:
        if not any(array is other for other in found):
            found.append(array)
    return found


def where_in(arrays, array):
    return [other is array for other in arrays].index(True)


def parameters():
    return pltpu.CompilerParams(vmem_limit_bytes=BIG_VMEM)


def cost(flops, moved):
    return pl.CostEstimate(flops=int(flops), bytes_accessed=int(moved), transcendentals=0)


class Copies:
    def __init__(self, sems):
        self.sems, self.used, self.leaving = sems, 0, []

    def start(self, source, target):
        moved = pltpu.make_async_copy(source, target, self.sems.at[self.used])
        self.used += 1
        moved.start()
        return moved

    def leave(self, source, target):
        self.leaving.append(self.start(source, target))

    def finish(self):
        for moved in self.leaving:
            moved.wait()


class Arrivals:
    def __init__(self, copies, refs, groups):
        self._copies, self._refs, self._groups, self._coming = copies, refs, groups, {}
        self.more()

    def more(self):
        for name, origin, target in self._groups.pop(0) if self._groups else ():
            self._coming.setdefault(name, []).append(self._copies.start(origin, target))

    def finish(self):
        while self._groups:
            self.more()
        for name in self._refs:
            getattr(self, name)

    def __getattr__(self, name):
        while name not in self._coming and any(name == move[0] for group in self._groups for move in group):
            self.more()
        for moved in self._coming.get(name, ()):
            moved.wait()
        self._coming[name] = []
        return self._refs[name]


class Stage(typing.NamedTuple):
    scalars: typing.Any
    use: typing.Any
    out: typing.Any
    work: typing.Any
    copies: typing.Any
    targets: typing.Any

    def push(self, *buffers):
        for buffer in buffers:
            self.push_part(buffer, ())

    def push_part(self, buffer, index):
        target = [result for ref, result in self.targets if ref is buffer][0]
        if isinstance(target, list):
            self.copies.leave(buffer.at[index], target[index[0]].at[index[1:]] if index[1:] else target[index[0]])
        else:
            self.copies.leave(buffer.at[index] if index else buffer, target.at[index] if index else target)


def run_stage(name, body, scalars, parts, outs, work, flops, moved, after=()):
    all_parts = {key: part for group in parts for key, part in group.items()}
    arrays = distinct([move[0] for part in all_parts.values() for move in part[2]])
    after = [array for array in distinct(after) if not any(array is other for other in arrays)]
    flat_outs, spots = [], {}
    for key, shape in outs.items():
        several = shape if isinstance(shape, list) else [shape]
        spots[key] = (len(flat_outs), len(several))
        flat_outs += several
    buffers = [shape_of((len(s),) + s[0].shape, s[0].dtype) if isinstance(s, list) else s for s in outs.values()]

    def kernel(*refs):
        refs = list(refs)

        def take(count):
            taken = refs[:count]
            del refs[:count]
            return taken

        scalar_refs = types.SimpleNamespace(**dict(zip(scalars, take(len(scalars)))))
        inputs = take(len(arrays))
        take(len(after))
        results = take(len(flat_outs))
        part_refs = dict(zip(all_parts, take(len(all_parts))))
        out_refs = dict(zip(outs, take(len(outs))))
        work_refs = dict(zip(work, take(len(work))))
        copies = Copies(refs[0])
        groups = []
        for wanted in parts:
            groups.append([])
            for key, part in wanted.items():
                for array, source, target in part[2]:
                    origin, place = inputs[where_in(arrays, array)], part_refs[key]
                    origin = origin if source is None else origin.at[source(scalar_refs)]
                    groups[-1].append((key, origin, place if target is None else place.at[target]))
        targets = []
        for key, (start, count) in spots.items():
            several = isinstance(outs[key], list)
            targets.append((out_refs[key], list(results[start : start + count]) if several else results[start]))
        use = Arrivals(copies, part_refs, groups)
        stage = Stage(
            scalar_refs, use, types.SimpleNamespace(**out_refs), types.SimpleNamespace(**work_refs), copies, targets
        )
        body(stage)
        use.finish()
        copies.finish()

    given = pl.pallas_call(
        kernel,
        name=name,
        out_shape=flat_outs,
        in_specs=[SMEM] * len(scalars) + [HBM] * (len(arrays) + len(after)),
        out_specs=[HBM] * len(flat_outs),
        scratch_shapes=[pltpu.VMEM(part[0], part[1]) for part in all_parts.values()]
        + [pltpu.VMEM(each.shape, each.dtype) for each in buffers]
        + [pltpu.VMEM(each.shape, each.dtype) for each in work.values()]
        + [pltpu.SemaphoreType.DMA((CHANNELS,))],
        compiler_params=parameters(),
        cost_estimate=cost(flops * COST, moved),
    )(*scalars.values(), *arrays, *after)
    found = {}
    for key, (start, count) in spots.items():
        found[key] = list(given[start : start + count]) if isinstance(outs[key], list) else given[start]
    return types.SimpleNamespace(**found)


def whole(array):
    return (tuple(array.shape), array.dtype, [(array, None, None)])


def layer(array, index):
    return (tuple(array.shape[1:]), array.dtype, [(array, lambda s: index, None)])


def dot_nn(a, b):
    return lax.dot_general(a, b, (((1,), (0,)), ((), ())), preferred_element_type=WIDE)


def dot_nt(a, b):
    return lax.dot_general(a, b, (((1,), (1,)), ((), ())), preferred_element_type=WIDE)


def dot_tn(a, b):
    return lax.dot_general(a, b, (((0,), (0,)), ((), ())), preferred_element_type=WIDE)


def total(values):
    return jnp.sum(values, axis=0, keepdims=True)


def norm_parts(residual):
    centred = residual - jnp.mean(residual, axis=-1, keepdims=True)
    scale = lax.rsqrt(jnp.mean(centred * centred, axis=-1, keepdims=True) + EPSILON)
    return centred * scale, scale


def norm_keep(stage, residual, gain, shift, hat_ref, scale_ref):
    hat, scale = norm_parts(residual)
    hat_ref[...] = hat.astype(LOW)
    scale_ref[...] = jnp.broadcast_to(scale, scale_ref.shape)
    stage.push(hat_ref, scale_ref)
    return hat * gain + shift


def norm_back(grad, hat, scale, gain):
    scaled = grad * gain
    inner = jnp.mean(scaled, axis=-1, keepdims=True)
    along = jnp.mean(scaled * hat, axis=-1, keepdims=True)
    return scale * (scaled - inner - hat * along), total(grad * hat), total(grad)


def segment_ids(lengths_ref, row, places):
    end = jnp.int32(0)
    found = jnp.zeros(places.shape, jnp.int32)
    for slot in range(lengths_ref.shape[1]):
        end = end + lengths_ref[row, slot]
        found = found + (end <= places).astype(jnp.int32)
    return found


def positions(me, length, shape, axis):
    token = lax.broadcasted_iota(jnp.int32, shape, axis)
    bits = length.bit_length() - 1
    block = lax.shift_right_logical(token, jnp.int32(bits))
    return lax.shift_left(jnp.bitwise_xor(block, me), jnp.int32(bits)) + jnp.bitwise_and(token, length - 1)


def fill_bias(bias_ref, query_lengths, key_lengths, me, length):
    tokens = bias_ref.shape[0]
    query_seg = segment_ids(query_lengths, me, positions(me, length, (1, tokens), 1))
    key_seg = segment_ids(key_lengths, me, positions(me, length, (tokens, 1), 0))
    bias_ref[...] = jnp.where(key_seg == query_seg, 0.0, NEG_FILL)


def heads_of(values):
    return values.reshape(HEADS, HEAD_DIM, values.shape[-1])


def flat(ref):
    return ref[...].reshape(HEADS * HEAD_DIM, ref.shape[-1])


def staggered(count, *steps):
    for i in range(count + len(steps) - 1):
        for lag, step in enumerate(steps):
            if 0 <= i - lag < count:
                step(i - lag)


def attention_forward(q_ref, k_ref, v_ref, bias_ref, exp_ref, inverse_ref, context_ref, score_ref):
    def form(head):
        score_ref[head % score_ref.shape[0]] = dot_tn(k_ref[head], q_ref[head]) + bias_ref[...]

    def exponentials(head):
        scores = score_ref[head % score_ref.shape[0]]
        exps = jnp.exp(scores - jnp.max(scores, axis=0, keepdims=True))
        exp_ref[head] = exps.astype(LOW)
        inverse_ref[head] = jnp.broadcast_to(1.0 / total(exps), inverse_ref.shape[1:])

    def contract(head):
        context_ref[head] = (dot_nn(v_ref[head], exp_ref[head]) * inverse_ref[head][0:1]).astype(LOW)

    staggered(HEADS, form, exponentials, contract)


def attention_backward(q_ref, k_ref, v_ref, exp_ref, inverse_ref, context_ref, work):
    for head in range(HEADS):
        exps = exp_ref[head]
        grad = (work.context_grad[head].astype(LOW).astype(WIDE) * inverse_ref[head][0:1]).astype(LOW)
        delta = total(grad.astype(WIDE) * context_ref[head].astype(WIDE))
        score_grad = (exps.astype(WIDE) * (dot_tn(v_ref[head], grad) - delta)).astype(LOW)
        dv = dot_nt(grad, exps)
        dq = dot_nn(k_ref[head], score_grad) * HEAD_DIM ** (-0.5)
        work.dv[head] = dv.astype(LOW)
        work.dk[head] = dot_nt(q_ref[head], score_grad).astype(LOW)
        work.dq[head] = dq.astype(LOW)
        wide = (HEAD_DIM, LANES)
        work.sums[0, head] = jnp.broadcast_to(jnp.sum(dq, axis=1, keepdims=True), wide)
        work.sums[1, head] = jnp.broadcast_to(jnp.sum(dv, axis=1, keepdims=True), wide)


def sum_row(sums_ref, which):
    return jnp.transpose(sums_ref[which].reshape(HEADS * HEAD_DIM, LANES))[0:1]


def qkv_forward(stage, weight, low_t, bias_t, q_col, v_col, q_ref, k_ref, v_ref):
    d = low_t.shape[0]
    queries = (dot_tn(weight[:, 0:d], low_t) + bias_t[:, q_col : q_col + 1]).astype(LOW)
    q_ref[...] = heads_of(queries * HEAD_DIM ** (-0.5))
    k_ref[...] = heads_of(dot_tn(weight[:, d : 2 * d], low_t).astype(LOW))
    v_ref[...] = heads_of((dot_tn(weight[:, 2 * d :], low_t) + bias_t[:, v_col : v_col + 1]).astype(LOW))
    stage.push(q_ref, k_ref, v_ref)


def gelu_parts(pre):
    half = 0.5 * (1.0 + lax.erf(pre * 0.5**0.5))
    density = jnp.exp(pre * pre * -0.5) * (0.5 / 3.141592653589793) ** 0.5
    return pre * half, half + pre * density


def feed_forward(low, up, up_bias, down, act_ref, slope_ref, pre_ref):
    width = low.shape[1]
    columns = [slice(j * width, (j + 1) * width) for j in range(act_ref.shape[1] // width)]

    def form(j):
        pre_ref[j % pre_ref.shape[0]] = dot_nn(low, up[:, columns[j]]) + up_bias[:, columns[j]]

    def activate(j):
        act, slope = gelu_parts(pre_ref[j % pre_ref.shape[0]])
        act_ref[:, columns[j]] = act.astype(LOW)
        slope_ref[:, columns[j]] = slope.astype(LOW)

    staggered(len(columns), form, activate)
    return dot_nn(act_ref[...], down[...])


class Halves(typing.NamedTuple):
    ref: typing.Any
    first: int
    rest: int
    me: typing.Any
    core: typing.Any
    stage: typing.Any

    def leave_regions(self, start, rows):
        for side in (0, 1):
            for begin in (start, start + 2 * (self.first + self.rest)):
                self.stage.push_part(self.ref, (side, slice(begin, begin + rows)))

    def leave_first(self, rows):
        self.leave_regions(0, 2 * self.first)

    def leave_rest(self, rows):
        self.leave_regions(2 * self.first, 2 * self.rest)

    def put(self, half, chunk, start, rows):
        away = jnp.bitwise_xor(self.me, chunk)
        low, high = jnp.bitwise_and(away, 1), lax.shift_right_logical(away, 1)
        both = 2 * (self.first + self.rest)
        if start < self.first:
            place = high * self.first + jnp.where(low == 1, 0, both) + start
        else:
            place = low * self.rest + jnp.where(high == 1, 0, both) + 2 * self.first + start - self.first
        side = jnp.bitwise_xor(self.core, half)
        self.ref[side, pl.ds(pl.multiple_of(place, 16), rows.shape[0])] = rows.astype(LOW)


def put_units(grads, block, half, unit):
    rows = LANES
    for chunk in range(block.shape[0] // rows):
        grads.put(half, chunk, unit * rows, block[chunk * rows : (chunk + 1) * rows])


def feed_back(out_grad, low, act, slope, up, down, vec_ref, vec_row, grads, pre_ref, more=None):
    width = out_grad.shape[1]
    half = width // 2
    out_low = out_grad.astype(LOW)
    columns = [slice(j * width, (j + 1) * width) for j in range(pre_ref.shape[1] // width)]
    for j, cols in enumerate(columns):
        pre = dot_nt(out_low, down[cols, :]) * slope[:, cols].astype(WIDE)
        vec_ref[vec_row + j : vec_row + j + 1, :] = total(pre)
        pre_ref[:, cols] = pre.astype(LOW)
        down_grad = dot_tn(act[:, cols], out_low)
        for r in range(2):
            grads.put(r, j, half, down_grad[r * half : (r + 1) * half])
    grads.leave_rest(half)
    low, up = low(), up()
    for j, cols in enumerate(columns):
        put_units(grads, dot_tn(low[...], pre_ref[:, cols]), j // 2, j % 2)
    grads.leave_first(half)
    return dot_nt(pre_ref[...], up[...])


def own_row(s):
    return s.ids[0]


def token_pieces(local, others, length, start=0):
    pieces = [(local, own_row, (slice(0, length),))]
    for d, array in enumerate(others, 1):
        pieces.append((array, lambda s: (slice(start, start + length),), (slice(d * length, (d + 1) * length),)))
    return pieces


def put_blocks(ref, values):
    for i in range(ref.shape[0]):
        ref[i] = values[i * ref.shape[1] : (i + 1) * ref.shape[1]]


def encoder_forward(length, stage):
    me, use, out = stage.scalars.ids[0], stage.use, stage.out
    fill_bias(stage.work.bias, stage.scalars.src, stage.scalars.src, me, length)
    x = use.x[...]
    x_t = jnp.transpose(x)
    out.x_t[...] = x_t
    stage.push(out.x_t)
    biases = use.biases[...]
    qkv = use.qkv
    use.more()
    qkv_forward(stage, qkv, x_t, jnp.transpose(biases), 0, 1, out.q, out.k, out.v)
    attention_forward(out.q, out.k, out.v, stage.work.bias, out.exps, out.inverse, out.context, stage.work.scores)
    stage.push(out.exps, out.inverse, out.context)
    gains = use.gains
    residual = x.astype(WIDE) + dot_tn(flat(out.context), use.proj[...]) + biases[2:3]
    hidden = norm_keep(stage, residual, gains[0:1], biases[11:12], out.hat0, out.scale0)
    hidden_low = hidden.astype(LOW)
    out.low1[...] = hidden_low
    stage.push(out.low1)
    ffn = feed_forward(hidden_low, use.up, use.up_bias[0:1], use.down, out.act1, out.slope1, stage.work.scores)
    stage.push(out.act1, out.slope1)
    memory = norm_keep(stage, hidden + ffn + biases[3:4], gains[1:2], biases[12:13], out.hat1, out.scale1)
    out.memory_t[...] = jnp.transpose(memory.astype(LOW))
    stage.push(out.memory_t)


def mask_columns(mask, d):
    row = jnp.concatenate([mask[i][0:1, 0:LANES].astype(WIDE) for i in range(mask.shape[0])], axis=1)
    columns = jnp.transpose(jnp.broadcast_to(row, (LANES, row.shape[1])))
    return jnp.concatenate([columns] * (d // LANES), axis=1)


def decoder(length, stage):
    me, use, out, work = stage.scalars.ids[0], stage.use, stage.out, stage.work
    biases = use.biases[...]
    bias_t = jnp.transpose(biases)
    gains = use.gains
    src, tgt = stage.scalars.src, stage.scalars.tgt
    fill_bias(work.bias, tgt, tgt, me, length)
    x = use.x[...].astype(WIDE)
    d = x.shape[1]
    y = x + mask_columns(use.mask, d) * use.embed[...]
    y_t = jnp.transpose(y.astype(LOW))
    out.x_t[...] = y_t
    stage.push(out.x_t)
    qkv = use.qkv
    use.more()
    qkv_forward(stage, qkv, y_t, bias_t, 4, 5, out.q2, out.k2, out.v2)
    use.more()
    attention_forward(out.q2, out.k2, out.v2, work.bias, out.exps2, out.inverse2, out.context2, work.scores)
    stage.push(out.exps2, out.inverse2, out.context2)
    residual = y + dot_tn(flat(out.context2), use.proj1[...]) + biases[6:7]
    hidden = norm_keep(stage, residual, gains[2:3], biases[13:14], out.hat2, out.scale2)
    hidden_t = jnp.transpose(hidden.astype(LOW))
    work.hidden_t[...] = hidden_t
    queries = (dot_tn(use.cross_q[...], hidden_t) + bias_t[:, 7:8]).astype(LOW)
    work.q[...] = heads_of(queries * HEAD_DIM ** (-0.5))
    memory_t = use.memory_t
    kv = use.cross_kv
    work.k[...] = heads_of(dot_tn(kv[:, 0:d], memory_t[...]).astype(LOW))
    work.v[...] = heads_of((dot_tn(kv[:, d:], memory_t[...]) + bias_t[:, 8:9]).astype(LOW))
    fill_bias(work.bias, tgt, src, me, length)
    attention_forward(work.q, work.k, work.v, work.bias, work.exps, work.inverse, work.context, work.scores)
    proj = use.proj2
    residual = hidden + dot_tn(flat(work.context), proj[...]) + biases[9:10]
    hat, scale = norm_parts(residual)
    work.hat[...] = hat
    work.scale[...] = jnp.broadcast_to(scale, work.scale.shape)
    hidden = hat * gains[3:4] + biases[14:15]
    work.low[...] = hidden.astype(LOW)
    up, down = use.up, use.down
    ffn = feed_forward(work.low[...], up, use.up_bias[1:2], down, work.act, work.slope, work.scores)
    hat, scale = norm_parts(hidden + ffn + biases[10:11])
    put_blocks(out.final, (hat * gains[4:5] + biases[15:16]).astype(LOW))
    for i in range(out.final.shape[0]):
        stage.push_part(out.final, (i,))
    vec, vec_cross = out.vec, out.vec_cross
    vec[...] = jnp.zeros_like(vec)
    vec_cross[...] = jnp.zeros_like(vec_cross)
    cotangent = use.cotangent[...].astype(WIDE)
    grad, vec[0:1, :], vec[1:2, :] = norm_back(cotangent, hat, scale, gains[4:5])
    vec[2:3, :] = total(grad)
    into = feed_back(
        grad,
        lambda: work.low,
        work.act,
        work.slope,
        lambda: up,
        down,
        vec,
        3,
        Halves(out.grads, 2 * LANES, 2 * LANES, me, stage.scalars.ids[1], stage),
        work.pre,
    )
    stage.push(vec)
    grads = Halves(out.grads_cross, LANES, LANES, me, stage.scalars.ids[1], stage)
    grad = out_backward(
        grad + into, work.hat[...], work.scale[:, 0:1], gains[3:4], proj, work.context, work, vec_cross, grads
    )
    attention_backward(work.q, work.k, work.v, work.exps, work.inverse, work.context, work)
    dq, dk, dv = attention_sums(work, vec_cross)
    stage.push(vec_cross)
    put_units(grads, dot_nt(work.hidden_t[...], dq), 0, 1)
    put_units(grads, dot_nt(memory_t[...], dk), 1, 0)
    put_units(grads, dot_nt(memory_t[...], dv), 1, 1)
    grads.leave_first(0)
    grads.leave_rest(0)
    out.memory_grad[...] = jnp.transpose(dot_nn(kv[:, 0:d], dk) + dot_nn(kv[:, d:], dv))
    stage.push(out.memory_grad)
    out.hidden_grad[...] = grad + jnp.transpose(dot_nn(use.cross_q[...], dq))
    stage.push(out.hidden_grad)


def out_backward(grad, hat, scale, gain, proj, context, work, vec, grads):
    grad, vec[0:1, :], vec[1:2, :] = norm_back(grad, hat, scale, gain)
    vec[2:3, :] = total(grad)
    low = grad.astype(LOW)
    work.context_grad[...] = heads_of(dot_nt(proj[...], low))
    put_units(grads, dot_nn(flat(context), low), 0, 0)
    return grad


def attention_sums(work, vec):
    vec[3:4, :] = sum_row(work.sums, 0)
    vec[4:5, :] = sum_row(work.sums, 1)
    return flat(work.dq), flat(work.dk), flat(work.dv)


def encoder_ffn_backward(stage):
    me, core = stage.scalars.ids[0], stage.scalars.ids[1]
    use, out = stage.use, stage.out
    vec = out.vec
    vec[...] = jnp.zeros_like(vec)
    hat, scale, grad = use.hat, use.scale, use.grad
    use.more()
    hat, scale = hat[...].astype(WIDE), scale[...][:, 0:1]
    grad, vec[0:1, :], vec[1:2, :] = norm_back(grad[...], hat, scale, use.gains[1:2])
    vec[2:3, :] = total(grad)
    grads = Halves(out.grads, 2 * LANES, 2 * LANES, me, core, stage)
    down, slope, act = use.down, use.slope, use.act
    use.more()
    into = feed_back(
        grad, lambda: use.low, act, slope, lambda: use.up, down, vec, 3, grads, stage.work.pre
    )
    stage.push(vec)
    out.grad1[...] = grad + into
    stage.push(out.grad1)


def put_vectors(grads, start, own, others):
    d = own.shape[1]
    for chunk in range(d // LANES):
        cols = slice(chunk * LANES, (chunk + 1) * LANES)
        first = jnp.concatenate([own[:, cols]] + [each[:, cols] for each in others[:3]], axis=1)
        first = jnp.concatenate([first, jnp.zeros_like(first)], axis=0)
        second = jnp.concatenate([others[3][:, cols], jnp.zeros((8, d - LANES), WIDE)], axis=1)
        ups = [each[3 + chunk : 4 + chunk] for each in (others[0], others[3])]
        second = jnp.concatenate([second] + ups + [jnp.zeros((6, d), WIDE)], axis=0)
        grads.put(0, chunk, start, first)
        grads.put(1, chunk, start, second)


def self_backward(norm_row, last, stage):
    me, core = stage.scalars.ids[0], stage.scalars.ids[1]
    use, out, work = stage.use, stage.out, stage.work
    vec = work.vec
    grads = Halves(out.grads, LANES, LANES + (16 if last else 0), me, core, stage)
    vec[...] = jnp.zeros_like(vec)
    hat, scale, grad, proj, context = use.hat, use.scale, use.grad, use.proj, use.context
    use.more()
    hat, scale = hat[...].astype(WIDE), scale[...][:, 0:1]
    gain = use.gains[norm_row : norm_row + 1]
    grad = out_backward(grad[...], hat, scale, gain, proj, context, work, vec, grads)
    q, k, v, exps, inverse = use.q, use.k, use.v, use.exps, use.inverse
    use.more()
    attention_backward(q, k, v, exps, inverse, context, work)
    dq, dk, dv = attention_sums(work, vec)
    x_t = use.x_t[...]
    put_units(grads, dot_nt(x_t, dk), 1, 0)
    grads.leave_first(0)
    put_units(grads, dot_nt(x_t, dq), 0, 1)
    put_units(grads, dot_nt(x_t, dv), 1, 1)
    if last:
        others = [each[...] for each in (use.vec_enc, use.vec_self, use.vec_cross, use.vec_dec)]
        put_vectors(grads, 2 * LANES, vec[...], others)
    grads.leave_rest(0)
    qkv = use.qkv
    d = x_t.shape[0]
    through = dot_nn(qkv[:, 0:d], dq) + dot_nn(qkv[:, d : 2 * d], dk) + dot_nn(qkv[:, 2 * d :], dv)
    input_grad = grad + jnp.transpose(through)
    if not last:
        vec[5:6, :] = total(input_grad * mask_columns(use.mask, d))
        out.vec[...] = vec[...]
        stage.push(out.vec)
    out.input_grad[...] = input_grad.astype(LOW)
    stage.push(out.input_grad)


def swap(array, axis_name, bit):
    size = lax.axis_size(axis_name)
    return lax.ppermute(array, axis_name, [(i, i ^ bit) for i in range(size)])


def spread_rows(local, me):
    return [
        swap(lax.dynamic_index_in_dim(local, me ^ d, 0, keepdims=False), "seq", d) for d in range(1, local.shape[0])
    ]


def pack_rows(ids, dec_input, cotangent, masked):
    count, length, d = dec_input.shape
    rows = 2 * length + 16

    def kernel(ids_ref, mask_ref, dec_ref, cot_ref, *refs):
        results, scratch, copies = refs[:count], refs[count], Copies(refs[count + 1])
        me = ids_ref[0]
        coming = []
        for away in range(1, count):
            row = jnp.bitwise_xor(me, away)
            coming.append(copies.start(dec_ref.at[row], scratch.at[away, 0:length]))
            coming.append(copies.start(cot_ref.at[row], scratch.at[away, length : 2 * length]))
        for away in range(count):
            row = mask_ref[jnp.bitwise_xor(me, away)].astype(WIDE).astype(LOW)
            row = jnp.concatenate([jnp.broadcast_to(row, (16, length))] * (d // length), axis=1)
            scratch[away, 2 * length : rows] = row
        copies.leave(scratch.at[0, 2 * length : rows], results[0])
        for away in range(1, count):
            coming[2 * away - 2].wait()
            coming[2 * away - 1].wait()
            copies.leave(scratch.at[away], results[away])
        copies.finish()

    return pl.pallas_call(
        kernel,
        name="pack_rows",
        out_shape=[shape_of((16, d), LOW)] + [shape_of((rows, d), LOW)] * (count - 1),
        in_specs=[SMEM, pl.BlockSpec(memory_space=pltpu.VMEM), HBM, HBM],
        out_specs=[HBM] * count,
        scratch_shapes=[pltpu.VMEM((count, rows, d), LOW), pltpu.SemaphoreType.DMA((3 * count,))],
        compiler_params=parameters(),
        cost_estimate=cost(0, 2e6),
    )(ids, masked.reshape(count, 1, length), dec_input, cotangent)


class Piece(typing.NamedTuple):
    array: typing.Any
    start: int
    rows: int
    half: int = -1

    def halved(self, half):
        return self._replace(half=half)

    @property
    def lanes(self):
        width = self.array.shape[-1]
        return width if self.half < 0 else width // 2

    def origin(self, ref, place):
        if self.half < 0:
            return ref.at[pl.ds(self.start, self.rows)]
        start = pl.multiple_of(jnp.bitwise_xor(place, self.half) * self.lanes, self.lanes)
        return ref.at[pl.ds(self.start, self.rows), pl.ds(start, self.lanes)]


class Step(typing.NamedTuple):
    channel: typing.Any
    sources: tuple


X, Y, DIAGONAL, PAIR, PAIRS = 0, 1, 2, 3, 4
CHANNEL = (("seq", 1), ("seq", 2), ("seq", 3), ("rows", 2), ("rows", 4))


def boundary(name, ids, steps, after=(), weight=1):
    arrays = distinct([piece.array for step in steps for piece in step.sources])
    after = [array for array in distinct(after) if not any(array is other for other in arrays)]
    outs, places = {}, []
    for step in steps:
        rows = step.sources[0].rows
        key = (step.channel, step.sources[0].lanes)
        start = outs.get(key, 0)
        outs[key] = start + rows
        places.append((key, start, rows))
    keys = list(outs)
    tally = sum(len(step.sources) for step in steps) + len(steps)

    def kernel(ids_ref, *refs):
        inputs, refs = refs[: len(arrays)], refs[len(arrays) + len(after) :]
        results, refs = dict(zip(keys, refs)), refs[len(keys) :]
        buffers, refs = dict(zip(keys, refs)), refs[len(keys) :]
        scratch, copies = list(refs[:-1]), Copies(refs[-1])
        coming = []
        for step in steps:
            for piece in step.sources:
                origin = piece.origin(inputs[where_in(arrays, piece.array)], ids_ref[2])
                coming.append((copies.start(origin, scratch[len(coming)]), scratch[len(coming)]))
        for step, (key, start, rows) in zip(steps, places):
            terms = []
            for _ in step.sources:
                moved, ref = coming.pop(0)
                moved.wait()
                terms.append(ref)
            rest = slice(start, start + rows)
            summed = functools.reduce(jnp.add, [term[...].astype(WIDE) for term in terms])
            buffers[key][rest, :] = summed.astype(LOW)
            copies.leave(buffers[key].at[rest], results[key].at[rest])
        copies.finish()

    shapes = [shape_of((outs[key], key[1]), LOW) for key in keys]
    given = pl.pallas_call(
        kernel,
        name=name,
        out_shape=shapes,
        in_specs=[SMEM] + [HBM] * (len(arrays) + len(after)),
        out_specs=[HBM] * len(keys),
        scratch_shapes=[pltpu.VMEM(each.shape, LOW) for each in shapes]
        + [pltpu.VMEM((piece.rows, piece.lanes), LOW) for step in steps for piece in step.sources]
        + [pltpu.SemaphoreType.DMA((tally,))],
        compiler_params=parameters(),
        cost_estimate=cost(MIX_COST * weight, 0),
    )(ids, *arrays, *after)
    formed = dict(zip(keys, given))
    arrived = {key: swap(formed[key], *CHANNEL[key[0]]) for key in keys if key[0] is not None}
    pieces = []
    for key, start, rows in places:
        mine = Piece(formed[key], start, rows)
        pieces.append((mine, mine._replace(array=arrived[key]) if key in arrived else None))
    return pieces, list(given)


class Flow:
    def __init__(self, grads, first, rest):
        keep, send = grads
        self.arrays = (keep, swap(send, "rows", 1))
        self.first, self.rest, self.at = first, rest, 0
        self.sent = self.arrived = None

    def both(self, start, rows):
        return tuple(Piece(array, start, rows) for array in self.arrays)

    def next_steps(self):
        a, b = self.first, self.rest
        own = 2 * (a + b)
        if self.at == 0:
            return [Step(X, self.both(0, 2 * a)), Step(Y, self.both(2 * a, 2 * b))]
        x, y = self.arrived
        if self.at == 1:
            self.x, self.y = x, y
            return [
                Step(Y, self.both(own + a, a) + (x._replace(start=x.start + a, rows=a),)),
                Step(X, self.both(own + 2 * a + b, b) + (y._replace(start=y.start + b, rows=b),)),
            ]
        if self.at == 2:
            sums = [
                self.both(own, a) + (self.x._replace(rows=a), x),
                self.both(own + 2 * a, b) + (self.y._replace(rows=b), y),
            ]
            return [
                Step(channel, tuple(piece.halved(half) for piece in each))
                for channel, half in ((PAIR, 1), (None, 0))
                for each in sums
            ]
        if self.at == 3:
            return [Step(PAIRS, (self.sent[2], x)), Step(PAIRS, (self.sent[3], y))]
        return [Step(PAIR, (self.sent[0], x)), Step(PAIR, (self.sent[1], y))]

    def take(self, pieces):
        self.sent = [piece[0] for piece in pieces]
        self.arrived = [piece[1] for piece in pieces[:2]]
        self.at += 1

    def parts(self, own, other):
        done = []
        for z_other, pieces in enumerate((self.sent, self.arrived)):
            start = 0
            for piece in pieces:
                for c_other, arrays in enumerate((own, other)):
                    done.append((piece._replace(array=arrays[z_other]), c_other, z_other, start))
                start += piece.rows
        return done

    @property
    def rows(self):
        return self.first + self.rest


def advance(name, ids, flows, extra=(), after=(), weight=1):
    steps, counts = [], []
    for flow in flows:
        own = flow.next_steps()
        counts.append(len(own))
        steps += own
    steps += list(extra)
    pieces, arrays = boundary(name, ids, steps, after, weight)
    for flow, n in zip(flows, counts):
        flow.take(pieces[:n])
        pieces = pieces[n:]
    return pieces, arrays


def cross_cores(flows):
    own = (flows[0].sent[0].array, flows[0].arrived[0].array)
    return own, tuple(swap(array, "rows", 1) for array in own)


def cross_both(flows):
    formed = flows[0].sent[0].array
    return (formed, flows[0].arrived[0].array), (swap(formed, "rows", 1), swap(formed, "rows", 3))


def finish_units(name, ids, groups, outs, old, returns=(), vectors=None, after=()):
    parts = [part for _, group, _ in groups for part in group]
    back = [block for _, blocks in returns for block in blocks]
    arrays = distinct([part[0].array for part in parts] + [block.array for block in back])
    kept, names = list(old), list(outs)
    vector_outs = [outs[each] for each in vectors or ()]
    d = HEADS * HEAD_DIM

    def kernel(ids_ref, *refs):
        refs = list(refs)

        def take(count):
            taken = refs[:count]
            del refs[:count]
            return taken

        inputs = take(len(arrays))
        take(len(kept) + len(after))
        results = dict(zip(names, take(len(names))))
        scratch, back_in = take(len(parts)), take(len(back))
        units, back_out, vec_out = take(len(groups)), take(len(returns)), take(len(vector_outs))
        copies = Copies(refs[0])
        me, core, place = ids_ref[0], ids_ref[1], ids_ref[2]

        def bring(piece, target):
            return copies.start(piece.origin(inputs[where_in(arrays, piece.array)], place), target)

        coming = [bring(part[0], target) for part, target in zip(parts, scratch)]
        blocks_coming = [bring(block, target) for block, target in zip(back, back_in)]
        slot = 0
        for (_, group, goals), unit in zip(groups, units):
            for piece, c_other, z_other, start in group:
                coming[slot].wait()
                side, rows = jnp.bitwise_xor(core, c_other), slice(start, start + piece.rows)
                if piece.lanes == d:
                    unit[side, rows, :] = scratch[slot][...].astype(WIDE)
                else:
                    offset = pl.multiple_of(jnp.bitwise_xor(place, z_other) * piece.lanes, piece.lanes)
                    unit[side, rows, pl.ds(offset, piece.lanes)] = scratch[slot][...].astype(WIDE)
                slot += 1
            for half, start, rows, output, index in goals:
                copies.leave(unit.at[half, start : start + rows], results[output].at[index])
        if vectors:
            last = groups[-1][0]
            top, low = units[-1][0, last - 16 : last, :], units[-1][1, last - 16 : last, :]
            stages = [top[0:8, i * LANES : (i + 1) * LANES] for i in range(4)] + [low[0:8, 0:LANES]]
            enc_s, enc_f, dec_s, crs, dec_f = stages
            gains, biases, ups, embed = vec_out
            for row, part in enumerate(stages):
                gains[row : row + 1, :] = part[0:1]
                biases[11 + row : 12 + row, :] = part[1:2]
            order = ((enc_s, 3), (enc_s, 4), (enc_s, 2), (enc_f, 2), (dec_s, 3), (dec_s, 4), (dec_s, 2))
            order += ((crs, 3), (crs, 4), (crs, 2), (dec_f, 2))
            for row, (part, at) in enumerate(order):
                biases[row : row + 1, :] = part[at : at + 1]
            ups[...] = low[8:10, :]
            embed[...] = dec_s[5:6]
            for output, buffer in zip(vectors, vec_out):
                copies.leave(buffer, results[output])
        slot = 0
        for (output, blocks), buffer in zip(returns, back_out):
            for block in range(len(blocks)):
                blocks_coming[slot].wait()
                buffer[jnp.bitwise_xor(me, block)] = back_in[slot][...].astype(buffer.dtype)
                slot += 1
            copies.leave(buffer, results[output])
        copies.finish()

    sems = len(parts) + len(back) + sum(len(goals) for _, _, goals in groups) + len(returns) + len(vector_outs)
    given = pl.pallas_call(
        kernel,
        name=name,
        out_shape=[outs[each] for each in names],
        in_specs=[SMEM] + [HBM] * (len(arrays) + len(kept) + len(after)),
        out_specs=[HBM] * len(names),
        scratch_shapes=[pltpu.VMEM((part[0].rows, part[0].lanes), LOW) for part in parts]
        + [pltpu.VMEM((block.rows, block.lanes), LOW) for block in back]
        + [pltpu.VMEM((2, rows, d), WIDE) for rows, _, _ in groups]
        + [pltpu.VMEM(outs[output].shape, outs[output].dtype) for output, _ in returns]
        + [pltpu.VMEM(each.shape, each.dtype) for each in vector_outs]
        + [pltpu.SemaphoreType.DMA((sems,))],
        input_output_aliases={1 + len(arrays) + i: names.index(each) for i, each in enumerate(kept)},
        compiler_params=parameters(),
        cost_estimate=cost(MIX_COST, 0),
    )(ids, *arrays, *[old[each] for each in kept], *after)
    return types.SimpleNamespace(**dict(zip(names, given)))


def by_rows(
    enc_input,
    dec_input,
    src_lengths,
    tgt_lengths,
    masked,
    cotangent,
    self_qkv,
    attn_out,
    cross_q,
    cross_kv,
    ffn_up,
    ffn_down,
    norm_gain,
    biases,
    up_bias,
    mask_embed,
):
    count, length, d = enc_input.shape
    tokens, ff = count * length, ffn_up.shape[2]
    me = lax.axis_index("seq")
    row = lax.axis_index("rows")
    ids = jnp.stack([me, row % 2, row // 2 % 2]).astype(jnp.int32)
    enc_others = spread_rows(enc_input, me)
    packed = pack_rows(ids, dec_input, cotangent, masked)
    packs = [swap(packed[away], "seq", away) for away in range(1, count)]
    embed = mask_embed.reshape(1, d)
    head_shape = (HEADS, HEAD_DIM, tokens)
    low_tokens, wide_tokens = shape_of((tokens, d), LOW), shape_of((tokens, d), WIDE)
    low_t, low_heads, low_ff = shape_of((d, tokens), LOW), shape_of(head_shape, LOW), shape_of((tokens, ff), LOW)
    exps, inverse = shape_of((HEADS, tokens, tokens), LOW), shape_of((HEADS, 8, tokens), WIDE)
    scale, vec = shape_of((tokens, LANES), WIDE), shape_of((8, d), WIDE)
    bias, scores = shape_of((tokens, tokens), WIDE), shape_of((3, tokens, tokens), WIDE)
    scalars = dict(ids=ids, src=src_lengths, tgt=tgt_lengths)
    step = dict(ids=ids)
    small = dict(biases=whole(biases), gains=whole(norm_gain))
    dense, score = 2 * tokens * d * d, 2 * tokens * tokens * d
    mask_pieces = [(packed[0], None, (0,))]
    for i, array in enumerate(packs, 1):
        mask_pieces.append((array, lambda s: (slice(2 * length, 2 * length + 16),), (i,)))
    mask_part = ((count, 16, d), LOW, mask_pieces)

    def tokens_of(local, others, start=0):
        return ((tokens, d), LOW, token_pieces(local, others, length, start))

    def halves(rows):
        return [shape_of((count * rows, d), LOW)] * 2

    enc = run_stage(
        "encoder_forward",
        functools.partial(encoder_forward, length),
        scalars,
        [dict(
            x=tokens_of(enc_input, enc_others),
            **small,
            qkv=layer(self_qkv, 0),
            proj=layer(attn_out, 0),
            up_bias=whole(up_bias),
            up=layer(ffn_up, 0),
            down=layer(ffn_down, 0),
        )],
        dict(
            x_t=low_t,
            q=low_heads,
            k=low_heads,
            v=low_heads,
            exps=exps,
            inverse=inverse,
            context=low_heads,
            hat0=low_tokens,
            scale0=scale,
            low1=low_tokens,
            act1=low_ff,
            slope1=low_ff,
            hat1=low_tokens,
            scale1=scale,
            memory_t=low_t,
        ),
        dict(bias=bias, scores=scores),
        12 * dense + 2 * score,
        24e6,
        after=packed[1:],
    )
    attention_work = dict(
        context_grad=shape_of(head_shape, WIDE),
        dq=low_heads,
        dk=low_heads,
        dv=low_heads,
        sums=shape_of((2, HEADS, HEAD_DIM, LANES), WIDE),
    )
    dec = run_stage(
        "decoder",
        functools.partial(decoder, length),
        scalars,
        [dict(
            **small,
            mask=mask_part,
            x=tokens_of(dec_input, packs),
            embed=whole(embed),
            qkv=layer(self_qkv, 1),
            proj1=layer(attn_out, 1),
            cross_q=whole(cross_q),
            memory_t=whole(enc.memory_t),
            cross_kv=whole(cross_kv),
            proj2=layer(attn_out, 2),
            up_bias=whole(up_bias),
            up=layer(ffn_up, 1),
            down=layer(ffn_down, 1),
            cotangent=tokens_of(cotangent, packs, length),
        )],
        dict(
            x_t=low_t,
            q2=low_heads,
            k2=low_heads,
            v2=low_heads,
            exps2=exps,
            inverse2=inverse,
            context2=low_heads,
            hat2=low_tokens,
            scale2=scale,
            final=[shape_of((length, d), LOW)] * count,
            vec=vec,
            vec_cross=vec,
            grads=halves(4 * LANES),
            grads_cross=halves(2 * LANES),
            memory_grad=wide_tokens,
            hidden_grad=wide_tokens,
        ),
        dict(
            bias=bias,
            scores=scores,
            low=low_tokens,
            act=low_ff,
            slope=low_ff,
            pre=low_ff,
            hidden_t=low_t,
            hat=wide_tokens,
            scale=scale,
            q=low_heads,
            k=low_heads,
            v=low_heads,
            exps=exps,
            inverse=inverse,
            context=low_heads,
            **attention_work,
        ),
        40 * dense + 8 * score,
        50e6,
    )

    def attention_parts(context, inverse, q, k, v, exps):
        return dict(
            context=whole(context),
            inverse=whole(inverse),
            q=whole(q),
            k=whole(k),
            v=whole(v),
            exps=whole(exps),
        )

    final_back = [swap(dec.final[i], "seq", i) for i in range(1, count)]
    flow_ffn, flow_cross = Flow(dec.grads, 2 * LANES, 2 * LANES), Flow(dec.grads_cross, LANES, LANES)
    first_flows = [flow_ffn, flow_cross]

    def self_stage(name, norm_row, last, grad, hat, scale, attention, x_t, index, more, after):
        rows = 2 * LANES + (16 if last else 0)
        return run_stage(
            name,
            functools.partial(self_backward, norm_row, last),
            step,
            [dict(
                gains=whole(norm_gain),
                grad=whole(grad),
                hat=whole(hat),
                scale=whole(scale),
                proj=layer(attn_out, index),
                **attention_parts(*attention),
                x_t=whole(x_t),
                qkv=layer(self_qkv, index),
                **more,
            )],
            dict(input_grad=low_tokens, grads=halves(rows), **({} if last else dict(vec=vec))),
            dict(vec=vec, **attention_work),
            8 * dense + 4 * score,
            20e6,
            after,
        )

    enc_ffn = run_stage(
        "encoder_ffn_backward",
        encoder_ffn_backward,
        step,
        [dict(
            gains=whole(norm_gain),
            grad=whole(dec.memory_grad),
            hat=whole(enc.hat1),
            scale=whole(enc.scale1),
            down=layer(ffn_down, 0),
            slope=whole(enc.slope1),
            act=whole(enc.act1),
            low=whole(enc.low1),
            up=layer(ffn_up, 0),
        )],
        dict(vec=vec, grad1=wide_tokens, grads=halves(4 * LANES)),
        dict(pre=low_ff),
        16 * dense,
        18e6,
    )
    flow_enc = Flow(enc_ffn.grads, 2 * LANES, 2 * LANES)
    _, formed = advance("first_xy", ids, first_flows, after=[enc_ffn.vec] + final_back, weight=BIG_WEIGHT)
    _, formed = advance("encoder_ffn_xy", ids, [flow_enc], after=formed)
    dec_self = self_stage(
        "decoder_self_backward",
        2,
        False,
        dec.hidden_grad,
        dec.hat2,
        dec.scale2,
        (dec.context2, dec.inverse2, dec.q2, dec.k2, dec.v2, dec.exps2),
        dec.x_t,
        1,
        dict(mask=mask_part),
        formed,
    )
    flow_dec = Flow(dec_self.grads, LANES, LANES)
    _, formed = advance("first_yx", ids, first_flows, after=[dec_self.vec], weight=BIG_WEIGHT)
    dec_blocks = [Piece(dec_self.input_grad, i * length, length) for i in range(count)]

    def sent_back(blocks):
        return [Step(channel, (blocks[i],)) for i, channel in ((1, X), (2, Y), (3, X))]

    def forwarded(pieces):
        return [Step(Y, (pieces[2][1],))]

    def came_back(blocks, pieces):
        return [blocks[0]] + [pieces[i][1] for i in (0, 1, 3)]

    _, formed = advance("decoder_self_xy", ids, [flow_dec], after=formed)
    enc_self = self_stage(
        "encoder_self_backward",
        0,
        True,
        enc_ffn.grad1,
        enc.hat0,
        enc.scale0,
        (enc.context, enc.inverse, enc.q, enc.k, enc.v, enc.exps),
        enc.x_t,
        0,
        dict(
            vec_enc=whole(enc_ffn.vec),
            vec_self=whole(dec_self.vec),
            vec_cross=whole(dec.vec_cross),
            vec_dec=whole(dec.vec),
        ),
        formed,
    )
    flow_last = Flow(enc_self.grads, LANES, LANES + 16)
    next_flows = [flow_enc, flow_dec]
    four = first_flows + next_flows
    enc_blocks = [Piece(enc_self.input_grad, i * length, length) for i in range(count)]


    def arrivals(pieces):
        return [piece[1].array for piece in pieces]

    _, formed = advance("four_one", ids, four, after=[enc_self.input_grad], weight=BIG_WEIGHT)
    _, formed = advance("last_xy", ids, [flow_last], after=formed)
    _, formed = advance("four_two", ids, four, after=formed)
    back, formed = advance("last_yx", ids, [flow_last], sent_back(dec_blocks) + sent_back(enc_blocks), after=formed)
    dec_back, enc_back = back[:3], back[3:]
    _, formed = advance("four_three", ids, four, after=formed)
    first_done = cross_cores(first_flows)
    back, formed = advance("last_pair", ids, [flow_last], forwarded(dec_back) + forwarded(enc_back), after=formed)
    dec_back, enc_back = dec_back + back[:1], enc_back + back[1:]
    _, formed = advance("next_four", ids, next_flows, after=formed)
    next_done = cross_cores(next_flows)
    _, formed = advance("last_pairs", ids, [flow_last], after=formed + arrivals(back))
    _, formed = advance("last_back", ids, [flow_last], after=formed)
    last_done = cross_both([flow_last])
    half = 2 * LANES

    def ffn_targets(index):
        goals = []
        for side in (0, 1):
            for unit in (0, 1):
                j = side * 2 + unit
                goals.append((side, unit * LANES, LANES, "up", (index, slice(None), slice(j * d, (j + 1) * d))))
            goals.append((side, half, half, "down", (index, slice(side * half, (side + 1) * half))))
        return goals

    def self_targets(index):
        goals = [(0, 0, LANES, "proj", (index,))]
        for j, (side, unit) in enumerate(((0, 1), (1, 0), (1, 1))):
            goals.append((side, unit * LANES, LANES, "qkv", (index, slice(None), slice(j * d, (j + 1) * d))))
        return goals

    cross_targets = [
        (0, 0, LANES, "proj", (2,)),
        (0, LANES, LANES, "cross_q", (slice(None),)),
        (1, 0, LANES, "cross_kv", (slice(None), slice(0, d))),
        (1, LANES, LANES, "cross_kv", (slice(None), slice(d, 2 * d))),
    ]
    local_rows = (count, length, d)
    up_down = dict(up=shape_of((2, LANES, ff), WIDE), down=shape_of((2, d, d), WIDE))
    proj = shape_of((3, LANES, d), WIDE)
    proj_qkv = dict(proj=proj, qkv=shape_of((2, LANES, 3 * d), WIDE))
    first = finish_units(
        "finish_four",
        ids,
        [
            (flow_ffn.rows, flow_ffn.parts(*first_done), ffn_targets(1)),
            (flow_cross.rows, flow_cross.parts(*first_done), cross_targets),
            (flow_enc.rows, flow_enc.parts(*next_done), ffn_targets(0)),
            (flow_dec.rows, flow_dec.parts(*next_done), self_targets(1)),
        ],
        dict(
            final=shape_of(local_rows, LOW),
            dec_grad=shape_of(local_rows, WIDE),
            cross_q=shape_of((LANES, d), WIDE),
            cross_kv=shape_of((LANES, 2 * d), WIDE),
            **up_down,
            **proj_qkv,
        ),
        {},
        [
            ("final", [Piece(array, 0, length) for array in [dec.final[0]] + final_back]),
            ("dec_grad", came_back(dec_blocks, dec_back)),
        ],
        after=formed,
    )
    third = finish_units(
        "finish_last",
        ids,
        [(flow_last.rows, flow_last.parts(*last_done), self_targets(0))],
        dict(
            enc_grad=shape_of(local_rows, WIDE),
            gains=shape_of((5, LANES), WIDE),
            biases=shape_of((16, LANES), WIDE),
            ups=shape_of((2, d), WIDE),
            embed=shape_of((1, LANES), WIDE),
            **proj_qkv,
        ),
        dict(proj=first.proj, qkv=first.qkv),
        [("enc_grad", came_back(enc_blocks, enc_back))],
        ("gains", "biases", "ups", "embed"),
    )
    return (
        first.final,
        third.enc_grad,
        first.dec_grad,
        third.qkv,
        third.proj,
        first.cross_q,
        first.cross_kv,
        first.up,
        first.down,
        third.gains,
        third.biases,
        third.ups,
        third.embed.reshape(LANES),
    )


def fits_by_rows(mesh, enc_input, ffn_up):
    count, length = enc_input.shape[0], enc_input.shape[1]
    return (
        mesh.shape["seq"] == 4
        and count == 4
        and mesh.shape["rows"] == 8
        and length == LANES
        and ffn_up.shape[2] == count * ffn_up.shape[1]
        and enc_input.shape[2] == HEADS * HEAD_DIM == count * LANES
    )


def device_program(mesh, *arrays):
    if fits_by_rows(mesh, arrays[0], arrays[10]):
        return by_rows(*arrays)
    return local(*arrays)


def solution(mesh):
    return jax.shard_map(
        functools.partial(device_program, mesh),
        mesh=mesh,
        in_specs=(
            P("rows", "seq", None),
            P("rows", "seq", None),
            P("rows", None),
            P("rows", None),
            P("rows", "seq"),
            P("rows", "seq", None),
            P(),
            P(),
            P(),
            P(),
            P(),
            P(),
            P(),
            P(),
            P(),
            P(),
        ),
        out_specs=(
            P("rows", "seq", None),
            P("rows", "seq", None),
            P("rows", "seq", None),
            P(None, "seq", None),
            P(None, "seq", None),
            P("seq", None),
            P("seq", None),
            P(None, "seq", None),
            P(None, "seq", None),
            P(None, "seq"),
            P(None, "seq"),
            P(None, "seq"),
            P("seq"),
        ),
        check_vma=False,
    )
```

```python
import functools
import types
import typing

import jax
import jax.numpy as jnp
from jax import lax
from jax.experimental import pallas as pl
from jax.experimental.pallas import tpu as pltpu
from jax.sharding import PartitionSpec as P

D = 512
HEADS = 8
HEAD_DIM = 64


EPSILON = 1e-05
NEG_FILL = -1000000000.0
START_FILL = -1e30


def normalize(residual, scale_gain, offset):
    centred = residual - jnp.mean(residual, axis=-1, keepdims=True)
    spread = jnp.mean(centred * centred, axis=-1, keepdims=True)
    return centred * lax.rsqrt(spread + EPSILON) * scale_gain + offset


def gelu_exact(values):
    return jax.nn.gelu(values, approximate=False)


def segments(lengths, places):
    doc_ends = jnp.cumsum(lengths, axis=1)
    return jnp.sum((doc_ends[:, None, :] <= places[None, :, None]).astype(jnp.int32), axis=2)


def project(inputs, weight):
    return jnp.einsum("rsd,df->rsf", inputs, weight, preferred_element_type=jnp.float32)


def project_back(gradient, weight):
    return jnp.einsum("rsf,df->rsd", gradient, weight, preferred_element_type=jnp.float32)


def weight_grad(inputs, gradient):
    return jnp.einsum("rsd,rsf->df", inputs, gradient, preferred_element_type=jnp.float32)


def token_sum(gradient):
    return jnp.sum(gradient, axis=(0, 1))


def split_heads(tensor):
    return tensor.reshape(tensor.shape[:2] + (HEADS, HEAD_DIM))


def split_blocks(tensor, block_size):
    new_shape = (tensor.shape[0], tensor.shape[1] // block_size, block_size) + tensor.shape[2:]
    return jnp.swapaxes(tensor.reshape(new_shape), 0, 1)


def block_scores(query_heads, key_heads, query_seg, key_seg):
    scores = jnp.einsum(
        "rqhd,rkhd->rhqk", query_heads, key_heads, preferred_element_type=jnp.float32
    ) * HEAD_DIM ** (-0.5)
    allowed = query_seg[:, None, :, None] == key_seg[:, None, None, :]
    return jnp.where(allowed, scores, NEG_FILL)


def block_grads(
    query_heads, grad_heads, log_total, delta_rows, query_seg, key_heads, value_heads, key_seg
):
    scores = block_scores(query_heads, key_heads, query_seg, key_seg)
    probs = jnp.exp(scores - log_total[..., None])
    dprobs = jnp.einsum(
        "rqhd,rkhd->rhqk", grad_heads, value_heads, preferred_element_type=jnp.float32
    )
    dscores = (probs * (dprobs - delta_rows[..., None])).astype(jnp.bfloat16)
    scaling = HEAD_DIM ** (-0.5)
    query_part = (
        jnp.einsum("rhqk,rkhd->rqhd", dscores, key_heads, preferred_element_type=jnp.float32)
        * scaling
    )
    key_part = (
        jnp.einsum("rhqk,rqhd->rkhd", dscores, query_heads, preferred_element_type=jnp.float32)
        * scaling
    )
    value_part = jnp.einsum(
        "rhqk,rqhd->rkhd",
        probs.astype(jnp.bfloat16),
        grad_heads,
        preferred_element_type=jnp.float32,
    )
    return (query_part, key_part, value_part)


def start_state(row_count, length):
    return (
        jnp.full((row_count, HEADS, length), START_FILL, jnp.float32),
        jnp.zeros((row_count, HEADS, length), jnp.float32),
        jnp.zeros((row_count, length, HEADS, HEAD_DIM), jnp.float32),
    )


def finish_state(state):
    running_max, running_sum, running_acc = state
    context = running_acc / jnp.swapaxes(running_sum, 1, 2)[..., None]
    return (
        context.reshape(context.shape[:2] + (HEADS * HEAD_DIM,)),
        running_max + jnp.log(running_sum),
    )


def absorber(query_heads, query_seg, key_lengths, length):

    def absorb(carried, piece_pair, first_pos):
        key_piece, value_piece = piece_pair
        piece_len = key_piece.shape[1]
        seg_piece = segments(key_lengths, jnp.arange(piece_len, dtype=jnp.int32))

        def advance(running, inputs):
            running_max, running_sum, running_acc = running
            key_block, value_block, seg_block = inputs
            scores = block_scores(query_heads, key_block, query_seg, seg_block)
            new_max = jnp.maximum(running_max, jnp.max(scores, axis=-1))
            factor = jnp.exp(running_max - new_max)
            exp_scores = jnp.exp(scores - new_max[..., None])
            running_sum = running_sum * factor + jnp.sum(exp_scores, axis=-1)
            running_acc = running_acc * jnp.swapaxes(factor, 1, 2)[..., None] + jnp.einsum(
                "rhqk,rkhd->rqhd",
                exp_scores.astype(jnp.bfloat16),
                value_block,
                preferred_element_type=jnp.float32,
            )
            return ((new_max, running_sum, running_acc), None)

        blocks = (
            split_blocks(split_heads(key_piece), length),
            split_blocks(split_heads(value_piece), length),
            split_blocks(seg_piece, length),
        )
        result, unused = lax.scan(advance, carried, blocks)
        return result

    return absorb


def attend_forward(queries, keys, values, query_seg, key_lengths):
    row_count, length = (queries.shape[0], queries.shape[1])
    query_heads = split_heads(queries)
    absorb = absorber(query_heads, query_seg, key_lengths, length)
    state = absorb(
        start_state(row_count, length),
        (
            lax.all_gather(keys, "seq", axis=1, tiled=True),
            lax.all_gather(values, "seq", axis=1, tiled=True),
        ),
        jnp.int32(0),
    )
    context, log_total = finish_state(state)
    return (context, log_total, None)


def attend_backward(
    queries,
    keys,
    values,
    query_seg,
    key_seg,
    query_lengths,
    key_lengths,
    context,
    log_total,
    context_grad,
):
    row_count, length = (queries.shape[0], queries.shape[1])
    grad_low = context_grad.astype(jnp.bfloat16)
    query_heads = split_heads(queries)
    grad_heads = split_heads(grad_low)
    delta_rows = jnp.swapaxes(
        jnp.sum(grad_heads.astype(jnp.float32) * split_heads(context), axis=-1), 1, 2
    )
    zero_heads = jnp.zeros((row_count, length, HEADS, HEAD_DIM), jnp.float32)
    key_piece = lax.all_gather(keys, "seq", axis=1, tiled=True)
    value_piece = lax.all_gather(values, "seq", axis=1, tiled=True)
    piece_len = key_piece.shape[1]
    block_size = length
    seg_piece = segments(key_lengths, jnp.arange(piece_len, dtype=jnp.int32))

    def advance(running, inputs):
        key_block, value_block, seg_block = inputs
        query_part, unused_keys, unused_values = block_grads(
            query_heads,
            grad_heads,
            log_total,
            delta_rows,
            query_seg,
            key_block,
            value_block,
            seg_block,
        )
        return (running + query_part, None)

    blocks = (
        split_blocks(split_heads(key_piece), block_size),
        split_blocks(split_heads(value_piece), block_size),
        split_blocks(seg_piece, block_size),
    )
    result, unused = lax.scan(advance, zero_heads, blocks)
    query_grad = result
    total_all, delta_all = (
        lax.all_gather(log_total, "seq", axis=2, tiled=True),
        lax.all_gather(delta_rows, "seq", axis=2, tiled=True),
    )
    key_heads = split_heads(keys)
    value_heads = split_heads(values)
    query_piece = lax.all_gather(queries, "seq", axis=1, tiled=True)
    grad_piece = lax.all_gather(grad_low, "seq", axis=1, tiled=True)
    piece_len = query_piece.shape[1]
    block_size = length
    seg_piece = segments(query_lengths, jnp.arange(piece_len, dtype=jnp.int32))
    offsets = jnp.arange(piece_len // block_size, dtype=jnp.int32) * block_size

    def advance(running, inputs):
        query_block, grad_block, seg_block, offset = inputs
        total_block = lax.dynamic_slice_in_dim(total_all, offset, block_size, 2)
        delta_block = lax.dynamic_slice_in_dim(delta_all, offset, block_size, 2)
        unused_query, key_part, value_part = block_grads(
            query_block,
            grad_block,
            total_block,
            delta_block,
            seg_block,
            key_heads,
            value_heads,
            key_seg,
        )
        return ((running[0] + key_part, running[1] + value_part), None)

    blocks = (
        split_blocks(split_heads(query_piece), block_size),
        split_blocks(split_heads(grad_piece), block_size),
        split_blocks(seg_piece, block_size),
        offsets,
    )
    result, unused = lax.scan(advance, (zero_heads, zero_heads), blocks)
    key_grad, value_grad = result
    return (
        query_grad.reshape(queries.shape),
        key_grad.reshape(queries.shape),
        value_grad.reshape(queries.shape),
    )


def self_forward(inputs_low, w_qkv, bias_q, bias_v, segment, lengths):
    projected = project(inputs_low, w_qkv)
    queries = (projected[..., :D] + bias_q).astype(jnp.bfloat16)
    keys = projected[..., D : 2 * D].astype(jnp.bfloat16)
    values = (projected[..., 2 * D :] + bias_v).astype(jnp.bfloat16)
    context, log_total, stored = attend_forward(queries, keys, values, segment, lengths)
    return (queries, keys, values, context, log_total, stored)


def ffn_forward(hidden, w_up, bias_up, w_down, bias_down):
    hidden_low = hidden.astype(jnp.bfloat16)
    pre_act = project(hidden_low, w_up) + bias_up
    activated, act_back = jax.vjp(gelu_exact, pre_act)
    act_low = activated.astype(jnp.bfloat16)
    return (project(act_low, w_down) + bias_down, (hidden_low, act_low, act_back))


def ffn_backward(out_grad, stored, w_up, w_down):
    hidden_low, act_low, act_back = stored
    out_low = out_grad.astype(jnp.bfloat16)
    down_grad = weight_grad(act_low, out_low)
    (pre_grad,) = act_back(project_back(out_low, w_down))
    pre_low = pre_grad.astype(jnp.bfloat16)
    up_grad = weight_grad(hidden_low, pre_low)
    return (
        project_back(pre_low, w_up),
        up_grad,
        token_sum(pre_grad),
        down_grad,
        token_sum(out_grad),
    )


def local(
    enc_input,
    dec_input,
    src_lengths,
    tgt_lengths,
    masked,
    cotangent,
    self_qkv,
    attn_out,
    cross_q,
    cross_kv,
    ffn_up,
    ffn_down,
    norm_gain,
    biases,
    up_bias,
    mask_embed,
):
    length = enc_input.shape[1]
    places = lax.axis_index("seq") * length + jnp.arange(length, dtype=jnp.int32)
    src_seg = segments(src_lengths, places)
    tgt_seg = segments(tgt_lengths, places)
    mask_float = masked.astype(jnp.float32)[..., None]
    enc_queries, enc_keys, enc_values, enc_context, enc_total, enc_stored = self_forward(
        enc_input, self_qkv[0], biases[0], biases[1], src_seg, src_lengths
    )
    enc_ctx_low = enc_context.astype(jnp.bfloat16)
    enc_resid = enc_input.astype(jnp.float32) + project(enc_ctx_low, attn_out[0]) + biases[2]
    enc_hidden, enc_norm_back = jax.vjp(normalize, enc_resid, norm_gain[0], biases[11])
    enc_ffn, enc_kept = ffn_forward(enc_hidden, ffn_up[0], up_bias[0], ffn_down[0], biases[3])
    memory, memory_back = jax.vjp(normalize, enc_hidden + enc_ffn, norm_gain[1], biases[12])
    memory_low = memory.astype(jnp.bfloat16)
    dec_inputs = dec_input.astype(jnp.float32) + mask_float * mask_embed
    dec_low = dec_inputs.astype(jnp.bfloat16)
    dec_queries, dec_keys, dec_values, dec_context, dec_total, dec_stored = self_forward(
        dec_low, self_qkv[1], biases[4], biases[5], tgt_seg, tgt_lengths
    )
    dec_ctx_low = dec_context.astype(jnp.bfloat16)
    dec_hidden, dec_norm_back = jax.vjp(
        normalize,
        dec_inputs + project(dec_ctx_low, attn_out[1]) + biases[6],
        norm_gain[2],
        biases[13],
    )
    dec_hidden_low = dec_hidden.astype(jnp.bfloat16)
    cross_queries = (project(dec_hidden_low, cross_q) + biases[7]).astype(jnp.bfloat16)
    cross_pair = project(memory_low, cross_kv)
    cross_keys = cross_pair[..., :D].astype(jnp.bfloat16)
    cross_values = (cross_pair[..., D:] + biases[8]).astype(jnp.bfloat16)
    cross_context, cross_total, cross_stored = attend_forward(
        cross_queries, cross_keys, cross_values, tgt_seg, src_lengths
    )
    cross_ctx_low = cross_context.astype(jnp.bfloat16)
    cross_hidden, cross_norm_back = jax.vjp(
        normalize,
        dec_hidden + project(cross_ctx_low, attn_out[2]) + biases[9],
        norm_gain[3],
        biases[14],
    )
    last_ffn, last_kept = ffn_forward(cross_hidden, ffn_up[1], up_bias[1], ffn_down[1], biases[10])
    final, final_back = jax.vjp(normalize, cross_hidden + last_ffn, norm_gain[4], biases[15])
    final_grad, gain_four, shift_four = final_back(cotangent.astype(jnp.float32))
    into_cross, up_grad_one, upb_grad_one, down_grad_one, bias_ten = ffn_backward(
        final_grad, last_kept, ffn_up[1], ffn_down[1]
    )
    cross_resid_grad, gain_three, shift_three = cross_norm_back(final_grad + into_cross)
    cross_out_low = cross_resid_grad.astype(jnp.bfloat16)
    out_grad_two = weight_grad(cross_ctx_low, cross_out_low)
    cross_q_part, cross_k_part, cross_v_part = attend_backward(
        cross_queries,
        cross_keys,
        cross_values,
        tgt_seg,
        src_seg,
        tgt_lengths,
        src_lengths,
        cross_context,
        cross_total,
        project_back(cross_out_low, attn_out[2]),
    )
    cross_q_low = cross_q_part.astype(jnp.bfloat16)
    cross_kv_low = jnp.concatenate([cross_k_part, cross_v_part], axis=-1).astype(jnp.bfloat16)
    cross_q_weight = weight_grad(dec_hidden_low, cross_q_low)
    cross_kv_weight = weight_grad(memory_low, cross_kv_low)
    memory_grad = project_back(cross_kv_low, cross_kv)
    dec_resid_grad, gain_two, shift_two = dec_norm_back(
        cross_resid_grad + project_back(cross_q_low, cross_q)
    )
    dec_out_low = dec_resid_grad.astype(jnp.bfloat16)
    out_grad_one = weight_grad(dec_ctx_low, dec_out_low)
    dec_q_part, dec_k_part, dec_v_part = attend_backward(
        dec_queries,
        dec_keys,
        dec_values,
        tgt_seg,
        tgt_seg,
        tgt_lengths,
        tgt_lengths,
        dec_context,
        dec_total,
        project_back(dec_out_low, attn_out[1]),
    )
    dec_qkv_low = jnp.concatenate([dec_q_part, dec_k_part, dec_v_part], axis=-1).astype(
        jnp.bfloat16
    )
    qkv_grad_one = weight_grad(dec_low, dec_qkv_low)
    dec_input_grad = dec_resid_grad + project_back(dec_qkv_low, self_qkv[1])
    mask_grad = jnp.sum(dec_input_grad * mask_float, axis=(0, 1))
    memory_resid_grad, gain_one, shift_one = memory_back(memory_grad)
    into_enc, up_grad_zero, upb_grad_zero, down_grad_zero, bias_three = ffn_backward(
        memory_resid_grad, enc_kept, ffn_up[0], ffn_down[0]
    )
    enc_resid_grad, gain_zero, shift_zero = enc_norm_back(memory_resid_grad + into_enc)
    enc_out_low = enc_resid_grad.astype(jnp.bfloat16)
    out_grad_zero = weight_grad(enc_ctx_low, enc_out_low)
    enc_q_part, enc_k_part, enc_v_part = attend_backward(
        enc_queries,
        enc_keys,
        enc_values,
        src_seg,
        src_seg,
        src_lengths,
        src_lengths,
        enc_context,
        enc_total,
        project_back(enc_out_low, attn_out[0]),
    )
    enc_qkv_low = jnp.concatenate([enc_q_part, enc_k_part, enc_v_part], axis=-1).astype(
        jnp.bfloat16
    )
    qkv_grad_zero = weight_grad(enc_input, enc_qkv_low)
    enc_input_grad = enc_resid_grad + project_back(enc_qkv_low, self_qkv[0])
    bias_rows = jnp.stack(
        [
            token_sum(enc_q_part),
            token_sum(enc_v_part),
            token_sum(enc_resid_grad),
            bias_three,
            token_sum(dec_q_part),
            token_sum(dec_v_part),
            token_sum(dec_resid_grad),
            token_sum(cross_q_part),
            token_sum(cross_v_part),
            token_sum(cross_resid_grad),
            bias_ten,
            shift_zero,
            shift_one,
            shift_two,
            shift_three,
            shift_four,
        ]
    )
    shares = (
        lax.psum_scatter(
            jnp.stack([qkv_grad_zero, qkv_grad_one]), "seq", scatter_dimension=1, tiled=True
        ),
        lax.psum_scatter(
            jnp.stack([out_grad_zero, out_grad_one, out_grad_two]),
            "seq",
            scatter_dimension=1,
            tiled=True,
        ),
        lax.psum_scatter(cross_q_weight, "seq", scatter_dimension=0, tiled=True),
        lax.psum_scatter(cross_kv_weight, "seq", scatter_dimension=0, tiled=True),
        lax.psum_scatter(
            jnp.stack([up_grad_zero, up_grad_one]), "seq", scatter_dimension=1, tiled=True
        ),
        lax.psum_scatter(
            jnp.stack([down_grad_zero, down_grad_one]), "seq", scatter_dimension=1, tiled=True
        ),
        lax.psum_scatter(
            jnp.stack([gain_zero, gain_one, gain_two, gain_three, gain_four]),
            "seq",
            scatter_dimension=1,
            tiled=True,
        ),
        lax.psum_scatter(bias_rows, "seq", scatter_dimension=1, tiled=True),
        lax.psum_scatter(
            jnp.stack([upb_grad_zero, upb_grad_one]), "seq", scatter_dimension=1, tiled=True
        ),
        lax.psum_scatter(mask_grad, "seq", scatter_dimension=0, tiled=True),
    )
    totals = lax.psum(
        (
            shares[0],
            shares[1],
            shares[2],
            shares[3],
            shares[4],
            shares[5],
            shares[6],
            shares[7],
            shares[8],
            shares[9],
        ),
        "rows",
    )
    return (
        final.astype(jnp.bfloat16),
        enc_input_grad,
        dec_input_grad,
        totals[0],
        totals[1],
        totals[2],
        totals[3],
        totals[4],
        totals[5],
        totals[6],
        totals[7],
        totals[8],
        totals[9],
    )


LANES = 128
CHANNELS = 96
COST = 50
MIX_COST = 4e9
BIG_WEIGHT = 2e11 / MIX_COST
BIG_VMEM = 64 * 2**20
LOW = jnp.bfloat16
WIDE = jnp.float32
HBM = pl.BlockSpec(memory_space=pltpu.HBM)
SMEM = pl.BlockSpec(memory_space=pltpu.SMEM)


def shape_of(dims, dtype):
    return jax.ShapeDtypeStruct(tuple(dims), dtype)


def distinct(arrays):
    found = []
    for array in arrays:
        if not any(array is other for other in found):
            found.append(array)
    return found


def where_in(arrays, array):
    return [other is array for other in arrays].index(True)


def parameters():
    return pltpu.CompilerParams(vmem_limit_bytes=BIG_VMEM)


def cost(flops, moved):
    return pl.CostEstimate(flops=int(flops), bytes_accessed=int(moved), transcendentals=0)


class Copies:
    def __init__(self, sems):
        self.sems, self.used, self.leaving = sems, 0, []

    def start(self, source, target):
        moved = pltpu.make_async_copy(source, target, self.sems.at[self.used])
        self.used += 1
        moved.start()
        return moved

    def leave(self, source, target):
        self.leaving.append(self.start(source, target))

    def finish(self):
        for moved in self.leaving:
            moved.wait()


class Arrivals:
    def __init__(self, copies, refs, groups):
        self._copies, self._refs, self._groups, self._coming = copies, refs, groups, {}
        self.more()

    def more(self):
        for name, origin, target in self._groups.pop(0) if self._groups else ():
            self._coming.setdefault(name, []).append(self._copies.start(origin, target))

    def finish(self):
        while self._groups:
            self.more()
        for name in self._refs:
            getattr(self, name)

    def __getattr__(self, name):
        while name not in self._coming and any(name == move[0] for group in self._groups for move in group):
            self.more()
        for moved in self._coming.get(name, ()):
            moved.wait()
        self._coming[name] = []
        return self._refs[name]


class Stage(typing.NamedTuple):
    scalars: typing.Any
    use: typing.Any
    out: typing.Any
    work: typing.Any
    copies: typing.Any
    targets: typing.Any

    def push(self, *buffers):
        for buffer in buffers:
            self.push_part(buffer, ())

    def push_part(self, buffer, index):
        target = [result for ref, result in self.targets if ref is buffer][0]
        if isinstance(target, list):
            self.copies.leave(buffer.at[index], target[index[0]].at[index[1:]] if index[1:] else target[index[0]])
        else:
            self.copies.leave(buffer.at[index] if index else buffer, target.at[index] if index else target)


def run_stage(name, body, scalars, parts, outs, work, flops, moved, after=()):
    all_parts = {key: part for group in parts for key, part in group.items()}
    arrays = distinct([move[0] for part in all_parts.values() for move in part[2]])
    after = [array for array in distinct(after) if not any(array is other for other in arrays)]
    flat_outs, spots = [], {}
    for key, shape in outs.items():
        several = shape if isinstance(shape, list) else [shape]
        spots[key] = (len(flat_outs), len(several))
        flat_outs += several
    buffers = [shape_of((len(s),) + s[0].shape, s[0].dtype) if isinstance(s, list) else s for s in outs.values()]

    def kernel(*refs):
        refs = list(refs)

        def take(count):
            taken = refs[:count]
            del refs[:count]
            return taken

        scalar_refs = types.SimpleNamespace(**dict(zip(scalars, take(len(scalars)))))
        inputs = take(len(arrays))
        take(len(after))
        results = take(len(flat_outs))
        part_refs = dict(zip(all_parts, take(len(all_parts))))
        out_refs = dict(zip(outs, take(len(outs))))
        work_refs = dict(zip(work, take(len(work))))
        copies = Copies(refs[0])
        groups = []
        for wanted in parts:
            groups.append([])
            for key, part in wanted.items():
                for array, source, target in part[2]:
                    origin, place = inputs[where_in(arrays, array)], part_refs[key]
                    origin = origin if source is None else origin.at[source(scalar_refs)]
                    groups[-1].append((key, origin, place if target is None else place.at[target]))
        targets = []
        for key, (start, count) in spots.items():
            several = isinstance(outs[key], list)
            targets.append((out_refs[key], list(results[start : start + count]) if several else results[start]))
        use = Arrivals(copies, part_refs, groups)
        stage = Stage(
            scalar_refs, use, types.SimpleNamespace(**out_refs), types.SimpleNamespace(**work_refs), copies, targets
        )
        body(stage)
        use.finish()
        copies.finish()

    given = pl.pallas_call(
        kernel,
        name=name,
        out_shape=flat_outs,
        in_specs=[SMEM] * len(scalars) + [HBM] * (len(arrays) + len(after)),
        out_specs=[HBM] * len(flat_outs),
        scratch_shapes=[pltpu.VMEM(part[0], part[1]) for part in all_parts.values()]
        + [pltpu.VMEM(each.shape, each.dtype) for each in buffers]
        + [pltpu.VMEM(each.shape, each.dtype) for each in work.values()]
        + [pltpu.SemaphoreType.DMA((CHANNELS,))],
        compiler_params=parameters(),
        cost_estimate=cost(flops * COST, moved),
    )(*scalars.values(), *arrays, *after)
    found = {}
    for key, (start, count) in spots.items():
        found[key] = list(given[start : start + count]) if isinstance(outs[key], list) else given[start]
    return types.SimpleNamespace(**found)


def whole(array):
    return (tuple(array.shape), array.dtype, [(array, None, None)])


def layer(array, index):
    return (tuple(array.shape[1:]), array.dtype, [(array, lambda s: index, None)])


def dot_nn(a, b):
    return lax.dot_general(a, b, (((1,), (0,)), ((), ())), preferred_element_type=WIDE)


def dot_nt(a, b):
    return lax.dot_general(a, b, (((1,), (1,)), ((), ())), preferred_element_type=WIDE)


def dot_tn(a, b):
    return lax.dot_general(a, b, (((0,), (0,)), ((), ())), preferred_element_type=WIDE)


def total(values):
    return jnp.sum(values, axis=0, keepdims=True)


def norm_parts(residual):
    centred = residual - jnp.mean(residual, axis=-1, keepdims=True)
    scale = lax.rsqrt(jnp.mean(centred * centred, axis=-1, keepdims=True) + EPSILON)
    return centred * scale, scale


def norm_keep(stage, residual, gain, shift, hat_ref, scale_ref):
    hat, scale = norm_parts(residual)
    hat_ref[...] = hat.astype(LOW)
    scale_ref[...] = jnp.broadcast_to(scale, scale_ref.shape)
    stage.push(hat_ref, scale_ref)
    return hat * gain + shift


def norm_back(grad, hat, scale, gain):
    scaled = grad * gain
    inner = jnp.mean(scaled, axis=-1, keepdims=True)
    along = jnp.mean(scaled * hat, axis=-1, keepdims=True)
    return scale * (scaled - inner - hat * along), total(grad * hat), total(grad)


def segment_ids(lengths_ref, row, places):
    end = jnp.int32(0)
    found = jnp.zeros(places.shape, jnp.int32)
    for slot in range(lengths_ref.shape[1]):
        end = end + lengths_ref[row, slot]
        found = found + (end <= places).astype(jnp.int32)
    return found


def positions(me, length, shape, axis):
    token = lax.broadcasted_iota(jnp.int32, shape, axis)
    bits = length.bit_length() - 1
    block = lax.shift_right_logical(token, jnp.int32(bits))
    return lax.shift_left(jnp.bitwise_xor(block, me), jnp.int32(bits)) + jnp.bitwise_and(token, length - 1)


def fill_bias(bias_ref, query_lengths, key_lengths, me, length):
    tokens = bias_ref.shape[0]
    query_seg = segment_ids(query_lengths, me, positions(me, length, (1, tokens), 1))
    key_seg = segment_ids(key_lengths, me, positions(me, length, (tokens, 1), 0))
    bias_ref[...] = jnp.where(key_seg == query_seg, 0.0, NEG_FILL)


def heads_of(values):
    return values.reshape(HEADS, HEAD_DIM, values.shape[-1])


def flat(ref):
    return ref[...].reshape(HEADS * HEAD_DIM, ref.shape[-1])


def staggered(count, *steps):
    for i in range(count + len(steps) - 1):
        for lag, step in enumerate(steps):
            if 0 <= i - lag < count:
                step(i - lag)


def attention_forward(q_ref, k_ref, v_ref, bias_ref, exp_ref, inverse_ref, context_ref, score_ref):
    def form(head):
        score_ref[head % score_ref.shape[0]] = dot_tn(k_ref[head], q_ref[head]) + bias_ref[...]

    def exponentials(head):
        scores = score_ref[head % score_ref.shape[0]]
        exps = jnp.exp(scores - jnp.max(scores, axis=0, keepdims=True))
        exp_ref[head] = exps.astype(LOW)
        inverse_ref[head] = jnp.broadcast_to(1.0 / total(exps), inverse_ref.shape[1:])

    def contract(head):
        context_ref[head] = (dot_nn(v_ref[head], exp_ref[head]) * inverse_ref[head][0:1]).astype(LOW)

    staggered(HEADS, form, exponentials, contract)


def attention_backward(q_ref, k_ref, v_ref, exp_ref, inverse_ref, context_ref, work):
    for head in range(HEADS):
        exps = exp_ref[head]
        grad = (work.context_grad[head].astype(LOW).astype(WIDE) * inverse_ref[head][0:1]).astype(LOW)
        delta = total(grad.astype(WIDE) * context_ref[head].astype(WIDE))
        score_grad = (exps.astype(WIDE) * (dot_tn(v_ref[head], grad) - delta)).astype(LOW)
        dv = dot_nt(grad, exps)
        dq = dot_nn(k_ref[head], score_grad) * HEAD_DIM ** (-0.5)
        work.dv[head] = dv.astype(LOW)
        work.dk[head] = dot_nt(q_ref[head], score_grad).astype(LOW)
        work.dq[head] = dq.astype(LOW)
        wide = (HEAD_DIM, LANES)
        work.sums[0, head] = jnp.broadcast_to(jnp.sum(dq, axis=1, keepdims=True), wide)
        work.sums[1, head] = jnp.broadcast_to(jnp.sum(dv, axis=1, keepdims=True), wide)


def sum_row(sums_ref, which):
    return jnp.transpose(sums_ref[which].reshape(HEADS * HEAD_DIM, LANES))[0:1]


def qkv_forward(stage, weight, low_t, bias_t, q_col, v_col, q_ref, k_ref, v_ref):
    d = low_t.shape[0]
    queries = (dot_tn(weight[:, 0:d], low_t) + bias_t[:, q_col : q_col + 1]).astype(LOW)
    q_ref[...] = heads_of(queries * HEAD_DIM ** (-0.5))
    k_ref[...] = heads_of(dot_tn(weight[:, d : 2 * d], low_t).astype(LOW))
    v_ref[...] = heads_of((dot_tn(weight[:, 2 * d :], low_t) + bias_t[:, v_col : v_col + 1]).astype(LOW))
    stage.push(q_ref, k_ref, v_ref)


def gelu_parts(pre):
    half = 0.5 * (1.0 + lax.erf(pre * 0.5**0.5))
    density = jnp.exp(pre * pre * -0.5) * (0.5 / 3.141592653589793) ** 0.5
    return pre * half, half + pre * density


def feed_forward(low, up, up_bias, down, act_ref, slope_ref, pre_ref):
    width = low.shape[1]
    columns = [slice(j * width, (j + 1) * width) for j in range(act_ref.shape[1] // width)]

    def form(j):
        pre_ref[j % pre_ref.shape[0]] = dot_nn(low, up[:, columns[j]]) + up_bias[:, columns[j]]

    def activate(j):
        act, slope = gelu_parts(pre_ref[j % pre_ref.shape[0]])
        act_ref[:, columns[j]] = act.astype(LOW)
        slope_ref[:, columns[j]] = slope.astype(LOW)

    staggered(len(columns), form, activate)
    return dot_nn(act_ref[...], down[...])


class Halves(typing.NamedTuple):
    ref: typing.Any
    first: int
    rest: int
    me: typing.Any
    core: typing.Any
    stage: typing.Any

    def leave_regions(self, start, rows):
        for side in (0, 1):
            for begin in (start, start + 2 * (self.first + self.rest)):
                self.stage.push_part(self.ref, (side, slice(begin, begin + rows)))

    def leave_first(self, rows):
        self.leave_regions(0, 2 * self.first)

    def leave_rest(self, rows):
        self.leave_regions(2 * self.first, 2 * self.rest)

    def put(self, half, chunk, start, rows):
        away = jnp.bitwise_xor(self.me, chunk)
        low, high = jnp.bitwise_and(away, 1), lax.shift_right_logical(away, 1)
        both = 2 * (self.first + self.rest)
        if start < self.first:
            place = high * self.first + jnp.where(low == 1, 0, both) + start
        else:
            place = low * self.rest + jnp.where(high == 1, 0, both) + 2 * self.first + start - self.first
        side = jnp.bitwise_xor(self.core, half)
        self.ref[side, pl.ds(pl.multiple_of(place, 16), rows.shape[0])] = rows.astype(LOW)


def put_units(grads, block, half, unit):
    rows = LANES
    for chunk in range(block.shape[0] // rows):
        grads.put(half, chunk, unit * rows, block[chunk * rows : (chunk + 1) * rows])


def feed_back(out_grad, low, act, slope, up, down, vec_ref, vec_row, grads, pre_ref, more=None):
    width = out_grad.shape[1]
    half = width // 2
    out_low = out_grad.astype(LOW)
    columns = [slice(j * width, (j + 1) * width) for j in range(pre_ref.shape[1] // width)]
    for j, cols in enumerate(columns):
        pre = dot_nt(out_low, down[cols, :]) * slope[:, cols].astype(WIDE)
        vec_ref[vec_row + j : vec_row + j + 1, :] = total(pre)
        pre_ref[:, cols] = pre.astype(LOW)
        down_grad = dot_tn(act[:, cols], out_low)
        for r in range(2):
            grads.put(r, j, half, down_grad[r * half : (r + 1) * half])
    grads.leave_rest(half)
    low, up = low(), up()
    for j, cols in enumerate(columns):
        put_units(grads, dot_tn(low[...], pre_ref[:, cols]), j // 2, j % 2)
    grads.leave_first(half)
    return dot_nt(pre_ref[...], up[...])


def own_row(s):
    return s.ids[0]


def token_pieces(local, others, length, start=0):
    pieces = [(local, own_row, (slice(0, length),))]
    for d, array in enumerate(others, 1):
        pieces.append((array, lambda s: (slice(start, start + length),), (slice(d * length, (d + 1) * length),)))
    return pieces


def put_blocks(ref, values):
    for i in range(ref.shape[0]):
        ref[i] = values[i * ref.shape[1] : (i + 1) * ref.shape[1]]


def encoder_forward(length, stage):
    me, use, out = stage.scalars.ids[0], stage.use, stage.out
    fill_bias(stage.work.bias, stage.scalars.src, stage.scalars.src, me, length)
    x = use.x[...]
    x_t = jnp.transpose(x)
    out.x_t[...] = x_t
    stage.push(out.x_t)
    biases = use.biases[...]
    qkv = use.qkv
    use.more()
    qkv_forward(stage, qkv, x_t, jnp.transpose(biases), 0, 1, out.q, out.k, out.v)
    attention_forward(out.q, out.k, out.v, stage.work.bias, out.exps, out.inverse, out.context, stage.work.scores)
    stage.push(out.exps, out.inverse, out.context)
    gains = use.gains
    residual = x.astype(WIDE) + dot_tn(flat(out.context), use.proj[...]) + biases[2:3]
    hidden = norm_keep(stage, residual, gains[0:1], biases[11:12], out.hat0, out.scale0)
    hidden_low = hidden.astype(LOW)
    out.low1[...] = hidden_low
    stage.push(out.low1)
    ffn = feed_forward(hidden_low, use.up, use.up_bias[0:1], use.down, out.act1, out.slope1, stage.work.scores)
    stage.push(out.act1, out.slope1)
    memory = norm_keep(stage, hidden + ffn + biases[3:4], gains[1:2], biases[12:13], out.hat1, out.scale1)
    out.memory_t[...] = jnp.transpose(memory.astype(LOW))
    stage.push(out.memory_t)


def mask_columns(mask, d):
    row = jnp.concatenate([mask[i][0:1, 0:LANES].astype(WIDE) for i in range(mask.shape[0])], axis=1)
    columns = jnp.transpose(jnp.broadcast_to(row, (LANES, row.shape[1])))
    return jnp.concatenate([columns] * (d // LANES), axis=1)


def decoder(length, stage):
    me, use, out, work = stage.scalars.ids[0], stage.use, stage.out, stage.work
    biases = use.biases[...]
    bias_t = jnp.transpose(biases)
    gains = use.gains
    src, tgt = stage.scalars.src, stage.scalars.tgt
    fill_bias(work.bias, tgt, tgt, me, length)
    x = use.x[...].astype(WIDE)
    d = x.shape[1]
    y = x + mask_columns(use.mask, d) * use.embed[...]
    y_t = jnp.transpose(y.astype(LOW))
    out.x_t[...] = y_t
    stage.push(out.x_t)
    qkv = use.qkv
    use.more()
    qkv_forward(stage, qkv, y_t, bias_t, 4, 5, out.q2, out.k2, out.v2)
    use.more()
    attention_forward(out.q2, out.k2, out.v2, work.bias, out.exps2, out.inverse2, out.context2, work.scores)
    stage.push(out.exps2, out.inverse2, out.context2)
    residual = y + dot_tn(flat(out.context2), use.proj1[...]) + biases[6:7]
    hidden = norm_keep(stage, residual, gains[2:3], biases[13:14], out.hat2, out.scale2)
    hidden_t = jnp.transpose(hidden.astype(LOW))
    work.hidden_t[...] = hidden_t
    queries = (dot_tn(use.cross_q[...], hidden_t) + bias_t[:, 7:8]).astype(LOW)
    work.q[...] = heads_of(queries * HEAD_DIM ** (-0.5))
    memory_t = use.memory_t
    kv = use.cross_kv
    work.k[...] = heads_of(dot_tn(kv[:, 0:d], memory_t[...]).astype(LOW))
    work.v[...] = heads_of((dot_tn(kv[:, d:], memory_t[...]) + bias_t[:, 8:9]).astype(LOW))
    fill_bias(work.bias, tgt, src, me, length)
    attention_forward(work.q, work.k, work.v, work.bias, work.exps, work.inverse, work.context, work.scores)
    proj = use.proj2
    residual = hidden + dot_tn(flat(work.context), proj[...]) + biases[9:10]
    hat, scale = norm_parts(residual)
    work.hat[...] = hat
    work.scale[...] = jnp.broadcast_to(scale, work.scale.shape)
    hidden = hat * gains[3:4] + biases[14:15]
    work.low[...] = hidden.astype(LOW)
    up, down = use.up, use.down
    ffn = feed_forward(work.low[...], up, use.up_bias[1:2], down, work.act, work.slope, work.scores)
    hat, scale = norm_parts(hidden + ffn + biases[10:11])
    put_blocks(out.final, (hat * gains[4:5] + biases[15:16]).astype(LOW))
    for i in range(out.final.shape[0]):
        stage.push_part(out.final, (i,))
    vec, vec_cross = out.vec, out.vec_cross
    vec[...] = jnp.zeros_like(vec)
    vec_cross[...] = jnp.zeros_like(vec_cross)
    cotangent = use.cotangent[...].astype(WIDE)
    grad, vec[0:1, :], vec[1:2, :] = norm_back(cotangent, hat, scale, gains[4:5])
    vec[2:3, :] = total(grad)
    into = feed_back(
        grad,
        lambda: work.low,
        work.act,
        work.slope,
        lambda: up,
        down,
        vec,
        3,
        Halves(out.grads, 2 * LANES, 2 * LANES, me, stage.scalars.ids[1], stage),
        work.pre,
    )
    stage.push(vec)
    grads = Halves(out.grads_cross, LANES, LANES, me, stage.scalars.ids[1], stage)
    grad = out_backward(
        grad + into, work.hat[...], work.scale[:, 0:1], gains[3:4], proj, work.context, work, vec_cross, grads
    )
    attention_backward(work.q, work.k, work.v, work.exps, work.inverse, work.context, work)
    dq, dk, dv = attention_sums(work, vec_cross)
    stage.push(vec_cross)
    put_units(grads, dot_nt(work.hidden_t[...], dq), 0, 1)
    put_units(grads, dot_nt(memory_t[...], dk), 1, 0)
    put_units(grads, dot_nt(memory_t[...], dv), 1, 1)
    grads.leave_first(0)
    grads.leave_rest(0)
    out.memory_grad[...] = jnp.transpose(dot_nn(kv[:, 0:d], dk) + dot_nn(kv[:, d:], dv))
    stage.push(out.memory_grad)
    out.hidden_grad[...] = grad + jnp.transpose(dot_nn(use.cross_q[...], dq))
    stage.push(out.hidden_grad)


def out_backward(grad, hat, scale, gain, proj, context, work, vec, grads):
    grad, vec[0:1, :], vec[1:2, :] = norm_back(grad, hat, scale, gain)
    vec[2:3, :] = total(grad)
    low = grad.astype(LOW)
    work.context_grad[...] = heads_of(dot_nt(proj[...], low))
    put_units(grads, dot_nn(flat(context), low), 0, 0)
    return grad


def attention_sums(work, vec):
    vec[3:4, :] = sum_row(work.sums, 0)
    vec[4:5, :] = sum_row(work.sums, 1)
    return flat(work.dq), flat(work.dk), flat(work.dv)


def encoder_ffn_backward(stage):
    me, core = stage.scalars.ids[0], stage.scalars.ids[1]
    use, out = stage.use, stage.out
    vec = out.vec
    vec[...] = jnp.zeros_like(vec)
    hat, scale, grad = use.hat, use.scale, use.grad
    use.more()
    hat, scale = hat[...].astype(WIDE), scale[...][:, 0:1]
    grad, vec[0:1, :], vec[1:2, :] = norm_back(grad[...], hat, scale, use.gains[1:2])
    vec[2:3, :] = total(grad)
    grads = Halves(out.grads, 2 * LANES, 2 * LANES, me, core, stage)
    down, slope, act = use.down, use.slope, use.act
    use.more()
    into = feed_back(
        grad, lambda: use.low, act, slope, lambda: use.up, down, vec, 3, grads, stage.work.pre
    )
    stage.push(vec)
    out.grad1[...] = grad + into
    stage.push(out.grad1)


def put_vectors(grads, start, own, others):
    d = own.shape[1]
    for chunk in range(d // LANES):
        cols = slice(chunk * LANES, (chunk + 1) * LANES)
        first = jnp.concatenate([own[:, cols]] + [each[:, cols] for each in others[:3]], axis=1)
        first = jnp.concatenate([first, jnp.zeros_like(first)], axis=0)
        second = jnp.concatenate([others[3][:, cols], jnp.zeros((8, d - LANES), WIDE)], axis=1)
        ups = [each[3 + chunk : 4 + chunk] for each in (others[0], others[3])]
        second = jnp.concatenate([second] + ups + [jnp.zeros((6, d), WIDE)], axis=0)
        grads.put(0, chunk, start, first)
        grads.put(1, chunk, start, second)


def self_backward(norm_row, last, stage):
    me, core = stage.scalars.ids[0], stage.scalars.ids[1]
    use, out, work = stage.use, stage.out, stage.work
    vec = work.vec
    grads = Halves(out.grads, LANES, LANES + (16 if last else 0), me, core, stage)
    vec[...] = jnp.zeros_like(vec)
    hat, scale, grad, proj, context = use.hat, use.scale, use.grad, use.proj, use.context
    use.more()
    hat, scale = hat[...].astype(WIDE), scale[...][:, 0:1]
    gain = use.gains[norm_row : norm_row + 1]
    grad = out_backward(grad[...], hat, scale, gain, proj, context, work, vec, grads)
    q, k, v, exps, inverse = use.q, use.k, use.v, use.exps, use.inverse
    use.more()
    attention_backward(q, k, v, exps, inverse, context, work)
    dq, dk, dv = attention_sums(work, vec)
    x_t = use.x_t[...]
    put_units(grads, dot_nt(x_t, dk), 1, 0)
    grads.leave_first(0)
    put_units(grads, dot_nt(x_t, dq), 0, 1)
    put_units(grads, dot_nt(x_t, dv), 1, 1)
    if last:
        others = [each[...] for each in (use.vec_enc, use.vec_self, use.vec_cross, use.vec_dec)]
        put_vectors(grads, 2 * LANES, vec[...], others)
    grads.leave_rest(0)
    qkv = use.qkv
    d = x_t.shape[0]
    through = dot_nn(qkv[:, 0:d], dq) + dot_nn(qkv[:, d : 2 * d], dk) + dot_nn(qkv[:, 2 * d :], dv)
    input_grad = grad + jnp.transpose(through)
    if not last:
        vec[5:6, :] = total(input_grad * mask_columns(use.mask, d))
        out.vec[...] = vec[...]
        stage.push(out.vec)
    out.input_grad[...] = input_grad.astype(LOW)
    stage.push(out.input_grad)


def swap(array, axis_name, bit):
    size = lax.axis_size(axis_name)
    return lax.ppermute(array, axis_name, [(i, i ^ bit) for i in range(size)])


def spread_rows(local, me):
    return [
        swap(lax.dynamic_index_in_dim(local, me ^ d, 0, keepdims=False), "seq", d) for d in range(1, local.shape[0])
    ]


def pack_rows(ids, dec_input, cotangent, masked):
    count, length, d = dec_input.shape
    rows = 2 * length + 16

    def kernel(ids_ref, mask_ref, dec_ref, cot_ref, *refs):
        results, scratch, copies = refs[:count], refs[count], Copies(refs[count + 1])
        me = ids_ref[0]
        coming = []
        for away in range(1, count):
            row = jnp.bitwise_xor(me, away)
            coming.append(copies.start(dec_ref.at[row], scratch.at[away, 0:length]))
            coming.append(copies.start(cot_ref.at[row], scratch.at[away, length : 2 * length]))
        for away in range(count):
            row = mask_ref[jnp.bitwise_xor(me, away)].astype(WIDE).astype(LOW)
            row = jnp.concatenate([jnp.broadcast_to(row, (16, length))] * (d // length), axis=1)
            scratch[away, 2 * length : rows] = row
        copies.leave(scratch.at[0, 2 * length : rows], results[0])
        for away in range(1, count):
            coming[2 * away - 2].wait()
            coming[2 * away - 1].wait()
            copies.leave(scratch.at[away], results[away])
        copies.finish()

    return pl.pallas_call(
        kernel,
        name="pack_rows",
        out_shape=[shape_of((16, d), LOW)] + [shape_of((rows, d), LOW)] * (count - 1),
        in_specs=[SMEM, pl.BlockSpec(memory_space=pltpu.VMEM), HBM, HBM],
        out_specs=[HBM] * count,
        scratch_shapes=[pltpu.VMEM((count, rows, d), LOW), pltpu.SemaphoreType.DMA((3 * count,))],
        compiler_params=parameters(),
        cost_estimate=cost(0, 2e6),
    )(ids, masked.reshape(count, 1, length), dec_input, cotangent)


class Piece(typing.NamedTuple):
    array: typing.Any
    start: int
    rows: int
    half: int = -1

    def halved(self, half):
        return self._replace(half=half)

    @property
    def lanes(self):
        width = self.array.shape[-1]
        return width if self.half < 0 else width // 2

    def origin(self, ref, place):
        if self.half < 0:
            return ref.at[pl.ds(self.start, self.rows)]
        start = pl.multiple_of(jnp.bitwise_xor(place, self.half) * self.lanes, self.lanes)
        return ref.at[pl.ds(self.start, self.rows), pl.ds(start, self.lanes)]


class Step(typing.NamedTuple):
    channel: typing.Any
    sources: tuple


X, Y, DIAGONAL, PAIR, PAIRS = 0, 1, 2, 3, 4
CHANNEL = (("seq", 1), ("seq", 2), ("seq", 3), ("rows", 2), ("rows", 4))


def boundary(name, ids, steps, after=(), weight=1):
    arrays = distinct([piece.array for step in steps for piece in step.sources])
    after = [array for array in distinct(after) if not any(array is other for other in arrays)]
    outs, places = {}, []
    for step in steps:
        rows = step.sources[0].rows
        key = (step.channel, step.sources[0].lanes)
        start = outs.get(key, 0)
        outs[key] = start + rows
        places.append((key, start, rows))
    keys = list(outs)
    tally = sum(len(step.sources) for step in steps) + len(steps)

    def kernel(ids_ref, *refs):
        inputs, refs = refs[: len(arrays)], refs[len(arrays) + len(after) :]
        results, refs = dict(zip(keys, refs)), refs[len(keys) :]
        buffers, refs = dict(zip(keys, refs)), refs[len(keys) :]
        scratch, copies = list(refs[:-1]), Copies(refs[-1])
        coming = []
        for step in steps:
            for piece in step.sources:
                origin = piece.origin(inputs[where_in(arrays, piece.array)], ids_ref[2])
                coming.append((copies.start(origin, scratch[len(coming)]), scratch[len(coming)]))
        for step, (key, start, rows) in zip(steps, places):
            terms = []
            for _ in step.sources:
                moved, ref = coming.pop(0)
                moved.wait()
                terms.append(ref)
            rest = slice(start, start + rows)
            summed = functools.reduce(jnp.add, [term[...].astype(WIDE) for term in terms])
            buffers[key][rest, :] = summed.astype(LOW)
            copies.leave(buffers[key].at[rest], results[key].at[rest])
        copies.finish()

    shapes = [shape_of((outs[key], key[1]), LOW) for key in keys]
    given = pl.pallas_call(
        kernel,
        name=name,
        out_shape=shapes,
        in_specs=[SMEM] + [HBM] * (len(arrays) + len(after)),
        out_specs=[HBM] * len(keys),
        scratch_shapes=[pltpu.VMEM(each.shape, LOW) for each in shapes]
        + [pltpu.VMEM((piece.rows, piece.lanes), LOW) for step in steps for piece in step.sources]
        + [pltpu.SemaphoreType.DMA((tally,))],
        compiler_params=parameters(),
        cost_estimate=cost(MIX_COST * weight, 0),
    )(ids, *arrays, *after)
    formed = dict(zip(keys, given))
    arrived = {key: swap(formed[key], *CHANNEL[key[0]]) for key in keys if key[0] is not None}
    pieces = []
    for key, start, rows in places:
        mine = Piece(formed[key], start, rows)
        pieces.append((mine, mine._replace(array=arrived[key]) if key in arrived else None))
    return pieces, list(given)


class Flow:
    def __init__(self, grads, first, rest):
        keep, send = grads
        self.arrays = (keep, swap(send, "rows", 1))
        self.first, self.rest, self.at = first, rest, 0
        self.sent = self.arrived = None

    def both(self, start, rows):
        return tuple(Piece(array, start, rows) for array in self.arrays)

    def next_steps(self):
        a, b = self.first, self.rest
        own = 2 * (a + b)
        if self.at == 0:
            return [Step(X, self.both(0, 2 * a)), Step(Y, self.both(2 * a, 2 * b))]
        x, y = self.arrived
        if self.at == 1:
            self.x, self.y = x, y
            return [
                Step(Y, self.both(own + a, a) + (x._replace(start=x.start + a, rows=a),)),
                Step(X, self.both(own + 2 * a + b, b) + (y._replace(start=y.start + b, rows=b),)),
            ]
        if self.at == 2:
            sums = [
                self.both(own, a) + (self.x._replace(rows=a), x),
                self.both(own + 2 * a, b) + (self.y._replace(rows=b), y),
            ]
            return [
                Step(channel, tuple(piece.halved(half) for piece in each))
                for channel, half in ((PAIR, 1), (None, 0))
                for each in sums
            ]
        if self.at == 3:
            return [Step(PAIRS, (self.sent[2], x)), Step(PAIRS, (self.sent[3], y))]
        return [Step(PAIR, (self.sent[0], x)), Step(PAIR, (self.sent[1], y))]

    def take(self, pieces):
        self.sent = [piece[0] for piece in pieces]
        self.arrived = [piece[1] for piece in pieces[:2]]
        self.at += 1

    def parts(self, own, other):
        done = []
        for z_other, pieces in enumerate((self.sent, self.arrived)):
            start = 0
            for piece in pieces:
                for c_other, arrays in enumerate((own, other)):
                    done.append((piece._replace(array=arrays[z_other]), c_other, z_other, start))
                start += piece.rows
        return done

    @property
    def rows(self):
        return self.first + self.rest


def advance(name, ids, flows, extra=(), after=(), weight=1):
    steps, counts = [], []
    for flow in flows:
        own = flow.next_steps()
        counts.append(len(own))
        steps += own
    steps += list(extra)
    pieces, arrays = boundary(name, ids, steps, after, weight)
    for flow, n in zip(flows, counts):
        flow.take(pieces[:n])
        pieces = pieces[n:]
    return pieces, arrays


def cross_cores(flows):
    own = (flows[0].sent[0].array, flows[0].arrived[0].array)
    return own, tuple(swap(array, "rows", 1) for array in own)


def cross_both(flows):
    formed = flows[0].sent[0].array
    return (formed, flows[0].arrived[0].array), (swap(formed, "rows", 1), swap(formed, "rows", 3))


def finish_units(name, ids, groups, outs, old, returns=(), vectors=None, after=()):
    parts = [part for _, group, _ in groups for part in group]
    back = [block for _, blocks in returns for block in blocks]
    arrays = distinct([part[0].array for part in parts] + [block.array for block in back])
    kept, names = list(old), list(outs)
    vector_outs = [outs[each] for each in vectors or ()]
    d = HEADS * HEAD_DIM

    def kernel(ids_ref, *refs):
        refs = list(refs)

        def take(count):
            taken = refs[:count]
            del refs[:count]
            return taken

        inputs = take(len(arrays))
        take(len(kept) + len(after))
        results = dict(zip(names, take(len(names))))
        scratch, back_in = take(len(parts)), take(len(back))
        units, back_out, vec_out = take(len(groups)), take(len(returns)), take(len(vector_outs))
        copies = Copies(refs[0])
        me, core, place = ids_ref[0], ids_ref[1], ids_ref[2]

        def bring(piece, target):
            return copies.start(piece.origin(inputs[where_in(arrays, piece.array)], place), target)

        coming = [bring(part[0], target) for part, target in zip(parts, scratch)]
        blocks_coming = [bring(block, target) for block, target in zip(back, back_in)]
        slot = 0
        for (_, group, goals), unit in zip(groups, units):
            for piece, c_other, z_other, start in group:
                coming[slot].wait()
                side, rows = jnp.bitwise_xor(core, c_other), slice(start, start + piece.rows)
                if piece.lanes == d:
                    unit[side, rows, :] = scratch[slot][...].astype(WIDE)
                else:
                    offset = pl.multiple_of(jnp.bitwise_xor(place, z_other) * piece.lanes, piece.lanes)
                    unit[side, rows, pl.ds(offset, piece.lanes)] = scratch[slot][...].astype(WIDE)
                slot += 1
            for half, start, rows, output, index in goals:
                copies.leave(unit.at[half, start : start + rows], results[output].at[index])
        if vectors:
            last = groups[-1][0]
            top, low = units[-1][0, last - 16 : last, :], units[-1][1, last - 16 : last, :]
            stages = [top[0:8, i * LANES : (i + 1) * LANES] for i in range(4)] + [low[0:8, 0:LANES]]
            enc_s, enc_f, dec_s, crs, dec_f = stages
            gains, biases, ups, embed = vec_out
            for row, part in enumerate(stages):
                gains[row : row + 1, :] = part[0:1]
                biases[11 + row : 12 + row, :] = part[1:2]
            order = ((enc_s, 3), (enc_s, 4), (enc_s, 2), (enc_f, 2), (dec_s, 3), (dec_s, 4), (dec_s, 2))
            order += ((crs, 3), (crs, 4), (crs, 2), (dec_f, 2))
            for row, (part, at) in enumerate(order):
                biases[row : row + 1, :] = part[at : at + 1]
            ups[...] = low[8:10, :]
            embed[...] = dec_s[5:6]
            for output, buffer in zip(vectors, vec_out):
                copies.leave(buffer, results[output])
        slot = 0
        for (output, blocks), buffer in zip(returns, back_out):
            for block in range(len(blocks)):
                blocks_coming[slot].wait()
                buffer[jnp.bitwise_xor(me, block)] = back_in[slot][...].astype(buffer.dtype)
                slot += 1
            copies.leave(buffer, results[output])
        copies.finish()

    sems = len(parts) + len(back) + sum(len(goals) for _, _, goals in groups) + len(returns) + len(vector_outs)
    given = pl.pallas_call(
        kernel,
        name=name,
        out_shape=[outs[each] for each in names],
        in_specs=[SMEM] + [HBM] * (len(arrays) + len(kept) + len(after)),
        out_specs=[HBM] * len(names),
        scratch_shapes=[pltpu.VMEM((part[0].rows, part[0].lanes), LOW) for part in parts]
        + [pltpu.VMEM((block.rows, block.lanes), LOW) for block in back]
        + [pltpu.VMEM((2, rows, d), WIDE) for rows, _, _ in groups]
        + [pltpu.VMEM(outs[output].shape, outs[output].dtype) for output, _ in returns]
        + [pltpu.VMEM(each.shape, each.dtype) for each in vector_outs]
        + [pltpu.SemaphoreType.DMA((sems,))],
        input_output_aliases={1 + len(arrays) + i: names.index(each) for i, each in enumerate(kept)},
        compiler_params=parameters(),
        cost_estimate=cost(MIX_COST, 0),
    )(ids, *arrays, *[old[each] for each in kept], *after)
    return types.SimpleNamespace(**dict(zip(names, given)))


def by_rows(
    enc_input,
    dec_input,
    src_lengths,
    tgt_lengths,
    masked,
    cotangent,
    self_qkv,
    attn_out,
    cross_q,
    cross_kv,
    ffn_up,
    ffn_down,
    norm_gain,
    biases,
    up_bias,
    mask_embed,
):
    count, length, d = enc_input.shape
    tokens, ff = count * length, ffn_up.shape[2]
    me = lax.axis_index("seq")
    row = lax.axis_index("rows")
    ids = jnp.stack([me, row % 2, row // 2 % 2]).astype(jnp.int32)
    enc_others = spread_rows(enc_input, me)
    packed = pack_rows(ids, dec_input, cotangent, masked)
    packs = [swap(packed[away], "seq", away) for away in range(1, count)]
    embed = mask_embed.reshape(1, d)
    head_shape = (HEADS, HEAD_DIM, tokens)
    low_tokens, wide_tokens = shape_of((tokens, d), LOW), shape_of((tokens, d), WIDE)
    low_t, low_heads, low_ff = shape_of((d, tokens), LOW), shape_of(head_shape, LOW), shape_of((tokens, ff), LOW)
    exps, inverse = shape_of((HEADS, tokens, tokens), LOW), shape_of((HEADS, 8, tokens), WIDE)
    scale, vec = shape_of((tokens, LANES), WIDE), shape_of((8, d), WIDE)
    bias, scores = shape_of((tokens, tokens), WIDE), shape_of((3, tokens, tokens), WIDE)
    scalars = dict(ids=ids, src=src_lengths, tgt=tgt_lengths)
    step = dict(ids=ids)
    small = dict(biases=whole(biases), gains=whole(norm_gain))
    dense, score = 2 * tokens * d * d, 2 * tokens * tokens * d
    mask_pieces = [(packed[0], None, (0,))]
    for i, array in enumerate(packs, 1):
        mask_pieces.append((array, lambda s: (slice(2 * length, 2 * length + 16),), (i,)))
    mask_part = ((count, 16, d), LOW, mask_pieces)

    def tokens_of(local, others, start=0):
        return ((tokens, d), LOW, token_pieces(local, others, length, start))

    def halves(rows):
        return [shape_of((count * rows, d), LOW)] * 2

    enc = run_stage(
        "encoder_forward",
        functools.partial(encoder_forward, length),
        scalars,
        [dict(
            x=tokens_of(enc_input, enc_others),
            **small,
            qkv=layer(self_qkv, 0),
            proj=layer(attn_out, 0),
            up_bias=whole(up_bias),
            up=layer(ffn_up, 0),
            down=layer(ffn_down, 0),
        )],
        dict(
            x_t=low_t,
            q=low_heads,
            k=low_heads,
            v=low_heads,
            exps=exps,
            inverse=inverse,
            context=low_heads,
            hat0=low_tokens,
            scale0=scale,
            low1=low_tokens,
            act1=low_ff,
            slope1=low_ff,
            hat1=low_tokens,
            scale1=scale,
            memory_t=low_t,
        ),
        dict(bias=bias, scores=scores),
        12 * dense + 2 * score,
        24e6,
        after=packed[1:],
    )
    attention_work = dict(
        context_grad=shape_of(head_shape, WIDE),
        dq=low_heads,
        dk=low_heads,
        dv=low_heads,
        sums=shape_of((2, HEADS, HEAD_DIM, LANES), WIDE),
    )
    dec = run_stage(
        "decoder",
        functools.partial(decoder, length),
        scalars,
        [dict(
            **small,
            mask=mask_part,
            x=tokens_of(dec_input, packs),
            embed=whole(embed),
            qkv=layer(self_qkv, 1),
            proj1=layer(attn_out, 1),
            cross_q=whole(cross_q),
            memory_t=whole(enc.memory_t),
            cross_kv=whole(cross_kv),
            proj2=layer(attn_out, 2),
            up_bias=whole(up_bias),
            up=layer(ffn_up, 1),
            down=layer(ffn_down, 1),
            cotangent=tokens_of(cotangent, packs, length),
        )],
        dict(
            x_t=low_t,
            q2=low_heads,
            k2=low_heads,
            v2=low_heads,
            exps2=exps,
            inverse2=inverse,
            context2=low_heads,
            hat2=low_tokens,
            scale2=scale,
            final=[shape_of((length, d), LOW)] * count,
            vec=vec,
            vec_cross=vec,
            grads=halves(4 * LANES),
            grads_cross=halves(2 * LANES),
            memory_grad=wide_tokens,
            hidden_grad=wide_tokens,
        ),
        dict(
            bias=bias,
            scores=scores,
            low=low_tokens,
            act=low_ff,
            slope=low_ff,
            pre=low_ff,
            hidden_t=low_t,
            hat=wide_tokens,
            scale=scale,
            q=low_heads,
            k=low_heads,
            v=low_heads,
            exps=exps,
            inverse=inverse,
            context=low_heads,
            **attention_work,
        ),
        40 * dense + 8 * score,
        50e6,
    )

    def attention_parts(context, inverse, q, k, v, exps):
        return dict(
            context=whole(context),
            inverse=whole(inverse),
            q=whole(q),
            k=whole(k),
            v=whole(v),
            exps=whole(exps),
        )

    flow_ffn, flow_cross = Flow(dec.grads, 2 * LANES, 2 * LANES), Flow(dec.grads_cross, LANES, LANES)
    first_flows = [flow_ffn, flow_cross]

    def self_stage(name, norm_row, last, grad, hat, scale, attention, x_t, index, more, after):
        rows = 2 * LANES + (16 if last else 0)
        return run_stage(
            name,
            functools.partial(self_backward, norm_row, last),
            step,
            [dict(
                gains=whole(norm_gain),
                grad=whole(grad),
                hat=whole(hat),
                scale=whole(scale),
                proj=layer(attn_out, index),
                **attention_parts(*attention),
                x_t=whole(x_t),
                qkv=layer(self_qkv, index),
                **more,
            )],
            dict(input_grad=low_tokens, grads=halves(rows), **({} if last else dict(vec=vec))),
            dict(vec=vec, **attention_work),
            8 * dense + 4 * score,
            20e6,
            after,
        )

    enc_ffn = run_stage(
        "encoder_ffn_backward",
        encoder_ffn_backward,
        step,
        [dict(
            gains=whole(norm_gain),
            grad=whole(dec.memory_grad),
            hat=whole(enc.hat1),
            scale=whole(enc.scale1),
            down=layer(ffn_down, 0),
            slope=whole(enc.slope1),
            act=whole(enc.act1),
            low=whole(enc.low1),
            up=layer(ffn_up, 0),
        )],
        dict(vec=vec, grad1=wide_tokens, grads=halves(4 * LANES)),
        dict(pre=low_ff),
        16 * dense,
        18e6,
    )
    flow_enc = Flow(enc_ffn.grads, 2 * LANES, 2 * LANES)
    _, formed = advance("first_xy", ids, first_flows, after=[enc_ffn.vec], weight=BIG_WEIGHT)
    _, formed = advance("encoder_ffn_xy", ids, [flow_enc], after=formed)
    dec_self = self_stage(
        "decoder_self_backward",
        2,
        False,
        dec.hidden_grad,
        dec.hat2,
        dec.scale2,
        (dec.context2, dec.inverse2, dec.q2, dec.k2, dec.v2, dec.exps2),
        dec.x_t,
        1,
        dict(mask=mask_part),
        formed,
    )
    flow_dec = Flow(dec_self.grads, LANES, LANES)
    _, formed = advance("first_yx", ids, first_flows, after=[dec_self.vec], weight=BIG_WEIGHT)
    dec_blocks = [Piece(dec_self.input_grad, i * length, length) for i in range(count)]

    def sent_back(blocks):
        return [Step(channel, (blocks[i],)) for i, channel in ((1, X), (2, Y), (3, X))]

    def forwarded(pieces):
        return [Step(Y, (pieces[2][1],))]

    def came_back(blocks, pieces):
        return [blocks[0]] + [pieces[i][1] for i in (0, 1, 3)]

    _, formed = advance("decoder_self_xy", ids, [flow_dec], after=formed)
    enc_self = self_stage(
        "encoder_self_backward",
        0,
        True,
        enc_ffn.grad1,
        enc.hat0,
        enc.scale0,
        (enc.context, enc.inverse, enc.q, enc.k, enc.v, enc.exps),
        enc.x_t,
        0,
        dict(
            vec_enc=whole(enc_ffn.vec),
            vec_self=whole(dec_self.vec),
            vec_cross=whole(dec.vec_cross),
            vec_dec=whole(dec.vec),
        ),
        formed,
    )
    flow_last = Flow(enc_self.grads, LANES, LANES + 16)
    next_flows = [flow_enc, flow_dec]
    four = first_flows + next_flows
    enc_blocks = [Piece(enc_self.input_grad, i * length, length) for i in range(count)]


    def arrivals(pieces):
        return [piece[1].array for piece in pieces]

    _, formed = advance("four_one", ids, four, after=[enc_self.input_grad], weight=BIG_WEIGHT)
    _, formed = advance("last_xy", ids, [flow_last], after=formed)
    _, formed = advance("four_two", ids, four, after=formed)
    finals = [Piece(array, 0, length) for array in dec.final]
    returned = [finals, dec_blocks, enc_blocks]
    back, formed = advance(
        "last_yx", ids, [flow_last], [step for blocks in returned for step in sent_back(blocks)], after=formed
    )
    backs = [back[3 * i : 3 * i + 3] for i in range(len(returned))]
    _, formed = advance("four_three", ids, four, after=formed, weight=3)
    first_done = cross_cores(first_flows)
    back, formed = advance(
        "last_pair", ids, [flow_last], [step for pieces in backs for step in forwarded(pieces)], after=formed
    )
    backs = [pieces + [last] for pieces, last in zip(backs, back)]
    _, formed = advance("next_four", ids, next_flows, after=formed)
    next_done = cross_cores(next_flows)
    _, formed = advance("last_pairs", ids, [flow_last], after=formed)
    _, formed = advance("last_back", ids, [flow_last], after=formed + arrivals(back))
    last_done = cross_both([flow_last])
    half = 2 * LANES

    def ffn_targets(index):
        goals = []
        for side in (0, 1):
            for unit in (0, 1):
                j = side * 2 + unit
                goals.append((side, unit * LANES, LANES, "up", (index, slice(None), slice(j * d, (j + 1) * d))))
            goals.append((side, half, half, "down", (index, slice(side * half, (side + 1) * half))))
        return goals

    def self_targets(index):
        goals = [(0, 0, LANES, "proj", (index,))]
        for j, (side, unit) in enumerate(((0, 1), (1, 0), (1, 1))):
            goals.append((side, unit * LANES, LANES, "qkv", (index, slice(None), slice(j * d, (j + 1) * d))))
        return goals

    cross_targets = [
        (0, 0, LANES, "proj", (2,)),
        (0, LANES, LANES, "cross_q", (slice(None),)),
        (1, 0, LANES, "cross_kv", (slice(None), slice(0, d))),
        (1, LANES, LANES, "cross_kv", (slice(None), slice(d, 2 * d))),
    ]
    local_rows = (count, length, d)
    up_down = dict(up=shape_of((2, LANES, ff), WIDE), down=shape_of((2, d, d), WIDE))
    proj = shape_of((3, LANES, d), WIDE)
    proj_qkv = dict(proj=proj, qkv=shape_of((2, LANES, 3 * d), WIDE))
    first = finish_units(
        "finish_four",
        ids,
        [
            (flow_ffn.rows, flow_ffn.parts(*first_done), ffn_targets(1)),
            (flow_cross.rows, flow_cross.parts(*first_done), cross_targets),
            (flow_enc.rows, flow_enc.parts(*next_done), ffn_targets(0)),
            (flow_dec.rows, flow_dec.parts(*next_done), self_targets(1)),
        ],
        dict(
            final=shape_of(local_rows, LOW),
            dec_grad=shape_of(local_rows, WIDE),
            cross_q=shape_of((LANES, d), WIDE),
            cross_kv=shape_of((LANES, 2 * d), WIDE),
            **up_down,
            **proj_qkv,
        ),
        {},
        [
            ("final", came_back(finals, backs[0])),
            ("dec_grad", came_back(dec_blocks, backs[1])),
        ],
        after=formed,
    )
    third = finish_units(
        "finish_last",
        ids,
        [(flow_last.rows, flow_last.parts(*last_done), self_targets(0))],
        dict(
            enc_grad=shape_of(local_rows, WIDE),
            gains=shape_of((5, LANES), WIDE),
            biases=shape_of((16, LANES), WIDE),
            ups=shape_of((2, d), WIDE),
            embed=shape_of((1, LANES), WIDE),
            **proj_qkv,
        ),
        dict(proj=first.proj, qkv=first.qkv),
        [("enc_grad", came_back(enc_blocks, backs[2]))],
        ("gains", "biases", "ups", "embed"),
    )
    return (
        first.final,
        third.enc_grad,
        first.dec_grad,
        third.qkv,
        third.proj,
        first.cross_q,
        first.cross_kv,
        first.up,
        first.down,
        third.gains,
        third.biases,
        third.ups,
        third.embed.reshape(LANES),
    )


def fits_by_rows(mesh, enc_input, ffn_up):
    count, length = enc_input.shape[0], enc_input.shape[1]
    return (
        mesh.shape["seq"] == 4
        and count == 4
        and mesh.shape["rows"] == 8
        and length == LANES
        and ffn_up.shape[2] == count * ffn_up.shape[1]
        and enc_input.shape[2] == HEADS * HEAD_DIM == count * LANES
    )


def device_program(mesh, *arrays):
    if fits_by_rows(mesh, arrays[0], arrays[10]):
        return by_rows(*arrays)
    return local(*arrays)


def solution(mesh):
    return jax.shard_map(
        functools.partial(device_program, mesh),
        mesh=mesh,
        in_specs=(
            P("rows", "seq", None),
            P("rows", "seq", None),
            P("rows", None),
            P("rows", None),
            P("rows", "seq"),
            P("rows", "seq", None),
            P(),
            P(),
            P(),
            P(),
            P(),
            P(),
            P(),
            P(),
            P(),
            P(),
        ),
        out_specs=(
            P("rows", "seq", None),
            P("rows", "seq", None),
            P("rows", "seq", None),
            P(None, "seq", None),
            P(None, "seq", None),
            P("seq", None),
            P("seq", None),
            P(None, "seq", None),
            P(None, "seq", None),
            P(None, "seq"),
            P(None, "seq"),
            P(None, "seq"),
            P("seq"),
        ),
        check_vma=False,
    )
```

```python
import functools
import types
import typing

import jax
import jax.numpy as jnp
from jax import lax
from jax.experimental import pallas as pl
from jax.experimental.pallas import tpu as pltpu
from jax.sharding import PartitionSpec as P

D = 512
HEADS = 8
HEAD_DIM = 64


EPSILON = 1e-05
NEG_FILL = -1000000000.0
START_FILL = -1e30


def normalize(residual, scale_gain, offset):
    centred = residual - jnp.mean(residual, axis=-1, keepdims=True)
    spread = jnp.mean(centred * centred, axis=-1, keepdims=True)
    return centred * lax.rsqrt(spread + EPSILON) * scale_gain + offset


def gelu_exact(values):
    return jax.nn.gelu(values, approximate=False)


def segments(lengths, places):
    doc_ends = jnp.cumsum(lengths, axis=1)
    return jnp.sum((doc_ends[:, None, :] <= places[None, :, None]).astype(jnp.int32), axis=2)


def project(inputs, weight):
    return jnp.einsum("rsd,df->rsf", inputs, weight, preferred_element_type=jnp.float32)


def project_back(gradient, weight):
    return jnp.einsum("rsf,df->rsd", gradient, weight, preferred_element_type=jnp.float32)


def weight_grad(inputs, gradient):
    return jnp.einsum("rsd,rsf->df", inputs, gradient, preferred_element_type=jnp.float32)


def token_sum(gradient):
    return jnp.sum(gradient, axis=(0, 1))


def split_heads(tensor):
    return tensor.reshape(tensor.shape[:2] + (HEADS, HEAD_DIM))


def split_blocks(tensor, block_size):
    new_shape = (tensor.shape[0], tensor.shape[1] // block_size, block_size) + tensor.shape[2:]
    return jnp.swapaxes(tensor.reshape(new_shape), 0, 1)


def block_scores(query_heads, key_heads, query_seg, key_seg):
    scores = jnp.einsum(
        "rqhd,rkhd->rhqk", query_heads, key_heads, preferred_element_type=jnp.float32
    ) * HEAD_DIM ** (-0.5)
    allowed = query_seg[:, None, :, None] == key_seg[:, None, None, :]
    return jnp.where(allowed, scores, NEG_FILL)


def block_grads(
    query_heads, grad_heads, log_total, delta_rows, query_seg, key_heads, value_heads, key_seg
):
    scores = block_scores(query_heads, key_heads, query_seg, key_seg)
    probs = jnp.exp(scores - log_total[..., None])
    dprobs = jnp.einsum(
        "rqhd,rkhd->rhqk", grad_heads, value_heads, preferred_element_type=jnp.float32
    )
    dscores = (probs * (dprobs - delta_rows[..., None])).astype(jnp.bfloat16)
    scaling = HEAD_DIM ** (-0.5)
    query_part = (
        jnp.einsum("rhqk,rkhd->rqhd", dscores, key_heads, preferred_element_type=jnp.float32)
        * scaling
    )
    key_part = (
        jnp.einsum("rhqk,rqhd->rkhd", dscores, query_heads, preferred_element_type=jnp.float32)
        * scaling
    )
    value_part = jnp.einsum(
        "rhqk,rqhd->rkhd",
        probs.astype(jnp.bfloat16),
        grad_heads,
        preferred_element_type=jnp.float32,
    )
    return (query_part, key_part, value_part)


def start_state(row_count, length):
    return (
        jnp.full((row_count, HEADS, length), START_FILL, jnp.float32),
        jnp.zeros((row_count, HEADS, length), jnp.float32),
        jnp.zeros((row_count, length, HEADS, HEAD_DIM), jnp.float32),
    )


def finish_state(state):
    running_max, running_sum, running_acc = state
    context = running_acc / jnp.swapaxes(running_sum, 1, 2)[..., None]
    return (
        context.reshape(context.shape[:2] + (HEADS * HEAD_DIM,)),
        running_max + jnp.log(running_sum),
    )


def absorber(query_heads, query_seg, key_lengths, length):

    def absorb(carried, piece_pair, first_pos):
        key_piece, value_piece = piece_pair
        piece_len = key_piece.shape[1]
        seg_piece = segments(key_lengths, jnp.arange(piece_len, dtype=jnp.int32))

        def advance(running, inputs):
            running_max, running_sum, running_acc = running
            key_block, value_block, seg_block = inputs
            scores = block_scores(query_heads, key_block, query_seg, seg_block)
            new_max = jnp.maximum(running_max, jnp.max(scores, axis=-1))
            factor = jnp.exp(running_max - new_max)
            exp_scores = jnp.exp(scores - new_max[..., None])
            running_sum = running_sum * factor + jnp.sum(exp_scores, axis=-1)
            running_acc = running_acc * jnp.swapaxes(factor, 1, 2)[..., None] + jnp.einsum(
                "rhqk,rkhd->rqhd",
                exp_scores.astype(jnp.bfloat16),
                value_block,
                preferred_element_type=jnp.float32,
            )
            return ((new_max, running_sum, running_acc), None)

        blocks = (
            split_blocks(split_heads(key_piece), length),
            split_blocks(split_heads(value_piece), length),
            split_blocks(seg_piece, length),
        )
        result, unused = lax.scan(advance, carried, blocks)
        return result

    return absorb


def attend_forward(queries, keys, values, query_seg, key_lengths):
    row_count, length = (queries.shape[0], queries.shape[1])
    query_heads = split_heads(queries)
    absorb = absorber(query_heads, query_seg, key_lengths, length)
    state = absorb(
        start_state(row_count, length),
        (
            lax.all_gather(keys, "seq", axis=1, tiled=True),
            lax.all_gather(values, "seq", axis=1, tiled=True),
        ),
        jnp.int32(0),
    )
    context, log_total = finish_state(state)
    return (context, log_total, None)


def attend_backward(
    queries,
    keys,
    values,
    query_seg,
    key_seg,
    query_lengths,
    key_lengths,
    context,
    log_total,
    context_grad,
):
    row_count, length = (queries.shape[0], queries.shape[1])
    grad_low = context_grad.astype(jnp.bfloat16)
    query_heads = split_heads(queries)
    grad_heads = split_heads(grad_low)
    delta_rows = jnp.swapaxes(
        jnp.sum(grad_heads.astype(jnp.float32) * split_heads(context), axis=-1), 1, 2
    )
    zero_heads = jnp.zeros((row_count, length, HEADS, HEAD_DIM), jnp.float32)
    key_piece = lax.all_gather(keys, "seq", axis=1, tiled=True)
    value_piece = lax.all_gather(values, "seq", axis=1, tiled=True)
    piece_len = key_piece.shape[1]
    block_size = length
    seg_piece = segments(key_lengths, jnp.arange(piece_len, dtype=jnp.int32))

    def advance(running, inputs):
        key_block, value_block, seg_block = inputs
        query_part, unused_keys, unused_values = block_grads(
            query_heads,
            grad_heads,
            log_total,
            delta_rows,
            query_seg,
            key_block,
            value_block,
            seg_block,
        )
        return (running + query_part, None)

    blocks = (
        split_blocks(split_heads(key_piece), block_size),
        split_blocks(split_heads(value_piece), block_size),
        split_blocks(seg_piece, block_size),
    )
    result, unused = lax.scan(advance, zero_heads, blocks)
    query_grad = result
    total_all, delta_all = (
        lax.all_gather(log_total, "seq", axis=2, tiled=True),
        lax.all_gather(delta_rows, "seq", axis=2, tiled=True),
    )
    key_heads = split_heads(keys)
    value_heads = split_heads(values)
    query_piece = lax.all_gather(queries, "seq", axis=1, tiled=True)
    grad_piece = lax.all_gather(grad_low, "seq", axis=1, tiled=True)
    piece_len = query_piece.shape[1]
    block_size = length
    seg_piece = segments(query_lengths, jnp.arange(piece_len, dtype=jnp.int32))
    offsets = jnp.arange(piece_len // block_size, dtype=jnp.int32) * block_size

    def advance(running, inputs):
        query_block, grad_block, seg_block, offset = inputs
        total_block = lax.dynamic_slice_in_dim(total_all, offset, block_size, 2)
        delta_block = lax.dynamic_slice_in_dim(delta_all, offset, block_size, 2)
        unused_query, key_part, value_part = block_grads(
            query_block,
            grad_block,
            total_block,
            delta_block,
            seg_block,
            key_heads,
            value_heads,
            key_seg,
        )
        return ((running[0] + key_part, running[1] + value_part), None)

    blocks = (
        split_blocks(split_heads(query_piece), block_size),
        split_blocks(split_heads(grad_piece), block_size),
        split_blocks(seg_piece, block_size),
        offsets,
    )
    result, unused = lax.scan(advance, (zero_heads, zero_heads), blocks)
    key_grad, value_grad = result
    return (
        query_grad.reshape(queries.shape),
        key_grad.reshape(queries.shape),
        value_grad.reshape(queries.shape),
    )


def self_forward(inputs_low, w_qkv, bias_q, bias_v, segment, lengths):
    projected = project(inputs_low, w_qkv)
    queries = (projected[..., :D] + bias_q).astype(jnp.bfloat16)
    keys = projected[..., D : 2 * D].astype(jnp.bfloat16)
    values = (projected[..., 2 * D :] + bias_v).astype(jnp.bfloat16)
    context, log_total, stored = attend_forward(queries, keys, values, segment, lengths)
    return (queries, keys, values, context, log_total, stored)


def ffn_forward(hidden, w_up, bias_up, w_down, bias_down):
    hidden_low = hidden.astype(jnp.bfloat16)
    pre_act = project(hidden_low, w_up) + bias_up
    activated, act_back = jax.vjp(gelu_exact, pre_act)
    act_low = activated.astype(jnp.bfloat16)
    return (project(act_low, w_down) + bias_down, (hidden_low, act_low, act_back))


def ffn_backward(out_grad, stored, w_up, w_down):
    hidden_low, act_low, act_back = stored
    out_low = out_grad.astype(jnp.bfloat16)
    down_grad = weight_grad(act_low, out_low)
    (pre_grad,) = act_back(project_back(out_low, w_down))
    pre_low = pre_grad.astype(jnp.bfloat16)
    up_grad = weight_grad(hidden_low, pre_low)
    return (
        project_back(pre_low, w_up),
        up_grad,
        token_sum(pre_grad),
        down_grad,
        token_sum(out_grad),
    )


def local(
    enc_input,
    dec_input,
    src_lengths,
    tgt_lengths,
    masked,
    cotangent,
    self_qkv,
    attn_out,
    cross_q,
    cross_kv,
    ffn_up,
    ffn_down,
    norm_gain,
    biases,
    up_bias,
    mask_embed,
):
    length = enc_input.shape[1]
    places = lax.axis_index("seq") * length + jnp.arange(length, dtype=jnp.int32)
    src_seg = segments(src_lengths, places)
    tgt_seg = segments(tgt_lengths, places)
    mask_float = masked.astype(jnp.float32)[..., None]
    enc_queries, enc_keys, enc_values, enc_context, enc_total, enc_stored = self_forward(
        enc_input, self_qkv[0], biases[0], biases[1], src_seg, src_lengths
    )
    enc_ctx_low = enc_context.astype(jnp.bfloat16)
    enc_resid = enc_input.astype(jnp.float32) + project(enc_ctx_low, attn_out[0]) + biases[2]
    enc_hidden, enc_norm_back = jax.vjp(normalize, enc_resid, norm_gain[0], biases[11])
    enc_ffn, enc_kept = ffn_forward(enc_hidden, ffn_up[0], up_bias[0], ffn_down[0], biases[3])
    memory, memory_back = jax.vjp(normalize, enc_hidden + enc_ffn, norm_gain[1], biases[12])
    memory_low = memory.astype(jnp.bfloat16)
    dec_inputs = dec_input.astype(jnp.float32) + mask_float * mask_embed
    dec_low = dec_inputs.astype(jnp.bfloat16)
    dec_queries, dec_keys, dec_values, dec_context, dec_total, dec_stored = self_forward(
        dec_low, self_qkv[1], biases[4], biases[5], tgt_seg, tgt_lengths
    )
    dec_ctx_low = dec_context.astype(jnp.bfloat16)
    dec_hidden, dec_norm_back = jax.vjp(
        normalize,
        dec_inputs + project(dec_ctx_low, attn_out[1]) + biases[6],
        norm_gain[2],
        biases[13],
    )
    dec_hidden_low = dec_hidden.astype(jnp.bfloat16)
    cross_queries = (project(dec_hidden_low, cross_q) + biases[7]).astype(jnp.bfloat16)
    cross_pair = project(memory_low, cross_kv)
    cross_keys = cross_pair[..., :D].astype(jnp.bfloat16)
    cross_values = (cross_pair[..., D:] + biases[8]).astype(jnp.bfloat16)
    cross_context, cross_total, cross_stored = attend_forward(
        cross_queries, cross_keys, cross_values, tgt_seg, src_lengths
    )
    cross_ctx_low = cross_context.astype(jnp.bfloat16)
    cross_hidden, cross_norm_back = jax.vjp(
        normalize,
        dec_hidden + project(cross_ctx_low, attn_out[2]) + biases[9],
        norm_gain[3],
        biases[14],
    )
    last_ffn, last_kept = ffn_forward(cross_hidden, ffn_up[1], up_bias[1], ffn_down[1], biases[10])
    final, final_back = jax.vjp(normalize, cross_hidden + last_ffn, norm_gain[4], biases[15])
    final_grad, gain_four, shift_four = final_back(cotangent.astype(jnp.float32))
    into_cross, up_grad_one, upb_grad_one, down_grad_one, bias_ten = ffn_backward(
        final_grad, last_kept, ffn_up[1], ffn_down[1]
    )
    cross_resid_grad, gain_three, shift_three = cross_norm_back(final_grad + into_cross)
    cross_out_low = cross_resid_grad.astype(jnp.bfloat16)
    out_grad_two = weight_grad(cross_ctx_low, cross_out_low)
    cross_q_part, cross_k_part, cross_v_part = attend_backward(
        cross_queries,
        cross_keys,
        cross_values,
        tgt_seg,
        src_seg,
        tgt_lengths,
        src_lengths,
        cross_context,
        cross_total,
        project_back(cross_out_low, attn_out[2]),
    )
    cross_q_low = cross_q_part.astype(jnp.bfloat16)
    cross_kv_low = jnp.concatenate([cross_k_part, cross_v_part], axis=-1).astype(jnp.bfloat16)
    cross_q_weight = weight_grad(dec_hidden_low, cross_q_low)
    cross_kv_weight = weight_grad(memory_low, cross_kv_low)
    memory_grad = project_back(cross_kv_low, cross_kv)
    dec_resid_grad, gain_two, shift_two = dec_norm_back(
        cross_resid_grad + project_back(cross_q_low, cross_q)
    )
    dec_out_low = dec_resid_grad.astype(jnp.bfloat16)
    out_grad_one = weight_grad(dec_ctx_low, dec_out_low)
    dec_q_part, dec_k_part, dec_v_part = attend_backward(
        dec_queries,
        dec_keys,
        dec_values,
        tgt_seg,
        tgt_seg,
        tgt_lengths,
        tgt_lengths,
        dec_context,
        dec_total,
        project_back(dec_out_low, attn_out[1]),
    )
    dec_qkv_low = jnp.concatenate([dec_q_part, dec_k_part, dec_v_part], axis=-1).astype(
        jnp.bfloat16
    )
    qkv_grad_one = weight_grad(dec_low, dec_qkv_low)
    dec_input_grad = dec_resid_grad + project_back(dec_qkv_low, self_qkv[1])
    mask_grad = jnp.sum(dec_input_grad * mask_float, axis=(0, 1))
    memory_resid_grad, gain_one, shift_one = memory_back(memory_grad)
    into_enc, up_grad_zero, upb_grad_zero, down_grad_zero, bias_three = ffn_backward(
        memory_resid_grad, enc_kept, ffn_up[0], ffn_down[0]
    )
    enc_resid_grad, gain_zero, shift_zero = enc_norm_back(memory_resid_grad + into_enc)
    enc_out_low = enc_resid_grad.astype(jnp.bfloat16)
    out_grad_zero = weight_grad(enc_ctx_low, enc_out_low)
    enc_q_part, enc_k_part, enc_v_part = attend_backward(
        enc_queries,
        enc_keys,
        enc_values,
        src_seg,
        src_seg,
        src_lengths,
        src_lengths,
        enc_context,
        enc_total,
        project_back(enc_out_low, attn_out[0]),
    )
    enc_qkv_low = jnp.concatenate([enc_q_part, enc_k_part, enc_v_part], axis=-1).astype(
        jnp.bfloat16
    )
    qkv_grad_zero = weight_grad(enc_input, enc_qkv_low)
    enc_input_grad = enc_resid_grad + project_back(enc_qkv_low, self_qkv[0])
    bias_rows = jnp.stack(
        [
            token_sum(enc_q_part),
            token_sum(enc_v_part),
            token_sum(enc_resid_grad),
            bias_three,
            token_sum(dec_q_part),
            token_sum(dec_v_part),
            token_sum(dec_resid_grad),
            token_sum(cross_q_part),
            token_sum(cross_v_part),
            token_sum(cross_resid_grad),
            bias_ten,
            shift_zero,
            shift_one,
            shift_two,
            shift_three,
            shift_four,
        ]
    )
    shares = (
        lax.psum_scatter(
            jnp.stack([qkv_grad_zero, qkv_grad_one]), "seq", scatter_dimension=1, tiled=True
        ),
        lax.psum_scatter(
            jnp.stack([out_grad_zero, out_grad_one, out_grad_two]),
            "seq",
            scatter_dimension=1,
            tiled=True,
        ),
        lax.psum_scatter(cross_q_weight, "seq", scatter_dimension=0, tiled=True),
        lax.psum_scatter(cross_kv_weight, "seq", scatter_dimension=0, tiled=True),
        lax.psum_scatter(
            jnp.stack([up_grad_zero, up_grad_one]), "seq", scatter_dimension=1, tiled=True
        ),
        lax.psum_scatter(
            jnp.stack([down_grad_zero, down_grad_one]), "seq", scatter_dimension=1, tiled=True
        ),
        lax.psum_scatter(
            jnp.stack([gain_zero, gain_one, gain_two, gain_three, gain_four]),
            "seq",
            scatter_dimension=1,
            tiled=True,
        ),
        lax.psum_scatter(bias_rows, "seq", scatter_dimension=1, tiled=True),
        lax.psum_scatter(
            jnp.stack([upb_grad_zero, upb_grad_one]), "seq", scatter_dimension=1, tiled=True
        ),
        lax.psum_scatter(mask_grad, "seq", scatter_dimension=0, tiled=True),
    )
    totals = lax.psum(
        (
            shares[0],
            shares[1],
            shares[2],
            shares[3],
            shares[4],
            shares[5],
            shares[6],
            shares[7],
            shares[8],
            shares[9],
        ),
        "rows",
    )
    return (
        final.astype(jnp.bfloat16),
        enc_input_grad,
        dec_input_grad,
        totals[0],
        totals[1],
        totals[2],
        totals[3],
        totals[4],
        totals[5],
        totals[6],
        totals[7],
        totals[8],
        totals[9],
    )


LANES = 128
CHANNELS = 96
COST = 50
MIX_COST = 4e9
BIG_WEIGHT = 2e11 / MIX_COST
BIG_VMEM = 64 * 2**20
LOW = jnp.bfloat16
WIDE = jnp.float32
HBM = pl.BlockSpec(memory_space=pltpu.HBM)
SMEM = pl.BlockSpec(memory_space=pltpu.SMEM)


def shape_of(dims, dtype):
    return jax.ShapeDtypeStruct(tuple(dims), dtype)


def distinct(arrays):
    found = []
    for array in arrays:
        if not any(array is other for other in found):
            found.append(array)
    return found


def where_in(arrays, array):
    return [other is array for other in arrays].index(True)


def parameters():
    return pltpu.CompilerParams(vmem_limit_bytes=BIG_VMEM)


def cost(flops, moved):
    return pl.CostEstimate(flops=int(flops), bytes_accessed=int(moved), transcendentals=0)


class Copies:
    def __init__(self, sems):
        self.sems, self.used, self.leaving = sems, 0, []

    def start(self, source, target):
        moved = pltpu.make_async_copy(source, target, self.sems.at[self.used])
        self.used += 1
        moved.start()
        return moved

    def leave(self, source, target):
        self.leaving.append(self.start(source, target))

    def finish(self):
        for moved in self.leaving:
            moved.wait()


class Arrivals:
    def __init__(self, copies, refs, groups):
        self._copies, self._refs, self._groups, self._coming = copies, refs, groups, {}
        self.more()

    def more(self):
        for name, origin, target in self._groups.pop(0) if self._groups else ():
            self._coming.setdefault(name, []).append(self._copies.start(origin, target))

    def finish(self):
        while self._groups:
            self.more()
        for name in self._refs:
            getattr(self, name)

    def __getattr__(self, name):
        while name not in self._coming and any(name == move[0] for group in self._groups for move in group):
            self.more()
        for moved in self._coming.get(name, ()):
            moved.wait()
        self._coming[name] = []
        return self._refs[name]


class Stage(typing.NamedTuple):
    scalars: typing.Any
    use: typing.Any
    out: typing.Any
    work: typing.Any
    copies: typing.Any
    targets: typing.Any

    def push(self, *buffers):
        for buffer in buffers:
            self.push_part(buffer, ())

    def push_part(self, buffer, index):
        target = [result for ref, result in self.targets if ref is buffer][0]
        if isinstance(target, list):
            self.copies.leave(buffer.at[index], target[index[0]].at[index[1:]] if index[1:] else target[index[0]])
        else:
            self.copies.leave(buffer.at[index] if index else buffer, target.at[index] if index else target)


def run_stage(name, body, scalars, parts, outs, work, flops, moved, after=()):
    all_parts = {key: part for group in parts for key, part in group.items()}
    arrays = distinct([move[0] for part in all_parts.values() for move in part[2]])
    after = [array for array in distinct(after) if not any(array is other for other in arrays)]
    flat_outs, spots = [], {}
    for key, shape in outs.items():
        several = shape if isinstance(shape, list) else [shape]
        spots[key] = (len(flat_outs), len(several))
        flat_outs += several
    buffers = [shape_of((len(s),) + s[0].shape, s[0].dtype) if isinstance(s, list) else s for s in outs.values()]

    def kernel(*refs):
        refs = list(refs)

        def take(count):
            taken = refs[:count]
            del refs[:count]
            return taken

        scalar_refs = types.SimpleNamespace(**dict(zip(scalars, take(len(scalars)))))
        inputs = take(len(arrays))
        take(len(after))
        results = take(len(flat_outs))
        part_refs = dict(zip(all_parts, take(len(all_parts))))
        out_refs = dict(zip(outs, take(len(outs))))
        work_refs = dict(zip(work, take(len(work))))
        copies = Copies(refs[0])
        groups = []
        for wanted in parts:
            groups.append([])
            for key, part in wanted.items():
                for array, source, target in part[2]:
                    origin, place = inputs[where_in(arrays, array)], part_refs[key]
                    origin = origin if source is None else origin.at[source(scalar_refs)]
                    groups[-1].append((key, origin, place if target is None else place.at[target]))
        targets = []
        for key, (start, count) in spots.items():
            several = isinstance(outs[key], list)
            targets.append((out_refs[key], list(results[start : start + count]) if several else results[start]))
        use = Arrivals(copies, part_refs, groups)
        stage = Stage(
            scalar_refs, use, types.SimpleNamespace(**out_refs), types.SimpleNamespace(**work_refs), copies, targets
        )
        body(stage)
        use.finish()
        copies.finish()

    given = pl.pallas_call(
        kernel,
        name=name,
        out_shape=flat_outs,
        in_specs=[SMEM] * len(scalars) + [HBM] * (len(arrays) + len(after)),
        out_specs=[HBM] * len(flat_outs),
        scratch_shapes=[pltpu.VMEM(part[0], part[1]) for part in all_parts.values()]
        + [pltpu.VMEM(each.shape, each.dtype) for each in buffers]
        + [pltpu.VMEM(each.shape, each.dtype) for each in work.values()]
        + [pltpu.SemaphoreType.DMA((CHANNELS,))],
        compiler_params=parameters(),
        cost_estimate=cost(flops * COST, moved),
    )(*scalars.values(), *arrays, *after)
    found = {}
    for key, (start, count) in spots.items():
        found[key] = list(given[start : start + count]) if isinstance(outs[key], list) else given[start]
    return types.SimpleNamespace(**found)


def whole(array):
    return (tuple(array.shape), array.dtype, [(array, None, None)])


def layer(array, index):
    return (tuple(array.shape[1:]), array.dtype, [(array, lambda s: index, None)])


def dot_nn(a, b):
    return lax.dot_general(a, b, (((1,), (0,)), ((), ())), preferred_element_type=WIDE)


def dot_nt(a, b):
    return lax.dot_general(a, b, (((1,), (1,)), ((), ())), preferred_element_type=WIDE)


def dot_tn(a, b):
    return lax.dot_general(a, b, (((0,), (0,)), ((), ())), preferred_element_type=WIDE)


def total(values):
    return jnp.sum(values, axis=0, keepdims=True)


def norm_parts(residual):
    centred = residual - jnp.mean(residual, axis=-1, keepdims=True)
    scale = lax.rsqrt(jnp.mean(centred * centred, axis=-1, keepdims=True) + EPSILON)
    return centred * scale, scale


def norm_keep(stage, residual, gain, shift, hat_ref, scale_ref):
    hat, scale = norm_parts(residual)
    hat_ref[...] = hat.astype(LOW)
    scale_ref[...] = jnp.broadcast_to(scale, scale_ref.shape)
    stage.push(hat_ref, scale_ref)
    return hat * gain + shift


def norm_back(grad, hat, scale, gain):
    scaled = grad * gain
    inner = jnp.mean(scaled, axis=-1, keepdims=True)
    along = jnp.mean(scaled * hat, axis=-1, keepdims=True)
    return scale * (scaled - inner - hat * along), total(grad * hat), total(grad)


def segment_ids(lengths_ref, row, places):
    end = jnp.int32(0)
    found = jnp.zeros(places.shape, jnp.int32)
    for slot in range(lengths_ref.shape[1]):
        end = end + lengths_ref[row, slot]
        found = found + (end <= places).astype(jnp.int32)
    return found


def positions(me, length, shape, axis):
    token = lax.broadcasted_iota(jnp.int32, shape, axis)
    bits = length.bit_length() - 1
    block = lax.shift_right_logical(token, jnp.int32(bits))
    return lax.shift_left(jnp.bitwise_xor(block, me), jnp.int32(bits)) + jnp.bitwise_and(token, length - 1)


def fill_bias(bias_ref, query_lengths, key_lengths, me, length):
    tokens = bias_ref.shape[0]
    query_seg = segment_ids(query_lengths, me, positions(me, length, (1, tokens), 1))
    key_seg = segment_ids(key_lengths, me, positions(me, length, (tokens, 1), 0))
    bias_ref[...] = jnp.where(key_seg == query_seg, 0.0, NEG_FILL)


def heads_of(values):
    return values.reshape(HEADS, HEAD_DIM, values.shape[-1])


def flat(ref):
    return ref[...].reshape(HEADS * HEAD_DIM, ref.shape[-1])


def staggered(count, *steps):
    for i in range(count + len(steps) - 1):
        for lag, step in enumerate(steps):
            if 0 <= i - lag < count:
                step(i - lag)


def attention_forward(q_ref, k_ref, v_ref, bias_ref, exp_ref, inverse_ref, context_ref, score_ref):
    def form(head):
        score_ref[head % score_ref.shape[0]] = dot_tn(k_ref[head], q_ref[head]) + bias_ref[...]

    def exponentials(head):
        scores = score_ref[head % score_ref.shape[0]]
        exps = jnp.exp(scores - jnp.max(scores, axis=0, keepdims=True))
        exp_ref[head] = exps.astype(LOW)
        inverse_ref[head] = jnp.broadcast_to(1.0 / total(exps), inverse_ref.shape[1:])

    def contract(head):
        context_ref[head] = (dot_nn(v_ref[head], exp_ref[head]) * inverse_ref[head][0:1]).astype(LOW)

    staggered(HEADS, form, exponentials, contract)


def attention_backward(q_ref, k_ref, v_ref, exp_ref, inverse_ref, context_ref, work):
    for head in range(HEADS):
        exps = exp_ref[head]
        grad = (work.context_grad[head].astype(LOW).astype(WIDE) * inverse_ref[head][0:1]).astype(LOW)
        delta = total(grad.astype(WIDE) * context_ref[head].astype(WIDE))
        score_grad = (exps.astype(WIDE) * (dot_tn(v_ref[head], grad) - delta)).astype(LOW)
        dv = dot_nt(grad, exps)
        dq = dot_nn(k_ref[head], score_grad) * HEAD_DIM ** (-0.5)
        work.dv[head] = dv.astype(LOW)
        work.dk[head] = dot_nt(q_ref[head], score_grad).astype(LOW)
        work.dq[head] = dq.astype(LOW)
        wide = (HEAD_DIM, LANES)
        work.sums[0, head] = jnp.broadcast_to(jnp.sum(dq, axis=1, keepdims=True), wide)
        work.sums[1, head] = jnp.broadcast_to(jnp.sum(dv, axis=1, keepdims=True), wide)


def sum_row(sums_ref, which):
    return jnp.transpose(sums_ref[which].reshape(HEADS * HEAD_DIM, LANES))[0:1]


def qkv_forward(stage, weight, low_t, bias_t, q_col, v_col, q_ref, k_ref, v_ref):
    d = low_t.shape[0]
    queries = (dot_tn(weight[:, 0:d], low_t) + bias_t[:, q_col : q_col + 1]).astype(LOW)
    q_ref[...] = heads_of(queries * HEAD_DIM ** (-0.5))
    k_ref[...] = heads_of(dot_tn(weight[:, d : 2 * d], low_t).astype(LOW))
    v_ref[...] = heads_of((dot_tn(weight[:, 2 * d :], low_t) + bias_t[:, v_col : v_col + 1]).astype(LOW))
    stage.push(q_ref, k_ref, v_ref)


def gelu_parts(pre):
    half = 0.5 * (1.0 + lax.erf(pre * 0.5**0.5))
    density = jnp.exp(pre * pre * -0.5) * (0.5 / 3.141592653589793) ** 0.5
    return pre * half, half + pre * density


def feed_forward(low, up, up_bias, down, act_ref, slope_ref, pre_ref, leave=None):
    width = low.shape[1]
    columns = [slice(j * width, (j + 1) * width) for j in range(act_ref.shape[1] // width)]

    def form(j):
        pre_ref[j % pre_ref.shape[0]] = dot_nn(low, up[:, columns[j]]) + up_bias[:, columns[j]]

    def activate(j):
        act, slope = gelu_parts(pre_ref[j % pre_ref.shape[0]])
        act_ref[:, columns[j]] = act.astype(LOW)
        slope_ref[:, columns[j]] = slope.astype(LOW)

    staggered(len(columns), form, activate)
    if leave is not None:
        leave(act_ref, slope_ref)
    return dot_nn(act_ref[...], down[...])


class Halves(typing.NamedTuple):
    ref: typing.Any
    first: int
    rest: int
    me: typing.Any
    core: typing.Any
    stage: typing.Any

    def leave_regions(self, start, rows):
        for side in (0, 1):
            for begin in (start, start + 2 * (self.first + self.rest)):
                self.stage.push_part(self.ref, (side, slice(begin, begin + rows)))

    def leave_first(self, rows):
        self.leave_regions(0, 2 * self.first)

    def leave_rest(self, rows):
        self.leave_regions(2 * self.first, 2 * self.rest)

    def put(self, half, chunk, start, rows):
        away = jnp.bitwise_xor(self.me, chunk)
        low, high = jnp.bitwise_and(away, 1), lax.shift_right_logical(away, 1)
        both = 2 * (self.first + self.rest)
        if start < self.first:
            place = high * self.first + jnp.where(low == 1, 0, both) + start
        else:
            place = low * self.rest + jnp.where(high == 1, 0, both) + 2 * self.first + start - self.first
        side = jnp.bitwise_xor(self.core, half)
        self.ref[side, pl.ds(pl.multiple_of(place, 16), rows.shape[0])] = rows.astype(LOW)


def put_units(grads, block, half, unit):
    rows = LANES
    for chunk in range(block.shape[0] // rows):
        grads.put(half, chunk, unit * rows, block[chunk * rows : (chunk + 1) * rows])


def feed_back(out_grad, low, act, slope, up, down, vec_ref, vec_row, grads, pre_ref, more=None):
    width = out_grad.shape[1]
    half = width // 2
    out_low = out_grad.astype(LOW)
    columns = [slice(j * width, (j + 1) * width) for j in range(pre_ref.shape[1] // width)]
    for j, cols in enumerate(columns):
        pre = dot_nt(out_low, down[cols, :]) * slope[:, cols].astype(WIDE)
        vec_ref[vec_row + j : vec_row + j + 1, :] = total(pre)
        pre_ref[:, cols] = pre.astype(LOW)
        down_grad = dot_tn(act[:, cols], out_low)
        for r in range(2):
            grads.put(r, j, half, down_grad[r * half : (r + 1) * half])
    grads.leave_rest(half)
    low, up = low(), up()
    for j, cols in enumerate(columns):
        put_units(grads, dot_tn(low[...], pre_ref[:, cols]), j // 2, j % 2)
    grads.leave_first(half)
    return dot_nt(pre_ref[...], up[...])


def own_row(s):
    return s.ids[0]


def token_pieces(local, others, length, start=0):
    pieces = [(local, own_row, (slice(0, length),))]
    for d, array in enumerate(others, 1):
        pieces.append((array, lambda s: (slice(start, start + length),), (slice(d * length, (d + 1) * length),)))
    return pieces


def put_blocks(ref, values):
    for i in range(ref.shape[0]):
        ref[i] = values[i * ref.shape[1] : (i + 1) * ref.shape[1]]


def encoder_forward(length, stage):
    me, use, out = stage.scalars.ids[0], stage.use, stage.out
    fill_bias(stage.work.bias, stage.scalars.src, stage.scalars.src, me, length)
    x = use.x[...]
    x_t = jnp.transpose(x)
    out.x_t[...] = x_t
    stage.push(out.x_t)
    biases = use.biases[...]
    qkv = use.qkv
    use.more()
    qkv_forward(stage, qkv, x_t, jnp.transpose(biases), 0, 1, out.q, out.k, out.v)
    attention_forward(out.q, out.k, out.v, stage.work.bias, out.exps, out.inverse, out.context, stage.work.scores)
    stage.push(out.exps, out.inverse, out.context)
    gains = use.gains
    residual = x.astype(WIDE) + dot_tn(flat(out.context), use.proj[...]) + biases[2:3]
    hidden = norm_keep(stage, residual, gains[0:1], biases[11:12], out.hat0, out.scale0)
    hidden_low = hidden.astype(LOW)
    out.low1[...] = hidden_low
    stage.push(out.low1)
    ffn = feed_forward(hidden_low, use.up, use.up_bias[0:1], use.down, out.act1, out.slope1, stage.work.scores, stage.push)
    memory = norm_keep(stage, hidden + ffn + biases[3:4], gains[1:2], biases[12:13], out.hat1, out.scale1)
    out.memory_t[...] = jnp.transpose(memory.astype(LOW))
    stage.push(out.memory_t)


def mask_columns(mask, d):
    row = jnp.concatenate([mask[i][0:1, 0:LANES].astype(WIDE) for i in range(mask.shape[0])], axis=1)
    columns = jnp.transpose(jnp.broadcast_to(row, (LANES, row.shape[1])))
    return jnp.concatenate([columns] * (d // LANES), axis=1)


def decoder(length, stage):
    me, use, out, work = stage.scalars.ids[0], stage.use, stage.out, stage.work
    biases = use.biases[...]
    bias_t = jnp.transpose(biases)
    gains = use.gains
    src, tgt = stage.scalars.src, stage.scalars.tgt
    fill_bias(work.bias, tgt, tgt, me, length)
    x = use.x[...].astype(WIDE)
    d = x.shape[1]
    y = x + mask_columns(use.mask, d) * use.embed[...]
    y_t = jnp.transpose(y.astype(LOW))
    out.x_t[...] = y_t
    stage.push(out.x_t)
    qkv = use.qkv
    use.more()
    qkv_forward(stage, qkv, y_t, bias_t, 4, 5, out.q2, out.k2, out.v2)
    use.more()
    attention_forward(out.q2, out.k2, out.v2, work.bias, out.exps2, out.inverse2, out.context2, work.scores)
    stage.push(out.exps2, out.inverse2, out.context2)
    residual = y + dot_tn(flat(out.context2), use.proj1[...]) + biases[6:7]
    hidden = norm_keep(stage, residual, gains[2:3], biases[13:14], out.hat2, out.scale2)
    hidden_t = jnp.transpose(hidden.astype(LOW))
    work.hidden_t[...] = hidden_t
    queries = (dot_tn(use.cross_q[...], hidden_t) + bias_t[:, 7:8]).astype(LOW)
    work.q[...] = heads_of(queries * HEAD_DIM ** (-0.5))
    memory_t = use.memory_t
    kv = use.cross_kv
    work.k[...] = heads_of(dot_tn(kv[:, 0:d], memory_t[...]).astype(LOW))
    work.v[...] = heads_of((dot_tn(kv[:, d:], memory_t[...]) + bias_t[:, 8:9]).astype(LOW))
    fill_bias(work.bias, tgt, src, me, length)
    attention_forward(work.q, work.k, work.v, work.bias, work.exps, work.inverse, work.context, work.scores)
    proj = use.proj2
    residual = hidden + dot_tn(flat(work.context), proj[...]) + biases[9:10]
    hat, scale = norm_parts(residual)
    work.hat[...] = hat
    work.scale[...] = jnp.broadcast_to(scale, work.scale.shape)
    hidden = hat * gains[3:4] + biases[14:15]
    work.low[...] = hidden.astype(LOW)
    up, down = use.up, use.down
    ffn = feed_forward(work.low[...], up, use.up_bias[1:2], down, work.act, work.slope, work.scores)
    hat, scale = norm_parts(hidden + ffn + biases[10:11])
    put_blocks(out.final, (hat * gains[4:5] + biases[15:16]).astype(LOW))
    for i in range(out.final.shape[0]):
        stage.push_part(out.final, (i,))
    vec, vec_cross = out.vec, out.vec_cross
    vec[...] = jnp.zeros_like(vec)
    vec_cross[...] = jnp.zeros_like(vec_cross)
    cotangent = use.cotangent[...].astype(WIDE)
    grad, vec[0:1, :], vec[1:2, :] = norm_back(cotangent, hat, scale, gains[4:5])
    vec[2:3, :] = total(grad)
    into = feed_back(
        grad,
        lambda: work.low,
        work.act,
        work.slope,
        lambda: up,
        down,
        vec,
        3,
        Halves(out.grads, 2 * LANES, 2 * LANES, me, stage.scalars.ids[1], stage),
        work.pre,
    )
    stage.push(vec)
    grads = Halves(out.grads_cross, LANES, LANES, me, stage.scalars.ids[1], stage)
    grad = out_backward(
        grad + into, work.hat[...], work.scale[:, 0:1], gains[3:4], proj, work.context, work, vec_cross, grads
    )
    attention_backward(work.q, work.k, work.v, work.exps, work.inverse, work.context, work)
    dq, dk, dv = attention_sums(work, vec_cross)
    stage.push(vec_cross)
    put_units(grads, dot_nt(work.hidden_t[...], dq), 0, 1)
    put_units(grads, dot_nt(memory_t[...], dk), 1, 0)
    put_units(grads, dot_nt(memory_t[...], dv), 1, 1)
    grads.leave_first(0)
    grads.leave_rest(0)
    out.memory_grad[...] = jnp.transpose(dot_nn(kv[:, 0:d], dk) + dot_nn(kv[:, d:], dv))
    stage.push(out.memory_grad)
    out.hidden_grad[...] = grad + jnp.transpose(dot_nn(use.cross_q[...], dq))
    stage.push(out.hidden_grad)


def out_backward(grad, hat, scale, gain, proj, context, work, vec, grads):
    grad, vec[0:1, :], vec[1:2, :] = norm_back(grad, hat, scale, gain)
    vec[2:3, :] = total(grad)
    low = grad.astype(LOW)
    work.context_grad[...] = heads_of(dot_nt(proj[...], low))
    put_units(grads, dot_nn(flat(context), low), 0, 0)
    return grad


def attention_sums(work, vec):
    vec[3:4, :] = sum_row(work.sums, 0)
    vec[4:5, :] = sum_row(work.sums, 1)
    return flat(work.dq), flat(work.dk), flat(work.dv)


def encoder_ffn_backward(stage):
    me, core = stage.scalars.ids[0], stage.scalars.ids[1]
    use, out = stage.use, stage.out
    vec = out.vec
    vec[...] = jnp.zeros_like(vec)
    hat, scale, grad = use.hat, use.scale, use.grad
    use.more()
    hat, scale = hat[...].astype(WIDE), scale[...][:, 0:1]
    grad, vec[0:1, :], vec[1:2, :] = norm_back(grad[...], hat, scale, use.gains[1:2])
    vec[2:3, :] = total(grad)
    grads = Halves(out.grads, 2 * LANES, 2 * LANES, me, core, stage)
    down, slope, act = use.down, use.slope, use.act
    use.more()
    into = feed_back(
        grad, lambda: use.low, act, slope, lambda: use.up, down, vec, 3, grads, stage.work.pre
    )
    stage.push(vec)
    out.grad1[...] = grad + into
    stage.push(out.grad1)


def put_vectors(grads, start, own, others):
    d = own.shape[1]
    for chunk in range(d // LANES):
        cols = slice(chunk * LANES, (chunk + 1) * LANES)
        first = jnp.concatenate([own[:, cols]] + [each[:, cols] for each in others[:3]], axis=1)
        first = jnp.concatenate([first, jnp.zeros_like(first)], axis=0)
        second = jnp.concatenate([others[3][:, cols], jnp.zeros((8, d - LANES), WIDE)], axis=1)
        ups = [each[3 + chunk : 4 + chunk] for each in (others[0], others[3])]
        second = jnp.concatenate([second] + ups + [jnp.zeros((6, d), WIDE)], axis=0)
        grads.put(0, chunk, start, first)
        grads.put(1, chunk, start, second)


def self_backward(norm_row, last, stage):
    me, core = stage.scalars.ids[0], stage.scalars.ids[1]
    use, out, work = stage.use, stage.out, stage.work
    vec = work.vec
    grads = Halves(out.grads, LANES, LANES + (16 if last else 0), me, core, stage)
    vec[...] = jnp.zeros_like(vec)
    hat, scale, grad, proj, context = use.hat, use.scale, use.grad, use.proj, use.context
    use.more()
    hat, scale = hat[...].astype(WIDE), scale[...][:, 0:1]
    gain = use.gains[norm_row : norm_row + 1]
    grad = out_backward(grad[...], hat, scale, gain, proj, context, work, vec, grads)
    q, k, v, exps, inverse = use.q, use.k, use.v, use.exps, use.inverse
    use.more()
    attention_backward(q, k, v, exps, inverse, context, work)
    dq, dk, dv = attention_sums(work, vec)
    x_t = use.x_t[...]
    put_units(grads, dot_nt(x_t, dk), 1, 0)
    grads.leave_first(0)
    put_units(grads, dot_nt(x_t, dq), 0, 1)
    put_units(grads, dot_nt(x_t, dv), 1, 1)
    if last:
        others = [each[...] for each in (use.vec_enc, use.vec_self, use.vec_cross, use.vec_dec)]
        put_vectors(grads, 2 * LANES, vec[...], others)
    grads.leave_rest(0)
    qkv = use.qkv
    d = x_t.shape[0]
    through = dot_nn(qkv[:, 0:d], dq) + dot_nn(qkv[:, d : 2 * d], dk) + dot_nn(qkv[:, 2 * d :], dv)
    input_grad = grad + jnp.transpose(through)
    if not last:
        vec[5:6, :] = total(input_grad * mask_columns(use.mask, d))
        out.vec[...] = vec[...]
        stage.push(out.vec)
    out.input_grad[...] = input_grad.astype(LOW)
    stage.push(out.input_grad)


def swap(array, axis_name, bit):
    size = lax.axis_size(axis_name)
    return lax.ppermute(array, axis_name, [(i, i ^ bit) for i in range(size)])


def spread_rows(local, me):
    return [
        swap(lax.dynamic_index_in_dim(local, me ^ d, 0, keepdims=False), "seq", d) for d in range(1, local.shape[0])
    ]


def pack_rows(ids, dec_input, cotangent, masked):
    count, length, d = dec_input.shape
    rows = 2 * length + 16

    def kernel(ids_ref, mask_ref, dec_ref, cot_ref, *refs):
        results, scratch, copies = refs[:count], refs[count], Copies(refs[count + 1])
        me = ids_ref[0]
        coming = []
        for away in range(1, count):
            row = jnp.bitwise_xor(me, away)
            coming.append(copies.start(dec_ref.at[row], scratch.at[away, 0:length]))
            coming.append(copies.start(cot_ref.at[row], scratch.at[away, length : 2 * length]))
        for away in range(count):
            row = mask_ref[jnp.bitwise_xor(me, away)].astype(WIDE).astype(LOW)
            row = jnp.concatenate([jnp.broadcast_to(row, (16, length))] * (d // length), axis=1)
            scratch[away, 2 * length : rows] = row
        copies.leave(scratch.at[0, 2 * length : rows], results[0])
        for away in range(1, count):
            coming[2 * away - 2].wait()
            coming[2 * away - 1].wait()
            copies.leave(scratch.at[away], results[away])
        copies.finish()

    return pl.pallas_call(
        kernel,
        name="pack_rows",
        out_shape=[shape_of((16, d), LOW)] + [shape_of((rows, d), LOW)] * (count - 1),
        in_specs=[SMEM, pl.BlockSpec(memory_space=pltpu.VMEM), HBM, HBM],
        out_specs=[HBM] * count,
        scratch_shapes=[pltpu.VMEM((count, rows, d), LOW), pltpu.SemaphoreType.DMA((3 * count,))],
        compiler_params=parameters(),
        cost_estimate=cost(0, 2e6),
    )(ids, masked.reshape(count, 1, length), dec_input, cotangent)


class Piece(typing.NamedTuple):
    array: typing.Any
    start: int
    rows: int
    half: int = -1

    def halved(self, half):
        return self._replace(half=half)

    @property
    def lanes(self):
        width = self.array.shape[-1]
        return width if self.half < 0 else width // 2

    def origin(self, ref, place):
        if self.half < 0:
            return ref.at[pl.ds(self.start, self.rows)]
        start = pl.multiple_of(jnp.bitwise_xor(place, self.half) * self.lanes, self.lanes)
        return ref.at[pl.ds(self.start, self.rows), pl.ds(start, self.lanes)]


class Step(typing.NamedTuple):
    channel: typing.Any
    sources: tuple


X, Y, DIAGONAL, PAIR, PAIRS = 0, 1, 2, 3, 4
CHANNEL = (("seq", 1), ("seq", 2), ("seq", 3), ("rows", 2), ("rows", 4))


def boundary(name, ids, steps, after=(), weight=1):
    arrays = distinct([piece.array for step in steps for piece in step.sources])
    after = [array for array in distinct(after) if not any(array is other for other in arrays)]
    outs, places = {}, []
    for step in steps:
        rows = step.sources[0].rows
        key = (step.channel, step.sources[0].lanes)
        start = outs.get(key, 0)
        outs[key] = start + rows
        places.append((key, start, rows))
    keys = list(outs)
    tally = sum(len(step.sources) for step in steps) + len(steps)

    def kernel(ids_ref, *refs):
        inputs, refs = refs[: len(arrays)], refs[len(arrays) + len(after) :]
        results, refs = dict(zip(keys, refs)), refs[len(keys) :]
        buffers, refs = dict(zip(keys, refs)), refs[len(keys) :]
        scratch, copies = list(refs[:-1]), Copies(refs[-1])
        coming = []
        for step in steps:
            for piece in step.sources:
                origin = piece.origin(inputs[where_in(arrays, piece.array)], ids_ref[2])
                coming.append((copies.start(origin, scratch[len(coming)]), scratch[len(coming)]))
        for step, (key, start, rows) in zip(steps, places):
            terms = []
            for _ in step.sources:
                moved, ref = coming.pop(0)
                moved.wait()
                terms.append(ref)
            rest = slice(start, start + rows)
            summed = functools.reduce(jnp.add, [term[...].astype(WIDE) for term in terms])
            buffers[key][rest, :] = summed.astype(LOW)
            copies.leave(buffers[key].at[rest], results[key].at[rest])
        copies.finish()

    shapes = [shape_of((outs[key], key[1]), LOW) for key in keys]
    given = pl.pallas_call(
        kernel,
        name=name,
        out_shape=shapes,
        in_specs=[SMEM] + [HBM] * (len(arrays) + len(after)),
        out_specs=[HBM] * len(keys),
        scratch_shapes=[pltpu.VMEM(each.shape, LOW) for each in shapes]
        + [pltpu.VMEM((piece.rows, piece.lanes), LOW) for step in steps for piece in step.sources]
        + [pltpu.SemaphoreType.DMA((tally,))],
        compiler_params=parameters(),
        cost_estimate=cost(MIX_COST * weight, 0),
    )(ids, *arrays, *after)
    formed = dict(zip(keys, given))
    arrived = {key: swap(formed[key], *CHANNEL[key[0]]) for key in keys if key[0] is not None}
    pieces = []
    for key, start, rows in places:
        mine = Piece(formed[key], start, rows)
        pieces.append((mine, mine._replace(array=arrived[key]) if key in arrived else None))
    return pieces, list(given)


class Flow:
    def __init__(self, grads, first, rest):
        keep, send = grads
        self.arrays = (keep, swap(send, "rows", 1))
        self.first, self.rest, self.at = first, rest, 0
        self.sent = self.arrived = None

    def both(self, start, rows):
        return tuple(Piece(array, start, rows) for array in self.arrays)

    def next_steps(self):
        a, b = self.first, self.rest
        own = 2 * (a + b)
        if self.at == 0:
            return [Step(X, self.both(0, 2 * a)), Step(Y, self.both(2 * a, 2 * b))]
        x, y = self.arrived
        if self.at == 1:
            self.x, self.y = x, y
            return [
                Step(Y, self.both(own + a, a) + (x._replace(start=x.start + a, rows=a),)),
                Step(X, self.both(own + 2 * a + b, b) + (y._replace(start=y.start + b, rows=b),)),
            ]
        if self.at == 2:
            sums = [
                self.both(own, a) + (self.x._replace(rows=a), x),
                self.both(own + 2 * a, b) + (self.y._replace(rows=b), y),
            ]
            return [
                Step(channel, tuple(piece.halved(half) for piece in each))
                for channel, half in ((PAIR, 1), (None, 0))
                for each in sums
            ]
        if self.at == 3:
            return [Step(PAIRS, (self.sent[2], x)), Step(PAIRS, (self.sent[3], y))]
        return [Step(PAIR, (self.sent[0], x)), Step(PAIR, (self.sent[1], y))]

    def take(self, pieces):
        self.sent = [piece[0] for piece in pieces]
        self.arrived = [piece[1] for piece in pieces[:2]]
        self.at += 1

    def parts(self, own, other):
        done = []
        for z_other, pieces in enumerate((self.sent, self.arrived)):
            start = 0
            for piece in pieces:
                for c_other, arrays in enumerate((own, other)):
                    done.append((piece._replace(array=arrays[z_other]), c_other, z_other, start))
                start += piece.rows
        return done

    @property
    def rows(self):
        return self.first + self.rest


def advance(name, ids, flows, extra=(), after=(), weight=1):
    steps, counts = [], []
    for flow in flows:
        own = flow.next_steps()
        counts.append(len(own))
        steps += own
    steps += list(extra)
    pieces, arrays = boundary(name, ids, steps, after, weight)
    for flow, n in zip(flows, counts):
        flow.take(pieces[:n])
        pieces = pieces[n:]
    return pieces, arrays


def cross_cores(flows):
    own = (flows[0].sent[0].array, flows[0].arrived[0].array)
    return own, tuple(swap(array, "rows", 1) for array in own)


def cross_both(flows):
    formed = flows[0].sent[0].array
    return (formed, flows[0].arrived[0].array), (swap(formed, "rows", 1), swap(formed, "rows", 3))


def finish_units(name, ids, groups, outs, old, returns=(), vectors=None, after=()):
    parts = [part for _, group, _ in groups for part in group]
    back = [block for _, blocks in returns for block in blocks]
    arrays = distinct([part[0].array for part in parts] + [block.array for block in back])
    kept, names = list(old), list(outs)
    vector_outs = [outs[each] for each in vectors or ()]
    d = HEADS * HEAD_DIM

    def kernel(ids_ref, *refs):
        refs = list(refs)

        def take(count):
            taken = refs[:count]
            del refs[:count]
            return taken

        inputs = take(len(arrays))
        take(len(kept) + len(after))
        results = dict(zip(names, take(len(names))))
        scratch, back_in = take(len(parts)), take(len(back))
        units, back_out, vec_out = take(len(groups)), take(len(returns)), take(len(vector_outs))
        copies = Copies(refs[0])
        me, core, place = ids_ref[0], ids_ref[1], ids_ref[2]

        def bring(piece, target):
            return copies.start(piece.origin(inputs[where_in(arrays, piece.array)], place), target)

        coming = [bring(part[0], target) for part, target in zip(parts, scratch)]
        blocks_coming = [bring(block, target) for block, target in zip(back, back_in)]
        slot = 0
        for (_, group, goals), unit in zip(groups, units):
            for piece, c_other, z_other, start in group:
                coming[slot].wait()
                side, rows = jnp.bitwise_xor(core, c_other), slice(start, start + piece.rows)
                if piece.lanes == d:
                    unit[side, rows, :] = scratch[slot][...].astype(WIDE)
                else:
                    offset = pl.multiple_of(jnp.bitwise_xor(place, z_other) * piece.lanes, piece.lanes)
                    unit[side, rows, pl.ds(offset, piece.lanes)] = scratch[slot][...].astype(WIDE)
                slot += 1
            for half, start, rows, output, index in goals:
                copies.leave(unit.at[half, start : start + rows], results[output].at[index])
        if vectors:
            last = groups[-1][0]
            top, low = units[-1][0, last - 16 : last, :], units[-1][1, last - 16 : last, :]
            stages = [top[0:8, i * LANES : (i + 1) * LANES] for i in range(4)] + [low[0:8, 0:LANES]]
            enc_s, enc_f, dec_s, crs, dec_f = stages
            gains, biases, ups, embed = vec_out
            for row, part in enumerate(stages):
                gains[row : row + 1, :] = part[0:1]
                biases[11 + row : 12 + row, :] = part[1:2]
            order = ((enc_s, 3), (enc_s, 4), (enc_s, 2), (enc_f, 2), (dec_s, 3), (dec_s, 4), (dec_s, 2))
            order += ((crs, 3), (crs, 4), (crs, 2), (dec_f, 2))
            for row, (part, at) in enumerate(order):
                biases[row : row + 1, :] = part[at : at + 1]
            ups[...] = low[8:10, :]
            embed[...] = dec_s[5:6]
            for output, buffer in zip(vectors, vec_out):
                copies.leave(buffer, results[output])
        slot = 0
        for (output, blocks), buffer in zip(returns, back_out):
            for block in range(len(blocks)):
                blocks_coming[slot].wait()
                buffer[jnp.bitwise_xor(me, block)] = back_in[slot][...].astype(buffer.dtype)
                slot += 1
            copies.leave(buffer, results[output])
        copies.finish()

    sems = len(parts) + len(back) + sum(len(goals) for _, _, goals in groups) + len(returns) + len(vector_outs)
    given = pl.pallas_call(
        kernel,
        name=name,
        out_shape=[outs[each] for each in names],
        in_specs=[SMEM] + [HBM] * (len(arrays) + len(kept) + len(after)),
        out_specs=[HBM] * len(names),
        scratch_shapes=[pltpu.VMEM((part[0].rows, part[0].lanes), LOW) for part in parts]
        + [pltpu.VMEM((block.rows, block.lanes), LOW) for block in back]
        + [pltpu.VMEM((2, rows, d), WIDE) for rows, _, _ in groups]
        + [pltpu.VMEM(outs[output].shape, outs[output].dtype) for output, _ in returns]
        + [pltpu.VMEM(each.shape, each.dtype) for each in vector_outs]
        + [pltpu.SemaphoreType.DMA((sems,))],
        input_output_aliases={1 + len(arrays) + i: names.index(each) for i, each in enumerate(kept)},
        compiler_params=parameters(),
        cost_estimate=cost(MIX_COST, 0),
    )(ids, *arrays, *[old[each] for each in kept], *after)
    return types.SimpleNamespace(**dict(zip(names, given)))


def by_rows(
    enc_input,
    dec_input,
    src_lengths,
    tgt_lengths,
    masked,
    cotangent,
    self_qkv,
    attn_out,
    cross_q,
    cross_kv,
    ffn_up,
    ffn_down,
    norm_gain,
    biases,
    up_bias,
    mask_embed,
):
    count, length, d = enc_input.shape
    tokens, ff = count * length, ffn_up.shape[2]
    me = lax.axis_index("seq")
    row = lax.axis_index("rows")
    ids = jnp.stack([me, row % 2, row // 2 % 2]).astype(jnp.int32)
    enc_others = spread_rows(enc_input, me)
    packed = pack_rows(ids, dec_input, cotangent, masked)
    packs = [swap(packed[away], "seq", away) for away in range(1, count)]
    embed = mask_embed.reshape(1, d)
    head_shape = (HEADS, HEAD_DIM, tokens)
    low_tokens, wide_tokens = shape_of((tokens, d), LOW), shape_of((tokens, d), WIDE)
    low_t, low_heads, low_ff = shape_of((d, tokens), LOW), shape_of(head_shape, LOW), shape_of((tokens, ff), LOW)
    exps, inverse = shape_of((HEADS, tokens, tokens), LOW), shape_of((HEADS, 8, tokens), WIDE)
    scale, vec = shape_of((tokens, LANES), WIDE), shape_of((8, d), WIDE)
    bias, scores = shape_of((tokens, tokens), WIDE), shape_of((3, tokens, tokens), WIDE)
    scalars = dict(ids=ids, src=src_lengths, tgt=tgt_lengths)
    step = dict(ids=ids)
    small = dict(biases=whole(biases), gains=whole(norm_gain))
    dense, score = 2 * tokens * d * d, 2 * tokens * tokens * d
    mask_pieces = [(packed[0], None, (0,))]
    for i, array in enumerate(packs, 1):
        mask_pieces.append((array, lambda s: (slice(2 * length, 2 * length + 16),), (i,)))
    mask_part = ((count, 16, d), LOW, mask_pieces)

    def tokens_of(local, others, start=0):
        return ((tokens, d), LOW, token_pieces(local, others, length, start))

    def halves(rows):
        return [shape_of((count * rows, d), LOW)] * 2

    enc = run_stage(
        "encoder_forward",
        functools.partial(encoder_forward, length),
        scalars,
        [dict(
            x=tokens_of(enc_input, enc_others),
            **small,
            qkv=layer(self_qkv, 0),
            proj=layer(attn_out, 0),
            up_bias=whole(up_bias),
            up=layer(ffn_up, 0),
            down=layer(ffn_down, 0),
        )],
        dict(
            x_t=low_t,
            q=low_heads,
            k=low_heads,
            v=low_heads,
            exps=exps,
            inverse=inverse,
            context=low_heads,
            hat0=low_tokens,
            scale0=scale,
            low1=low_tokens,
            act1=low_ff,
            slope1=low_ff,
            hat1=low_tokens,
            scale1=scale,
            memory_t=low_t,
        ),
        dict(bias=bias, scores=scores),
        12 * dense + 2 * score,
        24e6,
        after=packed[1:],
    )
    attention_work = dict(
        context_grad=shape_of(head_shape, WIDE),
        dq=low_heads,
        dk=low_heads,
        dv=low_heads,
        sums=shape_of((2, HEADS, HEAD_DIM, LANES), WIDE),
    )
    dec = run_stage(
        "decoder",
        functools.partial(decoder, length),
        scalars,
        [dict(
            **small,
            mask=mask_part,
            x=tokens_of(dec_input, packs),
            embed=whole(embed),
            qkv=layer(self_qkv, 1),
            proj1=layer(attn_out, 1),
            cross_q=whole(cross_q),
            memory_t=whole(enc.memory_t),
            cross_kv=whole(cross_kv),
            proj2=layer(attn_out, 2),
            up_bias=whole(up_bias),
            up=layer(ffn_up, 1),
            down=layer(ffn_down, 1),
            cotangent=tokens_of(cotangent, packs, length),
        )],
        dict(
            x_t=low_t,
            q2=low_heads,
            k2=low_heads,
            v2=low_heads,
            exps2=exps,
            inverse2=inverse,
            context2=low_heads,
            hat2=low_tokens,
            scale2=scale,
            final=[shape_of((length, d), LOW)] * count,
            vec=vec,
            vec_cross=vec,
            grads=halves(4 * LANES),
            grads_cross=halves(2 * LANES),
            memory_grad=wide_tokens,
            hidden_grad=wide_tokens,
        ),
        dict(
            bias=bias,
            scores=scores,
            low=low_tokens,
            act=low_ff,
            slope=low_ff,
            pre=low_ff,
            hidden_t=low_t,
            hat=wide_tokens,
            scale=scale,
            q=low_heads,
            k=low_heads,
            v=low_heads,
            exps=exps,
            inverse=inverse,
            context=low_heads,
            **attention_work,
        ),
        40 * dense + 8 * score,
        50e6,
    )

    def attention_parts(context, inverse, q, k, v, exps):
        return dict(
            context=whole(context),
            inverse=whole(inverse),
            q=whole(q),
            k=whole(k),
            v=whole(v),
            exps=whole(exps),
        )

    flow_ffn, flow_cross = Flow(dec.grads, 2 * LANES, 2 * LANES), Flow(dec.grads_cross, LANES, LANES)
    first_flows = [flow_ffn, flow_cross]

    def self_stage(name, norm_row, last, grad, hat, scale, attention, x_t, index, more, after):
        rows = 2 * LANES + (16 if last else 0)
        return run_stage(
            name,
            functools.partial(self_backward, norm_row, last),
            step,
            [dict(
                gains=whole(norm_gain),
                grad=whole(grad),
                hat=whole(hat),
                scale=whole(scale),
                proj=layer(attn_out, index),
                **attention_parts(*attention),
                x_t=whole(x_t),
                qkv=layer(self_qkv, index),
                **more,
            )],
            dict(input_grad=low_tokens, grads=halves(rows), **({} if last else dict(vec=vec))),
            dict(vec=vec, **attention_work),
            8 * dense + 4 * score,
            20e6,
            after,
        )

    enc_ffn = run_stage(
        "encoder_ffn_backward",
        encoder_ffn_backward,
        step,
        [dict(
            gains=whole(norm_gain),
            grad=whole(dec.memory_grad),
            hat=whole(enc.hat1),
            scale=whole(enc.scale1),
            down=layer(ffn_down, 0),
            slope=whole(enc.slope1),
            act=whole(enc.act1),
            low=whole(enc.low1),
            up=layer(ffn_up, 0),
        )],
        dict(vec=vec, grad1=wide_tokens, grads=halves(4 * LANES)),
        dict(pre=low_ff),
        16 * dense,
        18e6,
    )
    flow_enc = Flow(enc_ffn.grads, 2 * LANES, 2 * LANES)
    _, formed = advance("first_xy", ids, first_flows, after=[enc_ffn.vec], weight=BIG_WEIGHT)
    _, formed = advance("encoder_ffn_xy", ids, [flow_enc], after=formed)
    dec_self = self_stage(
        "decoder_self_backward",
        2,
        False,
        dec.hidden_grad,
        dec.hat2,
        dec.scale2,
        (dec.context2, dec.inverse2, dec.q2, dec.k2, dec.v2, dec.exps2),
        dec.x_t,
        1,
        dict(mask=mask_part),
        formed,
    )
    flow_dec = Flow(dec_self.grads, LANES, LANES)
    _, formed = advance("first_yx", ids, first_flows, after=[dec_self.vec], weight=BIG_WEIGHT)
    dec_blocks = [Piece(dec_self.input_grad, i * length, length) for i in range(count)]

    def sent_back(blocks):
        return [Step(channel, (blocks[i],)) for i, channel in ((1, X), (2, Y), (3, X))]

    def forwarded(pieces):
        return [Step(Y, (pieces[2][1],))]

    def came_back(blocks, pieces):
        return [blocks[0]] + [pieces[i][1] for i in (0, 1, 3)]

    _, formed = advance("decoder_self_xy", ids, [flow_dec], after=formed)
    enc_self = self_stage(
        "encoder_self_backward",
        0,
        True,
        enc_ffn.grad1,
        enc.hat0,
        enc.scale0,
        (enc.context, enc.inverse, enc.q, enc.k, enc.v, enc.exps),
        enc.x_t,
        0,
        dict(
            vec_enc=whole(enc_ffn.vec),
            vec_self=whole(dec_self.vec),
            vec_cross=whole(dec.vec_cross),
            vec_dec=whole(dec.vec),
        ),
        formed,
    )
    flow_last = Flow(enc_self.grads, LANES, LANES + 16)
    next_flows = [flow_enc, flow_dec]
    four = first_flows + next_flows
    enc_blocks = [Piece(enc_self.input_grad, i * length, length) for i in range(count)]


    def arrivals(pieces):
        return [piece[1].array for piece in pieces]

    _, formed = advance("four_one", ids, four, after=[enc_self.input_grad], weight=BIG_WEIGHT)
    _, formed = advance("last_xy", ids, [flow_last], after=formed)
    _, formed = advance("four_two", ids, four, after=formed)
    finals = [Piece(array, 0, length) for array in dec.final]
    returned = [finals, dec_blocks, enc_blocks]
    back, formed = advance(
        "last_yx", ids, [flow_last], [step for blocks in returned for step in sent_back(blocks)], after=formed
    )
    backs = [back[3 * i : 3 * i + 3] for i in range(len(returned))]
    _, formed = advance("four_three", ids, four, after=formed, weight=3)
    first_done = cross_cores(first_flows)
    back, formed = advance(
        "last_pair", ids, [flow_last], [step for pieces in backs for step in forwarded(pieces)], after=formed
    )
    backs = [pieces + [last] for pieces, last in zip(backs, back)]
    _, formed = advance("next_four", ids, next_flows, after=formed)
    next_done = cross_cores(next_flows)
    _, formed = advance("last_pairs", ids, [flow_last], after=formed)
    _, formed = advance("last_back", ids, [flow_last], after=formed + arrivals(back))
    last_done = cross_both([flow_last])
    half = 2 * LANES

    def ffn_targets(index):
        goals = []
        for side in (0, 1):
            for unit in (0, 1):
                j = side * 2 + unit
                goals.append((side, unit * LANES, LANES, "up", (index, slice(None), slice(j * d, (j + 1) * d))))
            goals.append((side, half, half, "down", (index, slice(side * half, (side + 1) * half))))
        return goals

    def self_targets(index):
        goals = [(0, 0, LANES, "proj", (index,))]
        for j, (side, unit) in enumerate(((0, 1), (1, 0), (1, 1))):
            goals.append((side, unit * LANES, LANES, "qkv", (index, slice(None), slice(j * d, (j + 1) * d))))
        return goals

    cross_targets = [
        (0, 0, LANES, "proj", (2,)),
        (0, LANES, LANES, "cross_q", (slice(None),)),
        (1, 0, LANES, "cross_kv", (slice(None), slice(0, d))),
        (1, LANES, LANES, "cross_kv", (slice(None), slice(d, 2 * d))),
    ]
    local_rows = (count, length, d)
    up_down = dict(up=shape_of((2, LANES, ff), WIDE), down=shape_of((2, d, d), WIDE))
    proj = shape_of((3, LANES, d), WIDE)
    proj_qkv = dict(proj=proj, qkv=shape_of((2, LANES, 3 * d), WIDE))
    first = finish_units(
        "finish_four",
        ids,
        [
            (flow_ffn.rows, flow_ffn.parts(*first_done), ffn_targets(1)),
            (flow_cross.rows, flow_cross.parts(*first_done), cross_targets),
            (flow_enc.rows, flow_enc.parts(*next_done), ffn_targets(0)),
            (flow_dec.rows, flow_dec.parts(*next_done), self_targets(1)),
        ],
        dict(
            final=shape_of(local_rows, LOW),
            dec_grad=shape_of(local_rows, WIDE),
            cross_q=shape_of((LANES, d), WIDE),
            cross_kv=shape_of((LANES, 2 * d), WIDE),
            **up_down,
            **proj_qkv,
        ),
        {},
        [
            ("final", came_back(finals, backs[0])),
            ("dec_grad", came_back(dec_blocks, backs[1])),
        ],
        after=formed,
    )
    third = finish_units(
        "finish_last",
        ids,
        [(flow_last.rows, flow_last.parts(*last_done), self_targets(0))],
        dict(
            enc_grad=shape_of(local_rows, WIDE),
            gains=shape_of((5, LANES), WIDE),
            biases=shape_of((16, LANES), WIDE),
            ups=shape_of((2, d), WIDE),
            embed=shape_of((1, LANES), WIDE),
            **proj_qkv,
        ),
        dict(proj=first.proj, qkv=first.qkv),
        [("enc_grad", came_back(enc_blocks, backs[2]))],
        ("gains", "biases", "ups", "embed"),
    )
    return (
        first.final,
        third.enc_grad,
        first.dec_grad,
        third.qkv,
        third.proj,
        first.cross_q,
        first.cross_kv,
        first.up,
        first.down,
        third.gains,
        third.biases,
        third.ups,
        third.embed.reshape(LANES),
    )


def fits_by_rows(mesh, enc_input, ffn_up):
    count, length = enc_input.shape[0], enc_input.shape[1]
    return (
        mesh.shape["seq"] == 4
        and count == 4
        and mesh.shape["rows"] == 8
        and length == LANES
        and ffn_up.shape[2] == count * ffn_up.shape[1]
        and enc_input.shape[2] == HEADS * HEAD_DIM == count * LANES
    )


def device_program(mesh, *arrays):
    if fits_by_rows(mesh, arrays[0], arrays[10]):
        return by_rows(*arrays)
    return local(*arrays)


def solution(mesh):
    return jax.shard_map(
        functools.partial(device_program, mesh),
        mesh=mesh,
        in_specs=(
            P("rows", "seq", None),
            P("rows", "seq", None),
            P("rows", None),
            P("rows", None),
            P("rows", "seq"),
            P("rows", "seq", None),
            P(),
            P(),
            P(),
            P(),
            P(),
            P(),
            P(),
            P(),
            P(),
            P(),
        ),
        out_specs=(
            P("rows", "seq", None),
            P("rows", "seq", None),
            P("rows", "seq", None),
            P(None, "seq", None),
            P(None, "seq", None),
            P("seq", None),
            P("seq", None),
            P(None, "seq", None),
            P(None, "seq", None),
            P(None, "seq"),
            P(None, "seq"),
            P(None, "seq"),
            P("seq"),
        ),
        check_vma=False,
    )
```
